256 devices in a mesh: ax: 16 (over z, core), az: 16 (over y, x).
Axes of the slice: x: 4, y: 4, z: 8, core: 2. Of those that a mesh axis runs over, the one named last changes fastest.
Arguments:
- gas_init: float32 [256, 512, 128], P('ax', 'az'), may hold values from -6 to 6
- transport: bfloat16 [3, 256, 512, 128], P(None, 'ax', 'az'), may hold values from -0.5 to 0.5, as said below
- heat_coef: float32 [256, 512], P('ax', 'az'), may hold values from 0.15 to 2.8
- bed_mask: int32 [256, 512], P('ax', 'az'), may hold values from 0 to 1, as said below
- wall_init: float32 [256, 48, 512], P(('ax', 'az')), may hold values from -6 to 6
- interface_init: float32 [256, 512], P(('ax', 'az')), may hold values from -6 to 6
- inverse_blocks: float32 [512, 48, 48], replicated, may hold values from -0.9 to 0.9, as said below
- rotation: int32 [1], replicated, may hold values from 1 to 511
Outputs:
- gas_temp: float32 [256, 512, 128], P('ax', 'az')
- wall_temp: float32 [256, 48, 512], P(('ax', 'az'))
- interface: float32 [256, 512], P(('ax', 'az'))
The draws below stay inside these ranges and needn't reach their ends.
Inputs may be any that keep to these rules, and one draw needn't show every extreme that they name: `transport`: components 0 and 1 are Courant numbers between 0.12 and 0.3; component 2 is a heat source of one sweep. `bed_mask`: in each axial row the cells with 1 form one arc of azimuth. `inverse_blocks`: block k acts on the wall layers of Hartley mode k of the azimuth.
All inputs are finite; a program needn't handle non-finite values.
Results may differ from the reference program's by a relative error of at most 0.0003.
Values may be sent and summed in bfloat16 or wider, within the bound.
A program may use at most 128 MiB of HBM per device.

```python
import jax
import jax.numpy as jnp
from jax import lax

A = 512
R = 128
LAYERS = 48
SWEEPS = 3
ITERS = 2
NX = 256


def draw_transport(key, part):
    key = jax.random.fold_in(key, 11)
    subkeys = jax.random.split(key, 3)
    grid_shape = (NX, A, R)
    axial_courant = jax.random.uniform(subkeys[0], grid_shape, jnp.float32, 0.12, 0.3)
    swirl_courant = jax.random.uniform(subkeys[1], grid_shape, jnp.float32, 0.12, 0.3)
    source = 0.1 * jnp.clip(jax.random.normal(subkeys[2], grid_shape, jnp.float32), -4.5, 4.5)
    return jnp.stack([axial_courant, swirl_courant, source]).astype(jnp.bfloat16)


def draw_heat_coef(key, part):
    key = jax.random.fold_in(key, 12)
    positions = jnp.arange(NX, dtype=jnp.float32)[:, None] / NX
    axial_ramp = jnp.exp(jnp.log(3.0) * positions)
    roughness = jnp.exp(jax.random.uniform(key, (NX, A), jnp.float32, jnp.log(0.6), jnp.log(1.6)))
    return 0.3 * axial_ramp * roughness


def draw_bed_mask(key, part):
    key = jax.random.fold_in(key, 13)
    subkeys = jax.random.split(key, 2)
    centre = jax.random.randint(subkeys[0], (NX, 1), A // 2, A)
    half_width = jax.random.randint(subkeys[1], (NX, 1), A // 16, A // 6)
    positions = jnp.arange(A, dtype=jnp.int32)[None, :]
    arc_gap = jnp.abs(positions - centre)
    arc_gap = jnp.minimum(arc_gap, A - arc_gap)
    return (arc_gap <= half_width).astype(jnp.int32)


def draw_inverse_blocks(key, part):
    key = jax.random.fold_in(key, 14)
    subkeys = jax.random.split(key, 2)
    identity = jnp.eye(LAYERS, dtype=jnp.float32)
    diagonal = jnp.exp(jax.random.uniform(subkeys[0], (A, LAYERS, 1), jnp.float32, jnp.log(0.3), jnp.log(0.9)))
    off_diagonal = 0.25 * jnp.clip(jax.random.normal(subkeys[1], (A, LAYERS, LAYERS), jnp.float32), -4.0, 4.0) / LAYERS ** 0.5
    return identity * diagonal + (1.0 - identity) * off_diagonal


def level_of(rng, dims, pieces, smallest, top_value):
    gain, own = 1.0, jax.random.fold_in(rng, 6)
    for dim, shards_of in pieces:
        draws = jnp.exp(jax.random.uniform(jax.random.fold_in(own, dim), (shards_of,), jnp.float32, smallest / len(pieces), top_value / len(pieces)))
        gain = gain * jnp.repeat(draws, dims[dim] // shards_of).reshape([-1 if axis == dim else 1 for axis in range(len(dims))])
    return gain


def gaussian(key, dims, width, most, cuts=(), held_as=jnp.bfloat16):
    result = jax.random.normal(key, dims, jnp.float32) * width
    if len(cuts) > 0:
        result = level_of(key, dims, cuts, -0.22, 0.18) * result
    return jnp.clip(result, min=-most, max=most).astype(held_as)


def setup_inputs(seed: int = 0) -> dict:
    streams_of = jax.random.split(jax.random.key(seed), 9)
    return {
        "gas_init": gaussian(streams_of[0], (NX, A, R), 1.0, 6.0, ((0, 16), (1, 16)), jnp.float32),
        "transport": draw_transport(jax.random.fold_in(streams_of[8], 71), 0),
        "heat_coef": draw_heat_coef(jax.random.fold_in(streams_of[8], 71), 0),
        "bed_mask": draw_bed_mask(jax.random.fold_in(streams_of[8], 71), 0),
        "wall_init": gaussian(streams_of[4], (NX, LAYERS, A), 1.0, 6.0, ((0, 256),), jnp.float32),
        "interface_init": gaussian(streams_of[5], (NX, A), 1.0, 6.0, ((0, 256),), jnp.float32),
        "inverse_blocks": draw_inverse_blocks(jax.random.fold_in(streams_of[8], 71), 0),
        "rotation": jax.random.randint(streams_of[7], (1,), 1, A).astype(jnp.int32),
    }


DIFFUSE = 0.04
RADIAL = 0.06
BED_COEF = 0.8
FIRST_RELAX = 0.5
TINY = 1e-06
HIGHEST = lax.Precision.HIGHEST

def hartley(length):
    positions = jnp.arange(length, dtype=jnp.int32)
    product = positions[:, None] * positions[None, :] % length
    phases = 2.0 * jnp.pi / length * product.astype(jnp.float32)
    return (jnp.cos(phases) + jnp.sin(phases)) / jnp.sqrt(jnp.float32(length))

def advance(padded, courant_axial, courant_swirl, source, edge_values):
    centre = padded[1:-1, 1:-1]
    west_cell = padded[:-2, 1:-1]
    east_cell = padded[2:, 1:-1]
    south_cell = padded[1:-1, :-2]
    north_cell = padded[1:-1, 2:]
    inner_cell = jnp.concatenate([centre[:, :, :1], centre[:, :, :-1]], axis=2)
    outer_cell = jnp.concatenate([centre[:, :, 1:], edge_values[:, :, None]], axis=2)
    return centre + courant_axial * (west_cell - centre) + courant_swirl * (south_cell - centre) + DIFFUSE * (west_cell + east_cell + south_cell + north_cell - 4.0 * centre) + RADIAL * (inner_cell + outer_cell - 2.0 * centre) + source

def gas_sweep(gas_now, transport, edge_values):
    widened = jnp.concatenate([gas_now[:, -1:], gas_now, gas_now[:, :1]], axis=1)
    padded = jnp.pad(widened, ((1, 1), (0, 0), (0, 0)))
    return advance(padded, transport[0].astype(jnp.float32), transport[1].astype(jnp.float32), transport[2].astype(jnp.float32), edge_values)

def solve_wall(wall_init, flux_rows, inverse_blocks, hartley_table):
    wall_load = jnp.concatenate([wall_init[:, :1, :] + flux_rows[:, None, :], wall_init[:, 1:, :]], axis=1)
    row_count, layers, length = wall_load.shape
    spectral = jnp.dot(wall_load.reshape(row_count * layers, length), hartley_table, precision=HIGHEST)
    spectral = spectral.reshape(row_count, layers, length)
    blended = jnp.einsum('klm,xmk->xlk', inverse_blocks, spectral, precision=HIGHEST)
    result_rows = jnp.dot(blended.reshape(row_count * layers, length), hartley_table, precision=HIGHEST)
    return result_rows.reshape(row_count, layers, length)

def reference(gas_init, transport, heat_coef, bed_mask, wall_init, interface_init, inverse_blocks, rotation):
    hartley_table = hartley(A)
    rotate_by = rotation[0]
    bed_cover = bed_mask == 1
    theta = interface_init
    relax_now = FIRST_RELAX
    previous = interface_init
    gas_now = gas_init
    wall_now = wall_init
    for outer_index in range(ITERS):
        gas_now = gas_init
        for sweep_index in range(SWEEPS):
            gas_now = gas_sweep(gas_now, transport, theta)
        near_wall = gas_now[:, :, -1]
        heat_flux = jnp.where(bed_cover, -BED_COEF * theta, heat_coef * (near_wall - theta))
        flux_rows = jnp.roll(heat_flux, -rotate_by, axis=1)
        wall_now = solve_wall(wall_init, flux_rows, inverse_blocks, hartley_table)
        wall_face = jnp.roll(wall_now[:, 0, :], rotate_by, axis=1)
        residual = wall_face - theta
        if outer_index == 0:
            relax_now = FIRST_RELAX
        else:
            change = residual - previous
            numerator = jnp.sum(previous * change)
            denominator = jnp.sum(change * change)
            relax_now = -relax_now * numerator / (denominator + TINY)
        theta = theta + relax_now * residual
        previous = residual
    return (gas_now, wall_now, theta)
```

```python
import functools

import jax
import jax.numpy as jnp
import ml_dtypes
import numpy as np
from jax import lax
from jax.experimental import pallas as pl
from jax.experimental.pallas import tpu as pltpu
from jax.sharding import PartitionSpec as P

DIFFUSE = 0.04
RADIAL = 0.06
BED_COEF = 0.8
FIRST_RELAX = 0.5
TINY = 1e-06
MESH = pl.DeviceIdType.MESH
F32 = jnp.float32
BF16 = jnp.bfloat16
SECTOR = 32
TOP = 8
FIELDS = (
    [(0, r) for r in (124, 125, 126, 127)]
    + [(1, r) for r in (124, 125, 126, 127)]
    + [(0, r) for r in (125, 126, 127)]
    + [(1, r) for r in (125, 126, 127)]
    + [(2, 125), (3, 125)]
    + [(2, 127), (3, 127), (4, 127), (2, 126), (3, 126), (4, 126), (4, 125), None]
    + [(2, 127), (3, 127), (4, 127), None, None, None, None, None]
)
NFIELD = len(FIELDS)
WINDOWS = (-3, 0, -2, 0)


def hartley_parts(length):
    positions = np.arange(length, dtype=np.int64)
    phases = 2.0 * np.pi / length * ((positions[:, None] * positions[None, :]) % length)
    table = ((np.cos(phases) + np.sin(phases)) / np.sqrt(length)).astype(np.float32)
    high = table.astype(ml_dtypes.bfloat16)
    low = (table - high.astype(np.float32)).astype(ml_dtypes.bfloat16)
    return high, low


def selector():
    table = np.zeros((NFIELD, 5 * 128), np.float32)
    for row, field in enumerate(FIELDS):
        if field is not None:
            table[row, field[0] * 128 + field[1]] = 1.0
    return table.astype(ml_dtypes.bfloat16)


def split(value):
    high = value.astype(BF16)
    return high, (value - high.astype(F32)).astype(BF16)


def roll_lanes(value, amount):
    return pltpu.roll(value, amount % value.shape[1], 1)


def kernel(
    nax, naz,
    gas_hbm, tr_hbm, heat_hbm, bed_hbm, wall_hbm, th_hbm, inv_hbm, rot_ref, hh_hbm, hl_hbm, sel_hbm,
    gas_out, wall_out, th_out,
    pad, tr, heat, bed, wall, th, inv, hh, hl, sel,
    msg, recv, recv_nb, fields, tht, thn, edge, ebuf, col_out, col_in, blend, wall_res, gas_res, redsrc, redbuf,
    load_sem, out_sem, bar_unused, msg_sem, nb_sem, th_sem, edge_sem, halo_ss, halo_rs, red_sem,
):
    ax, az = lax.axis_index("ax"), lax.axis_index("az")
    rows = naz
    length = SECTOR * naz
    quads = length // 128
    total = nax * rows
    inside = pl.ds(TOP, SECTOR)

    loads = {}
    for index, (name, source, target) in enumerate((
        ("gas", gas_hbm, pad.at[0, pl.ds(1, rows), inside]),
        ("tr", tr_hbm, tr),
        ("heat", heat_hbm, heat),
        ("bed", bed_hbm, bed),
        ("sel", sel_hbm, sel),
        ("th", th_hbm, th),
        ("wall", wall_hbm, wall),
        ("hh", hh_hbm, hh),
        ("hl", hl_hbm, hl),
        ("inv", inv_hbm, inv),
    )):
        loads[name] = pltpu.make_async_copy(source, target, load_sem.at[index])
        loads[name].start()

    barrier = pltpu.get_barrier_semaphore()

    def greet(to_ax, to_az):
        pl.semaphore_signal(barrier, inc=1, device_id=(to_ax, to_az), device_id_type=MESH)

    @pl.loop(1, naz)
    def _(k):
        greet(ax, lax.rem(az + k, naz))

    @pl.loop(1, nax)
    def _(k):
        greet(lax.rem(ax + k, nax), az)

    near_low = az < 3
    at_edge = jnp.logical_or(near_low, az >= naz - 3)
    beside = lax.rem(jnp.where(near_low, ax + nax - 1, ax + 1), nax)

    @pl.when(at_edge)
    def _():
        @pl.loop(0, naz)
        def _(k):
            greet(beside, k)

    lane = lax.broadcasted_iota(jnp.int32, (naz, 128), 1)
    sector = lax.broadcasted_iota(jnp.int32, (naz, 128), 0)
    cell = lane % SECTOR
    group = lane // SECTOR

    def tile_row(row):
        parts = [jnp.broadcast_to(row[:, 128 * q : 128 * q + 128], (4, 128)) for q in range(quads)]
        value = jnp.concatenate(parts, axis=0)
        turn = (sector - group) % 4
        result = value
        for k in range(1, 4):
            result = jnp.where(turn == k, roll_lanes(value, -SECTOR * k), result)
        return result

    def flatten(value):
        result = jnp.zeros_like(value)
        for p in range(4):
            moved = roll_lanes(value, SECTOR * (p - 2))
            result = jnp.where(jnp.logical_and(sector % 4 == p, group == p), moved, result)
        parts = [jnp.sum(result[4 * q : 4 * q + 4], axis=0, keepdims=True) for q in range(quads)]
        return jnp.concatenate(parts, axis=1)

    loads["th"].wait()
    theta0 = th[...]
    theta0_tiled = tile_row(theta0)
    tht[0] = theta0_tiled

    loads["gas"].wait()
    loads["tr"].wait()
    loads["heat"].wait()
    loads["bed"].wait()
    loads["sel"].wait()
    gas = pad[0, 1 : rows + 1, TOP : TOP + SECTOR, :].reshape(rows * SECTOR, 128)
    gas_high, gas_low = split(gas)
    stacked = jnp.concatenate(
        [gas_high, gas_low] + [tr[j].reshape(rows * SECTOR, 128) for j in range(3)], axis=1
    )
    near = lax.dot_general(
        sel[...], stacked, (((1,), (1,)), ((), ())), preferred_element_type=F32
    )
    turned = [near] + [roll_lanes(near, -SECTOR * k) for k in range(1, 4)]
    coded = jnp.where(bed[...] == 1, -heat[...], heat[...])
    coded = jnp.concatenate([coded] * 4, axis=1)
    coded_high = coded.astype(BF16).astype(F32)
    coded_low = coded - coded_high
    field8 = lax.broadcasted_iota(jnp.int32, (8, 128), 0)
    for i in range(rows):
        parts = []
        for part, first in enumerate(WINDOWS):
            start = (i + first) % rows
            quad = start // 4
            parts.append(turned[start % 4][8 * part : 8 * part + 8, 128 * quad : 128 * quad + 128])
        parts[3] = jnp.where(field8 == 3, coded_high[i : i + 1], parts[3])
        parts[3] = jnp.where(field8 == 4, coded_low[i : i + 1], parts[3])
        msg[i] = jnp.concatenate(parts, axis=0).astype(BF16)

    def stage_columns(step):
        col_out[step, 0] = pad[step, 1 : rows + 1, TOP, :]
        col_out[step, 1] = pad[step, 1 : rows + 1, TOP + SECTOR - 1, :]

    stage_columns(0)

    pl.semaphore_wait(barrier, naz - 1 + nax - 1 + 6)

    def remote(source, target, send, receive, to_ax, to_az):
        return pltpu.make_async_remote_copy(
            src_ref=source, dst_ref=target, send_sem=send, recv_sem=receive,
            device_id=(to_ax, to_az), device_id_type=MESH,
        )

    def wait_bytes(ref, sem):
        pltpu.make_async_copy(ref, ref, sem).wait()

    @pl.loop(1, naz)
    def _(k):
        to = lax.rem(az + k, naz)
        remote(msg.at[to], recv.at[az], msg_sem.at[0], msg_sem.at[1], ax, to).start()

    for low in (True, False):
        to_ax = lax.rem(ax + 1, nax) if low else lax.rem(ax + nax - 1, nax)

        @pl.loop(0, 3)
        def _(k):
            to = k if low else naz - 3 + k
            remote(msg.at[to], recv_nb.at[az], nb_sem.at[0], nb_sem.at[1], to_ax, to).start()

    flat = ax * naz + az

    def send_theta(which):
        for slot, offset in enumerate((2, 1, -1, -2)):
            to = lax.rem(flat + offset + total, total)
            remote(
                tht.at[which], thn.at[which, slot], th_sem.at[which, 0], th_sem.at[which, 1],
                lax.div(to, naz), lax.rem(to, naz),
            ).start()

    send_theta(0)

    def halo_copies(step):
        up_ax, down_ax = lax.rem(ax + 1, nax), lax.rem(ax + nax - 1, nax)
        up_az, down_az = lax.rem(az + 1, naz), lax.rem(az + naz - 1, naz)
        return (
            remote(pad.at[step, rows, inside], pad.at[step, 0, inside],
                   halo_ss.at[step, 0], halo_rs.at[step, 0], up_ax, az),
            remote(pad.at[step, 1, inside], pad.at[step, rows + 1, inside],
                   halo_ss.at[step, 1], halo_rs.at[step, 1], down_ax, az),
            remote(col_out.at[step, 1], col_in.at[step, 0],
                   halo_ss.at[step, 2], halo_rs.at[step, 2], ax, up_az),
            remote(col_out.at[step, 0], col_in.at[step, 1],
                   halo_ss.at[step, 3], halo_rs.at[step, 3], ax, down_az),
        )

    def send_halo(step):
        for copy in halo_copies(step):
            copy.start()

    def take_halo(step):
        for copy in halo_copies(step):
            copy.wait()

        @pl.when(ax == 0)
        def _():
            pad[step, 0, inside, :] = jnp.zeros((SECTOR, 128), F32)

        @pl.when(ax == nax - 1)
        def _():
            pad[step, rows + 1, inside, :] = jnp.zeros((SECTOR, 128), F32)

        pad[step, 1 : rows + 1, TOP - 1, :] = col_in[step, 0]
        pad[step, 1 : rows + 1, TOP + SECTOR, :] = col_in[step, 1]

    send_halo(0)
    recv[az] = msg[az]

    def times_table(value):
        high, low = split(value)
        count = value.shape[0]
        both = jnp.dot(jnp.concatenate([high, low], axis=0), hh[...], preferred_element_type=F32)
        return both[:count] + both[count:] + jnp.dot(high, hl[...], preferred_element_type=F32)

    def row_times_table(row):
        high, low = split(row)
        which = lax.broadcasted_iota(jnp.int32, (16, length), 0)
        both = jnp.where(which == 0, high.astype(F32), jnp.where(which == 1, low.astype(F32), 0.0)).astype(BF16)
        first = jnp.dot(both, hh[...], preferred_element_type=F32)
        second = jnp.dot(both, hl[...], preferred_element_type=F32)
        return first[0:1] + first[1:2] + second[0:1]

    loads["wall"].wait()
    loads["hh"].wait()
    loads["hl"].wait()
    layers = wall.shape[0]
    spectral = times_table(wall[...])
    loads["inv"].wait()

    @pl.loop(0, layers // 2)
    def _(pair):
        for j in range(2):
            layer = 2 * pair + j
            blend[pl.ds(layer, 1), :] = jnp.sum(inv[layer] * spectral, axis=0, keepdims=True)

    mode_gain = inv[0, 0:1, :]
    mode_base = blend[0:1, :]

    lane_row = lax.broadcasted_iota(jnp.int32, (SECTOR, 128), 1)

    def sweep(step, outer_edge, store):
        @pl.loop(0, rows)
        def _(x):
            centre = pad[step, x + 1, inside, :]
            west = pad[step, x, inside, :]
            east = pad[step, x + 2, inside, :]
            south = pad[step, x + 1, pl.ds(TOP - 1, SECTOR), :]
            north = pad[step, x + 1, pl.ds(TOP + 1, SECTOR), :]
            inner = jnp.where(lane_row == 0, centre, roll_lanes(centre, 1))
            outer = jnp.where(lane_row == 127, outer_edge(x), roll_lanes(centre, -1))
            store(x, (
                centre
                + tr[0, x].astype(F32) * (west - centre)
                + tr[1, x].astype(F32) * (south - centre)
                + DIFFUSE * (west + east + south + north - 4.0 * centre)
                + RADIAL * (inner + outer - 2.0 * centre)
                + tr[2, x].astype(F32)
            ))

    def store_pad(step):
        def store(x, value):
            pad[step, x + 1, inside, :] = value
        return store

    take_halo(0)
    sweep(0, lambda x: jnp.zeros((SECTOR, 128), F32), store_pad(1))

    wait_bytes(recv.at[pl.ds(0, naz - 1)], msg_sem.at[1])

    @pl.loop(0, naz)
    def _(source):
        fields[pl.ds(pl.multiple_of(source * NFIELD, NFIELD), NFIELD), :] = recv[source].astype(F32)

    @pl.when(at_edge)
    def _():
        wait_bytes(recv_nb, nb_sem.at[1])
        index = lax.broadcasted_iota(jnp.int32, (NFIELD, 128), 0)
        part = index // 8
        first = jnp.where(part == 0, WINDOWS[0], jnp.where(part == 2, WINDOWS[2], 0))
        place = az + first + lax.broadcasted_iota(jnp.int32, (NFIELD, 128), 1) // SECTOR
        own = jnp.logical_and(place >= 0, place < rows)
        own = jnp.logical_or(own, jnp.logical_and(index >= 27, index < 29))

        @pl.loop(0, naz)
        def _(source):
            here = pl.ds(pl.multiple_of(source * NFIELD, NFIELD), NFIELD)
            fields[here, :] = jnp.where(own, fields[here, :], recv_nb[source].astype(F32))

    def field(index):
        return fields[pl.ds(index, naz, stride=NFIELD), :]

    def in_domain(first):
        place = flat + first + group
        return jnp.logical_and(place >= 0, place < total)

    mask_a, mask_b, mask_c = in_domain(-3), in_domain(0), in_domain(-2)
    gas_a = [jnp.where(mask_a, field(j) + field(4 + j), 0.0) for j in range(4)]
    gas_b = [None] + [jnp.where(mask_b, field(8 + j) + field(11 + j), 0.0) for j in range(3)]
    coef_c = [[field(16 + j) for j in range(3)], [field(19 + j) for j in range(3)]]
    coef_d = [field(24 + j) for j in range(3)]
    coef_125 = [roll_lanes(field(14), 64), roll_lanes(field(15), 64), field(22)]
    coupling = field(27) + field(28)

    def stencil(coef, centre, west, east, inner, outer):
        south = jnp.where(cell == 0, pltpu.roll(roll_lanes(centre, -31), 1, 0), roll_lanes(centre, 1))
        north = jnp.where(
            cell == SECTOR - 1, pltpu.roll(roll_lanes(centre, 31), naz - 1, 0), roll_lanes(centre, -1)
        )
        return (
            centre
            + coef[0] * (west - centre)
            + coef[1] * (south - centre)
            + DIFFUSE * (west + east + south + north - 4.0 * centre)
            + RADIAL * (inner + outer - 2.0 * centre)
            + coef[2]
        )

    centres, easts = [], []
    for j in range(4):
        centre = roll_lanes(gas_a[j], -32)
        east = roll_lanes(gas_a[j], -64)
        if j:
            centre = jnp.where(group == 3, roll_lanes(gas_b[j], 64), centre)
            east = jnp.where(group >= 2, roll_lanes(gas_b[j], 32), east)
        centres.append(centre)
        easts.append(east)
    zero = jnp.zeros((naz, 128), F32)
    base_c = jnp.where(mask_c, stencil(coef_c[0], centres[3], gas_a[3], easts[3], centres[2], zero), 0.0)
    base_d = jnp.where(
        mask_b,
        stencil(coef_d, gas_b[3], roll_lanes(gas_b[3], 32), roll_lanes(gas_b[3], -32), gas_b[2], zero), 0.0,
    )
    one_126 = jnp.where(mask_c, stencil(coef_c[1], centres[2], gas_a[2], easts[2], centres[1], centres[3]), 0.0)
    one_125 = stencil(coef_125, centres[1], gas_a[1], easts[1], centres[0], centres[2])

    def flux_row(which, own):
        wait_bytes(thn.at[which], th_sem.at[which, 1])
        edge_c = jnp.where(
            group == 0, thn[which, 0], jnp.where(group == 1, thn[which, 1], jnp.where(group == 2, own, thn[which, 2]))
        )
        edge_d = thn[which, 3]
        one_c = base_c + jnp.where(mask_c, RADIAL * edge_c, 0.0)
        one_d = base_d + jnp.where(mask_b, RADIAL * edge_d, 0.0)
        east = jnp.where(group == 3, roll_lanes(one_d, 32), roll_lanes(one_c, -32))
        two_c = jnp.where(
            mask_c, stencil(coef_c[0], one_c, roll_lanes(one_c, 32), east, one_126, edge_c), 0.0
        )
        two_126 = stencil(coef_c[1], one_126, roll_lanes(one_126, 32), roll_lanes(one_126, -32), one_125, one_c)
        three = stencil(coef_c[0], two_c, roll_lanes(two_c, 32), roll_lanes(two_c, -32), two_126, edge_c)
        return flatten(jnp.where(coupling < 0, -BED_COEF * own, coupling * (three - own)))

    shift = rot_ref[0]
    shift_back = length - shift

    def wall_face(flux):
        modes = row_times_table(pltpu.roll(flux, shift_back, 1))
        face = row_times_table(modes * mode_gain + mode_base)
        return modes, pltpu.roll(face, shift, 1)

    _, face = wall_face(flux_row(0, theta0_tiled))
    residual1 = face - theta0
    theta1 = theta0 + FIRST_RELAX * residual1
    theta1_tiled = tile_row(theta1)
    tht[1] = theta1_tiled
    send_theta(1)

    @pl.loop(1, naz)
    def _(k):
        to = lax.rem(az + k, naz)
        remote(
            tht.at[1, pl.ds(to, 1)], edge.at[pl.ds(az, 1)], edge_sem.at[0], edge_sem.at[1], ax, to
        ).start()

    edge[pl.ds(az, 1), :] = tht[1, pl.ds(az, 1), :]

    modes, face = wall_face(flux_row(1, theta1_tiled))
    residual2 = face - theta1
    change = residual2 - residual1
    top = jnp.sum(residual1 * change, axis=1, keepdims=True)
    bottom = jnp.sum(change * change, axis=1, keepdims=True)
    lane8 = lax.broadcasted_iota(jnp.int32, (8, 128), 1)
    redsrc[0] = jnp.where(lane8 == 0, top, jnp.where(lane8 == 1, bottom, 0.0))

    @pl.loop(1, naz)
    def _(k):
        to = lax.rem(az + k, naz)
        remote(redsrc.at[0], redbuf.at[0, az], red_sem.at[0], red_sem.at[1], ax, to).start()

    redbuf[0, az] = redsrc[0]

    wait_bytes(edge.at[pl.ds(0, naz - 1)], edge_sem.at[1])
    own_cell = lane_row == lax.broadcasted_iota(jnp.int32, (SECTOR, 128), 0)

    @pl.loop(0, rows)
    def _(x):
        value = jnp.sum(jnp.where(own_cell, edge[pl.ds(x, 1), :], 0.0), axis=1, keepdims=True)
        value = jnp.where(lane_row == 127, value, 0.0)
        ebuf[x] = value
        pad[1, x + 1, inside, :] = pad[1, x + 1, inside, :] + RADIAL * value

    stage_columns(1)
    send_halo(1)

    wall_res[...] = times_table(blend[...] + inv[:, 0, :] * modes)
    wall_copy = pltpu.make_async_copy(wall_res, wall_out, out_sem.at[0])
    wall_copy.start()

    wait_bytes(redbuf.at[0, pl.ds(0, naz - 1)], red_sem.at[1])
    redsrc[1] = jnp.sum(redbuf[0, 0:naz], axis=0)

    @pl.loop(1, nax)
    def _(k):
        to = lax.rem(ax + k, nax)
        remote(redsrc.at[1], redbuf.at[1, ax], red_sem.at[2], red_sem.at[3], to, az).start()

    redbuf[1, ax] = redsrc[1]

    take_halo(1)
    sweep(1, lambda x: ebuf[x], store_pad(2))
    stage_columns(2)
    send_halo(2)

    wait_bytes(redbuf.at[1, pl.ds(0, nax - 1)], red_sem.at[3])
    sums = jnp.sum(redbuf[1, 0:nax], axis=0)
    top = jnp.sum(jnp.where(lane8 == 0, sums, 0.0)[0:1], axis=1, keepdims=True)
    bottom = jnp.sum(jnp.where(lane8 == 1, sums, 0.0)[0:1], axis=1, keepdims=True)
    relax = -FIRST_RELAX * top / (bottom + TINY)
    th[...] = theta1 + relax * residual2
    th_copy = pltpu.make_async_copy(th, th_out, out_sem.at[1])
    th_copy.start()

    take_halo(2)

    def store_result(x, value):
        gas_res[x] = value

    sweep(2, lambda x: ebuf[x], store_result)
    gas_copy = pltpu.make_async_copy(gas_res, gas_out, out_sem.at[2])
    gas_copy.start()

    wait_bytes(msg.at[pl.ds(0, naz - 1)], msg_sem.at[0])
    wait_bytes(msg.at[pl.ds(0, 6)], nb_sem.at[0])
    for which in range(2):
        wait_bytes(thn.at[which], th_sem.at[which, 0])
    wait_bytes(edge.at[pl.ds(0, naz - 1)], edge_sem.at[0])
    wait_bytes(redbuf.at[0, pl.ds(0, naz - 1)], red_sem.at[0])
    wait_bytes(redbuf.at[1, pl.ds(0, nax - 1)], red_sem.at[2])
    wall_copy.wait()
    th_copy.wait()
    gas_copy.wait()


def on_device(
    nax, naz, gas_init, transport, heat_coef, bed_mask, wall_init, interface_init, inverse_blocks, rotation
):
    rows = gas_init.shape[0]
    layers, length = wall_init.shape[1:]
    table_high, table_low = hartley_parts(length)
    anywhere = pl.BlockSpec(memory_space=pl.ANY)
    dma = pltpu.SemaphoreType.DMA
    gas_now, wall_now, theta = pl.pallas_call(
        functools.partial(kernel, nax, naz),
        out_shape=(
            jax.ShapeDtypeStruct(gas_init.shape, F32),
            jax.ShapeDtypeStruct((layers, length), F32),
            jax.ShapeDtypeStruct((1, length), F32),
        ),
        in_specs=[anywhere] * 7 + [pl.BlockSpec(memory_space=pltpu.SMEM)] + [anywhere] * 3,
        out_specs=(anywhere,) * 3,
        scratch_shapes=[
            pltpu.VMEM((3, rows + 2, SECTOR + 2 * TOP, 128), F32),
            pltpu.VMEM(transport.shape, BF16),
            pltpu.VMEM(heat_coef.shape, F32),
            pltpu.VMEM(bed_mask.shape, jnp.int32),
            pltpu.VMEM((layers, length), F32),
            pltpu.VMEM((1, length), F32),
            pltpu.VMEM((layers, layers, length), F32),
            pltpu.VMEM((length, length), BF16),
            pltpu.VMEM((length, length), BF16),
            pltpu.VMEM((NFIELD, 5 * 128), BF16),
            pltpu.VMEM((rows, NFIELD, 128), BF16),
            pltpu.VMEM((naz, NFIELD, 128), BF16),
            pltpu.VMEM((naz, NFIELD, 128), BF16),
            pltpu.VMEM((naz * NFIELD, 128), F32),
            pltpu.VMEM((2, naz, 128), F32),
            pltpu.VMEM((2, 4, naz, 128), F32),
            pltpu.VMEM((rows, 128), F32),
            pltpu.VMEM((rows, SECTOR, 128), F32),
            pltpu.VMEM((3, 2, rows, 128), F32),
            pltpu.VMEM((3, 2, rows, 128), F32),
            pltpu.VMEM((layers, length), F32),
            pltpu.VMEM((layers, length), F32),
            pltpu.VMEM((rows, SECTOR, 128), F32),
            pltpu.VMEM((2, 8, 128), F32),
            pltpu.VMEM((2, max(nax, naz), 8, 128), F32),
            dma((10,)),
            dma((3,)),
            dma((1,)),
            dma((2,)),
            dma((2,)),
            dma((2, 2)),
            dma((2,)),
            dma((3, 4)),
            dma((3, 4)),
            dma((4,)),
        ],
        compiler_params=pltpu.CompilerParams(
            collective_id=0, has_side_effects=True, vmem_limit_bytes=32 * 1024 * 1024
        ),
        name="kiln_step",
    )(
        gas_init, transport, heat_coef, bed_mask, wall_init.reshape(layers, length), interface_init,
        jnp.transpose(inverse_blocks, (1, 2, 0)), rotation,
        jnp.asarray(table_high), jnp.asarray(table_low), jnp.asarray(selector()),
    )
    return gas_now, wall_now.reshape(1, layers, length), theta


def solution(mesh):
    return jax.shard_map(
        functools.partial(on_device, mesh.shape["ax"], mesh.shape["az"]),
        mesh=mesh,
        in_specs=(
            P("ax", "az", None),
            P(None, "ax", "az", None),
            P("ax", "az"),
            P("ax", "az"),
            P(("ax", "az"), None, None),
            P(("ax", "az"), None),
            P(),
            P(),
        ),
        out_specs=(P("ax", "az", None), P(("ax", "az"), None, None), P(("ax", "az"), None)),
        check_vma=False,
    )
```

```python
import functools

import jax
import jax.numpy as jnp
import ml_dtypes
import numpy as np
from jax import lax
from jax.experimental import pallas as pl
from jax.experimental.pallas import tpu as pltpu
from jax.sharding import PartitionSpec as P

DIFFUSE = 0.04
RADIAL = 0.06
BED_COEF = 0.8
FIRST_RELAX = 0.5
TINY = 1e-06
MESH = pl.DeviceIdType.MESH
F32 = jnp.float32
BF16 = jnp.bfloat16
SECTOR = 32
TOP = 8
COUPLING, LOW = "coupling", "low"
GAS = [(part, r) for part in (0, 1) for r in (124, 125, 126, 127)]
WALLSIDE = [(2, 127), (3, 127), (4, 127), (2, 126), (3, 126), (4, 126), COUPLING, LOW]
FIELDS = (
    GAS
    + WALLSIDE
    + GAS
    + [(2, 125), (3, 125), (4, 125)] * 2 + [(4, 127), None]
    + [(part, r) for part in (0, 1) for r in (125, 126, 127)] + [(2, 127), (3, 127)]
    + WALLSIDE
)
NFIELD = len(FIELDS)
FIRSTS = [-5] * 8 + [-4] * 8 + [-1] * 8 + [-4] * 3 + [0] * 3 + [2] * 2 + [2] * 8 + [0] * 8
REACH = 5


def hartley_parts(length):
    positions = np.arange(length, dtype=np.int64)
    phases = 2.0 * np.pi / length * ((positions[:, None] * positions[None, :]) % length)
    table = ((np.cos(phases) + np.sin(phases)) / np.sqrt(length)).astype(np.float32)
    high = table.astype(ml_dtypes.bfloat16)
    low = (table - high.astype(np.float32)).astype(ml_dtypes.bfloat16)
    return high, low


def selector():
    table = np.zeros((NFIELD, 5 * 128), np.float32)
    for row, field in enumerate(FIELDS):
        if isinstance(field, tuple):
            table[row, field[0] * 128 + field[1]] = 1.0
    return table.astype(ml_dtypes.bfloat16)


def split(value):
    high = value.astype(BF16)
    return high, (value - high.astype(F32)).astype(BF16)


def roll_lanes(value, amount):
    amount = amount % value.shape[1]
    return pltpu.roll(value, amount, 1) if amount else value


def kernel(
    nax, naz,
    gas_hbm, tr_hbm, heat_hbm, bed_hbm, wall_hbm, th_hbm, inv_hbm, rot_ref, hh_hbm, hl_hbm, sel_hbm,
    gas_res, wall_res, th_res,
    pad, tr, heat, bed, wall, th, inv, hh, hl, sel,
    msg, recv, recv_nb, fields, th_rows, base_rows, window, edge, coef_out, coef_in, col_out, col_in, blend,
    redsrc, redbuf,
    load_sem, msg_sem, nb_sem, th_sem, base_sem, edge_sem, halo_ss, halo_rs, coef_ss, coef_rs, red_sem,
):
    ax, az = lax.axis_index("ax"), lax.axis_index("az")
    rows = naz
    length = SECTOR * naz
    quads = length // 128
    total = nax * rows
    flat = ax * naz + az
    up_ax, down_ax = lax.rem(ax + 1, nax), lax.rem(ax + nax - 1, nax)
    up_az, down_az = lax.rem(az + 1, naz), lax.rem(az + naz - 1, naz)
    inside = pl.ds(TOP, SECTOR)

    loads = {}
    for index, (name, source, target) in enumerate((
        ("gas", gas_hbm, pad.at[0, pl.ds(1, rows), inside]),
        ("tr", tr_hbm, tr),
        ("heat", heat_hbm, heat),
        ("bed", bed_hbm, bed),
        ("sel", sel_hbm, sel),
        ("th", th_hbm, th),
        ("wall", wall_hbm, wall),
        ("hh", hh_hbm, hh),
        ("hl", hl_hbm, hl),
        ("inv", inv_hbm, inv),
    )):
        loads[name] = pltpu.make_async_copy(source, target, load_sem.at[index])
        loads[name].start()

    barrier = pltpu.get_barrier_semaphore()

    def greet(to_ax, to_az):
        pl.semaphore_signal(barrier, inc=1, device_id=(to_ax, to_az), device_id_type=MESH)

    @pl.loop(1, naz)
    def _(k):
        greet(ax, lax.rem(az + k, naz))

    @pl.loop(1, nax)
    def _(k):
        greet(lax.rem(ax + k, nax), az)

    low_edge, high_edge = az < REACH, az >= naz - REACH
    at_edge = jnp.logical_or(low_edge, high_edge)
    beside = jnp.where(low_edge, down_ax, up_ax)
    at_rim = jnp.logical_or(az < 2, az >= naz - 2)

    @pl.when(at_edge)
    def _():
        @pl.loop(0, naz)
        def _(k):
            greet(beside, k)

    for k in range(2):
        greet(up_ax, k)
        greet(down_ax, naz - 2 + k)

    lane = lax.broadcasted_iota(jnp.int32, (naz, 128), 1)
    sector = lax.broadcasted_iota(jnp.int32, (naz, 128), 0)
    cell = lane % SECTOR
    group = lane // SECTOR
    turn = sector % 4

    def tile_rows(values):
        result = jnp.zeros((naz, 128), F32)
        for g, row in enumerate(values):
            if row is None:
                continue
            wide = jnp.concatenate(
                [jnp.broadcast_to(row[:, 128 * q : 128 * q + 128], (4, 128)) for q in range(quads)], axis=0
            )
            for p in range(4):
                here = jnp.logical_and(turn == p, group == g)
                result = jnp.where(here, roll_lanes(wide, SECTOR * (g - p)), result)
        return result

    def flatten(value, groups):
        moved = [roll_lanes(value, SECTOR * k) for k in range(4)]
        found = []
        for g in groups:
            result = jnp.zeros_like(value)
            for p in range(4):
                result = jnp.where(jnp.logical_and(turn == p, group == p), moved[(p - g) % 4], result)
            parts = [jnp.sum(result[4 * q : 4 * q + 4], axis=0, keepdims=True) for q in range(quads)]
            found.append(jnp.concatenate(parts, axis=1))
        return found

    def four_times(value):
        return jnp.concatenate([value] * 4, axis=1)

    loads["th"].wait()
    theta0 = th[...]
    th_rows[4:5, :] = theta0

    for name in ("gas", "tr", "heat", "bed", "sel"):
        loads[name].wait()
    gas = pad[0, 1 : rows + 1, TOP : TOP + SECTOR, :].reshape(rows * SECTOR, 128)
    gas_high, gas_low = split(gas)
    stacked = jnp.concatenate(
        [gas_high, gas_low] + [tr[j].reshape(rows * SECTOR, 128) for j in range(3)], axis=1
    )
    near = lax.dot_general(
        sel[...], stacked, (((1,), (1,)), ((), ())), preferred_element_type=F32
    )
    coded = four_times(jnp.where(bed[...] == 1, -heat[...], heat[...]))
    coded, = flatten(coded, (0,))
    coded_high = coded.astype(BF16).astype(F32)
    field_row = lax.broadcasted_iota(jnp.int32, (NFIELD, rows * SECTOR), 0)
    for index, one in enumerate(FIELDS):
        if one == COUPLING:
            near = jnp.where(field_row == index, coded_high, near)
        if one == LOW:
            near = jnp.where(field_row == index, coded - coded_high, near)
    turned = [near] + [roll_lanes(near, -SECTOR * k) for k in range(1, 4)]
    field8 = lax.broadcasted_iota(jnp.int32, (8, 128), 0)
    for i in range(rows):
        parts = []
        for part in range(NFIELD // 8):
            value = None
            for j in range(8):
                first = FIRSTS[8 * part + j]
                if j and first == FIRSTS[8 * part + j - 1]:
                    continue
                start = (i + first) % rows
                piece = turned[start % 4][8 * part : 8 * part + 8, 128 * (start // 4) : 128 * (start // 4) + 128]
                value = piece if value is None else jnp.where(field8 >= j, piece, value)
            parts.append(value)
        msg[i] = jnp.concatenate(parts, axis=0).astype(BF16)

    def stage_columns(step):
        col_out[step, 0] = pad[step, 1 : rows + 1, TOP, :]
        col_out[step, 1] = pad[step, 1 : rows + 1, TOP + SECTOR - 1, :]

    stage_columns(0)
    courant = [tile_rows([near[index : index + 1]] * 4) for index in (8, 9, 11, 12)]
    coef_out[0] = courant[0]
    coef_out[1] = courant[1]

    pl.semaphore_wait(barrier, naz - 1 + nax - 1 + 2 * REACH + jnp.where(at_rim, naz, 0))

    def remote(source, target, send, receive, to_ax, to_az):
        return pltpu.make_async_remote_copy(
            src_ref=source, dst_ref=target, send_sem=send, recv_sem=receive,
            device_id=(to_ax, to_az), device_id_type=MESH,
        )

    def wait_bytes(ref, sem):
        pltpu.make_async_copy(ref, ref, sem).wait()

    @pl.loop(0, REACH)
    def _(k):
        remote(msg.at[k, pl.ds(0, 32)], recv_nb.at[az], nb_sem.at[0], nb_sem.at[1], up_ax, k).start()
        high = naz - REACH + k
        remote(msg.at[high, pl.ds(16, 32)], recv_nb.at[az], nb_sem.at[0], nb_sem.at[1], down_ax, high).start()

    @pl.loop(1, naz)
    def _(k):
        to = lax.rem(az + k, naz)
        remote(msg.at[to], recv.at[az], msg_sem.at[0], msg_sem.at[1], ax, to).start()

    def send_row(ref, slot, reach, sems):
        for offset in range(-reach, reach + 1):
            if offset:
                to = lax.rem(flat + offset + total, total)
                remote(
                    ref.at[pl.ds(slot, 1)], ref.at[pl.ds(slot - offset, 1)], sems.at[0], sems.at[1],
                    lax.div(to, naz), lax.rem(to, naz),
                ).start()

    send_row(th_rows, 4, 4, th_sem)

    def times_table(value):
        high, low = split(value)
        count = value.shape[0]
        both = jnp.dot(jnp.concatenate([high, low], axis=0), hh[...], preferred_element_type=F32)
        return both[:count] + both[count:] + jnp.dot(high, hl[...], preferred_element_type=F32)

    def rows_times_table(value):
        count = value.shape[0]
        value = jnp.concatenate([value, jnp.zeros((8 - count, length), F32)], axis=0)
        high = value.astype(BF16).astype(F32)
        both = jnp.concatenate([high, value - high], axis=0).astype(BF16)
        first = jnp.dot(both, hh[...], preferred_element_type=F32)
        second = jnp.dot(both, hl[...], preferred_element_type=F32)
        return (first[0:8] + first[8:16] + second[0:8])[:count]

    loads["wall"].wait()
    loads["hh"].wait()
    loads["hl"].wait()
    layers = wall.shape[0]
    spectral = times_table(wall[...])
    loads["inv"].wait()
    mode_gain = inv[0, 0:1, :]
    mode_base = jnp.sum(inv[0] * spectral, axis=0, keepdims=True)
    base_rows[2:3, :] = mode_base
    send_row(base_rows, 2, 2, base_sem)

    def halo_copies(step):
        return (
            remote(pad.at[step, rows, inside], pad.at[step, 0, inside],
                   halo_ss.at[step, 0], halo_rs.at[step, 0], up_ax, az),
            remote(pad.at[step, 1, inside], pad.at[step, rows + 1, inside],
                   halo_ss.at[step, 1], halo_rs.at[step, 1], down_ax, az),
            remote(col_out.at[step, 1], col_in.at[step, 0],
                   halo_ss.at[step, 2], halo_rs.at[step, 2], ax, up_az),
            remote(col_out.at[step, 0], col_in.at[step, 1],
                   halo_ss.at[step, 3], halo_rs.at[step, 3], ax, down_az),
        )

    def send_halo(step):
        for copy in halo_copies(step):
            copy.start()

    def take_halo(step):
        for copy in halo_copies(step):
            copy.wait()

        @pl.when(ax == 0)
        def _():
            pad[step, 0, inside, :] = jnp.zeros((SECTOR, 128), F32)

        @pl.when(ax == nax - 1)
        def _():
            pad[step, rows + 1, inside, :] = jnp.zeros((SECTOR, 128), F32)

        pad[step, 1 : rows + 1, TOP - 1, :] = col_in[step, 0]
        pad[step, 1 : rows + 1, TOP + SECTOR, :] = col_in[step, 1]

    send_halo(0)
    coef_copies = [
        remote(coef_out, coef_in.at[slot], coef_ss.at[slot], coef_rs.at[slot], to_ax, to_az)
        for slot, (to_ax, to_az) in enumerate(((up_ax, az), (down_ax, az), (ax, up_az), (ax, down_az)))
    ]
    for copy in coef_copies:
        copy.start()
    recv[az] = msg[az]

    @pl.loop(0, layers // 2)
    def _(pair):
        for j in range(2):
            layer = 2 * pair + j
            blend[pl.ds(layer, 1), :] = jnp.sum(inv[layer] * spectral, axis=0, keepdims=True)

    lane_row = lax.broadcasted_iota(jnp.int32, (SECTOR, 128), 1)

    def sweep(step, store):
        @pl.loop(0, rows)
        def _(x):
            centre = pad[step, x + 1, inside, :]
            west = pad[step, x, inside, :]
            east = pad[step, x + 2, inside, :]
            south = pad[step, x + 1, pl.ds(TOP - 1, SECTOR), :]
            north = pad[step, x + 1, pl.ds(TOP + 1, SECTOR), :]
            inner = jnp.where(lane_row == 0, centre, roll_lanes(centre, 1))
            outer = jnp.where(lane_row == 127, 0.0, roll_lanes(centre, -1))
            store(x, (
                centre
                + tr[0, x].astype(F32) * (west - centre)
                + tr[1, x].astype(F32) * (south - centre)
                + DIFFUSE * (west + east + south + north - 4.0 * centre)
                + RADIAL * (inner + outer - 2.0 * centre)
                + tr[2, x].astype(F32)
            ))

    def store_pad(step):
        def store(x, value):
            pad[step, x + 1, inside, :] = value
        return store

    take_halo(0)
    sweep(0, store_pad(1))
    stage_columns(1)
    send_halo(1)

    wait_bytes(recv.at[pl.ds(0, naz - 1)], msg_sem.at[1])

    @pl.loop(0, naz)
    def _(source):
        fields[pl.ds(pl.multiple_of(source * NFIELD, NFIELD), NFIELD), :] = recv[source].astype(F32)

    def merge(start):
        firsts = jnp.zeros((32, 128), jnp.int32)
        index = lax.broadcasted_iota(jnp.int32, (32, 128), 0)
        for j in range(32):
            if j == 0 or FIRSTS[start + j] != FIRSTS[start + j - 1]:
                firsts = jnp.where(index >= j, FIRSTS[start + j], firsts)
        place = az + firsts + lax.broadcasted_iota(jnp.int32, (32, 128), 1) // SECTOR
        own = jnp.logical_and(place >= 0, place < rows)

        @pl.loop(0, naz)
        def _(source):
            here = pl.ds(pl.multiple_of(source * NFIELD + start, 16), 32)
            fields[here, :] = jnp.where(own, fields[here, :], recv_nb[source].astype(F32))

    @pl.when(low_edge)
    def _():
        wait_bytes(recv_nb, nb_sem.at[1])
        merge(0)

    @pl.when(high_edge)
    def _():
        wait_bytes(recv_nb, nb_sem.at[1])
        merge(16)

    def field(index):
        return fields[pl.ds(index, naz, stride=NFIELD), :]

    def in_domain(first):
        place = flat + first + group
        return jnp.logical_and(place >= 0, place < total)

    def masked(first, value):
        return jnp.where(in_domain(first), value, 0.0)

    gas_p = [masked(-5, field(j) + field(4 + j)) for j in range(4)]
    gas_q = [masked(-1, field(16 + j) + field(20 + j)) for j in range(4)]
    gas_r = [None] + [masked(2, field(32 + j) + field(35 + j)) for j in range(3)]
    coef_127 = [[field(8 + j) for j in range(3)], [field(40 + j) for j in range(3)]]
    coef_127.append([roll_lanes(field(j), -64) for j in (38, 39, 30)])
    coef_126 = [[field(11 + j) for j in range(3)], [field(43 + j) for j in range(3)]]
    coef_125 = [[field(24 + j) for j in range(3)], [field(27 + j) for j in range(3)]]
    coupling = [field(14) + field(15), field(46) + field(47)]

    def stencil(coef, centre, west, east, inner, outer):
        south = jnp.where(cell == 0, pltpu.roll(roll_lanes(centre, -31), 1, 0), roll_lanes(centre, 1))
        north = jnp.where(
            cell == SECTOR - 1, pltpu.roll(roll_lanes(centre, 31), naz - 1, 0), roll_lanes(centre, -1)
        )
        return (
            centre
            + coef[0] * (west - centre)
            + coef[1] * (south - centre)
            + DIFFUSE * (west + east + south + north - 4.0 * centre)
            + RADIAL * (inner + outer - 2.0 * centre)
            + coef[2]
        )

    def windows(p, q, r):
        if r is None:
            r = jnp.zeros_like(q)
        centres = (
            jnp.where(group == 3, roll_lanes(q, 96), roll_lanes(p, -32)),
            jnp.where(group == 3, roll_lanes(r, 64), roll_lanes(q, -32)),
        )
        easts = (
            jnp.where(group >= 2, roll_lanes(q, 64), roll_lanes(p, -64)),
            jnp.where(group >= 2, roll_lanes(r, 32), roll_lanes(q, -64)),
        )
        return centres, (p, q), easts

    def shifted(zero, one, two=None):
        west = (roll_lanes(zero, 32), jnp.where(group == 0, roll_lanes(zero, 32), roll_lanes(one, 32)))
        last = roll_lanes(one, -32)
        if two is not None:
            last = jnp.where(group == 3, roll_lanes(two, 96), last)
        east = (jnp.where(group == 3, roll_lanes(one, -32), roll_lanes(zero, -32)), last)
        return west, east

    none = jnp.zeros((naz, 128), F32)
    centre_124 = windows(gas_p[0], gas_q[0], None)[0]
    centre_125, west_125, east_125 = windows(gas_p[1], gas_q[1], gas_r[1])
    centre_126, west_126, east_126 = windows(gas_p[2], gas_q[2], gas_r[2])
    centre_127, west_127, east_127 = windows(gas_p[3], gas_q[3], gas_r[3])
    firsts = (-4, 0, 4)
    base = [
        masked(firsts[w], stencil(coef_127[w], centre_127[w], west_127[w], east_127[w], centre_126[w], none))
        for w in range(2)
    ]
    base.append(masked(4, stencil(
        coef_127[2], roll_lanes(gas_r[3], -64), roll_lanes(gas_r[3], -32), roll_lanes(gas_r[3], -96),
        roll_lanes(gas_r[2], -64), none,
    )))
    one_126 = [
        masked(firsts[w], stencil(coef_126[w], centre_126[w], west_126[w], east_126[w], centre_125[w], centre_127[w]))
        for w in range(2)
    ]
    one_125 = [
        stencil(coef_125[w], centre_125[w], west_125[w], east_125[w], centre_124[w], centre_126[w]) for w in range(2)
    ]
    west_one_126, east_one_126 = shifted(*one_126)

    def near_flux(edges, wanted):
        one = [base[w] + masked(firsts[w], RADIAL * edges[w]) for w in range(3)]
        west, east = shifted(*one)
        two = [
            masked(firsts[w], stencil(coef_127[w], one[w], west[w], east[w], one_126[w], edges[w])) for w in range(2)
        ]
        west, east = shifted(*two)
        result = []
        for w in wanted:
            two_126 = stencil(coef_126[w], one_126[w], west_one_126[w], east_one_126[w], one_125[w], one[w])
            three = stencil(coef_127[w], two[w], west[w], east[w], two_126, edges[w])
            result.append(jnp.where(
                coupling[w] < 0, -BED_COEF * edges[w], coupling[w] * (three - edges[w])
            ))
        return result

    shift = rot_ref[0]
    shift_back = length - shift

    def wall_face(flux, without):
        modes = rows_times_table(pltpu.roll(flux, shift_back, 1))
        face = rows_times_table(modes * mode_gain + without)
        return modes, pltpu.roll(face, shift, 1)

    wait_bytes(th_rows.at[pl.ds(0, 8)], th_sem.at[1])
    start = th_rows[0:9, :]
    rows_of = lambda values, *picks: tile_rows([None if k is None else values[k : k + 1] for k in picks])
    flux = near_flux(
        [rows_of(start, 0, 1, 2, 3), rows_of(start, 4, 5, 6, 7), rows_of(start, 8, None, None, None)], (0, 1)
    )
    flux = jnp.concatenate(flatten(flux[0], (2, 3)) + flatten(flux[1], (0, 1, 2)), axis=0)
    wait_bytes(base_rows.at[pl.ds(0, 4)], base_sem.at[1])
    _, face = wall_face(flux, base_rows[0:5, :])
    residual1 = face - start[2:7]
    theta1 = start[2:7] + FIRST_RELAX * residual1
    flux = near_flux(
        [rows_of(theta1, None, None, 0, 1), rows_of(theta1, 2, 3, 4, None), none], (1,)
    )
    modes, face = wall_face(flatten(flux[0], (0,))[0], mode_base)
    residual1 = residual1[2:3]
    theta1 = theta1[2:3]
    residual2 = face - theta1
    change = residual2 - residual1
    top = jnp.sum(residual1 * change, axis=1, keepdims=True)
    bottom = jnp.sum(change * change, axis=1, keepdims=True)
    lane1 = lax.broadcasted_iota(jnp.int32, (1, 128), 1)
    redsrc[0:1] = jnp.where(lane1 == 0, top, jnp.where(lane1 == 1, bottom, 0.0))

    @pl.loop(1, naz)
    def _(k):
        to = lax.rem(az + k, naz)
        remote(redsrc.at[pl.ds(0, 1)], redbuf.at[0, pl.ds(az, 1)], red_sem.at[0], red_sem.at[1], ax, to).start()

    redbuf[0, pl.ds(az, 1), :] = redsrc[0:1]

    turned = [roll_lanes(theta1, -SECTOR * (p - 1)) for p in range(4)]
    window[...] = jnp.concatenate(
        [turned[k % 4][:, 128 * (k // 4) : 128 * (k // 4) + 128] for k in range(naz)], axis=0
    )

    @pl.loop(1, naz)
    def _(k):
        to = lax.rem(az + k, naz)
        remote(
            window.at[pl.ds(to, 1)], edge.at[pl.ds(TOP + az, 1)], edge_sem.at[0], edge_sem.at[1], ax, to
        ).start()

    rim_ax = jnp.where(az < 2, down_ax, up_ax)
    rim_row = jnp.where(az < 2, TOP + rows + az, TOP - naz + az)

    @pl.when(at_rim)
    def _():
        @pl.loop(0, naz)
        def _(k):
            remote(
                window.at[pl.ds(k, 1)], edge.at[pl.ds(rim_row, 1)], edge_sem.at[2], edge_sem.at[3], rim_ax, k
            ).start()

    edge[pl.ds(TOP + az, 1), :] = window[pl.ds(az, 1), :]

    wall_res[...] = times_table(blend[...] + inv[:, 0, :] * modes)

    take_halo(1)
    sweep(1, store_pad(2))
    stage_columns(2)
    send_halo(2)

    wait_bytes(redbuf.at[0, pl.ds(0, naz - 1)], red_sem.at[1])
    redsrc[1:2] = jnp.sum(redbuf[0, 0:naz], axis=0, keepdims=True)

    @pl.loop(1, nax)
    def _(k):
        to = lax.rem(ax + k, nax)
        remote(redsrc.at[pl.ds(1, 1)], redbuf.at[1, pl.ds(ax, 1)], red_sem.at[2], red_sem.at[3], to, az).start()

    redbuf[1, pl.ds(ax, 1), :] = redsrc[1:2]

    take_halo(2)

    def store_result(x, value):
        gas_res[x] = value

    sweep(2, store_result)

    for copy in coef_copies:
        copy.wait()
    wait_bytes(edge.at[pl.ds(0, naz - 1)], edge_sem.at[1])
    wait_bytes(edge.at[pl.ds(0, 4)], edge_sem.at[3])
    tall = rows + 2 * TOP
    place = lax.broadcasted_iota(jnp.int32, (tall, 128), 0)
    row_x = ax * rows + place - TOP
    valid = jnp.logical_and(jnp.logical_and(row_x >= 0, row_x < total),
                            jnp.logical_and(place >= TOP - 2, place < TOP + rows + 2))
    theta = jnp.where(valid, edge[...], 0.0)

    def tall_coef(j):
        middle = jnp.where(group == 0, coef_in[2, j], jnp.where(group == 2, coef_in[3, j], courant[j]))
        below = jnp.broadcast_to(coef_in[0, j, rows - 1 : rows, :], (TOP, 128))
        above = jnp.broadcast_to(coef_in[1, j, 0:1, :], (TOP, 128))
        return jnp.concatenate([below, middle, above], axis=0)

    def tall_only(value):
        return jnp.concatenate([jnp.zeros((TOP, 128), F32), value, jnp.zeros((TOP, 128), F32)], axis=0)

    def answer(coef_x, coef_a, centre):
        west, east = pltpu.roll(centre, 1, 0), pltpu.roll(centre, tall - 1, 0)
        south, north = roll_lanes(centre, 1), roll_lanes(centre, -1)
        return (
            centre + coef_x * (west - centre) + coef_a * (south - centre)
            + DIFFUSE * (west + east + south + north - 4.0 * centre)
        )

    coef_x, coef_a = tall_coef(0), tall_coef(1)
    first = RADIAL * theta
    second = jnp.where(valid, answer(coef_x, coef_a, first) + RADIAL * (theta - 2.0 * first), 0.0)
    second_126 = RADIAL * first
    third = answer(coef_x, coef_a, second) + RADIAL * (second_126 + theta - 2.0 * second)
    third_126 = answer(tall_only(courant[2]), tall_only(courant[3]), second_126) + RADIAL * (second - 2.0 * second_126)
    third_125 = RADIAL * second_126
    added = [flatten(value[TOP : TOP + rows], (1,))[0] for value in (third_125, third_126, third)]
    added = jnp.concatenate(added + [jnp.zeros((5, length), F32)], axis=0)
    added_high = added.astype(BF16).astype(F32)
    added = jnp.concatenate([added_high, added - added_high], axis=0).astype(BF16)
    radius = lax.broadcasted_iota(jnp.int32, (16, 128), 1) - 125
    which = lax.broadcasted_iota(jnp.int32, (16, 128), 0) % 8
    spread = jnp.where(jnp.logical_and(radius == which, which < 3), 1.0, 0.0).astype(BF16)
    added = lax.dot_general(added, spread, (((0,), (0,)), ((), ())), preferred_element_type=F32)
    gas_res[...] = gas_res[...] + added.reshape(rows, SECTOR, 128)

    wait_bytes(redbuf.at[1, pl.ds(0, nax - 1)], red_sem.at[3])
    sums = jnp.sum(redbuf[1, 0:nax], axis=0, keepdims=True)
    top = jnp.sum(jnp.where(lane1 == 0, sums, 0.0), axis=1, keepdims=True)
    bottom = jnp.sum(jnp.where(lane1 == 1, sums, 0.0), axis=1, keepdims=True)
    relax = -FIRST_RELAX * top / (bottom + TINY)
    th_res[...] = theta1 + relax * residual2

    wait_bytes(msg.at[pl.ds(0, naz - 1)], msg_sem.at[0])
    wait_bytes(msg.at[pl.ds(0, 2 * REACH), pl.ds(0, 32)], nb_sem.at[0])
    wait_bytes(th_rows.at[pl.ds(0, 8)], th_sem.at[0])
    wait_bytes(base_rows.at[pl.ds(0, 4)], base_sem.at[0])
    wait_bytes(edge.at[pl.ds(0, naz - 1)], edge_sem.at[0])

    @pl.when(at_rim)
    def _():
        wait_bytes(edge.at[pl.ds(0, naz)], edge_sem.at[2])

    wait_bytes(redbuf.at[0, pl.ds(0, naz - 1)], red_sem.at[0])
    wait_bytes(redbuf.at[1, pl.ds(0, nax - 1)], red_sem.at[2])


def write_out(gas_res, wall_res, th_res, gas_out, wall_out, th_out, sem):
    copies = [
        pltpu.make_async_copy(source, target, sem.at[index])
        for index, (source, target) in enumerate(((gas_res, gas_out), (wall_res, wall_out), (th_res, th_out)))
    ]
    for copy in copies:
        copy.start()
    for copy in copies:
        copy.wait()


def on_device(
    nax, naz, gas_init, transport, heat_coef, bed_mask, wall_init, interface_init, inverse_blocks, rotation
):
    rows = gas_init.shape[0]
    layers, length = wall_init.shape[1:]
    table_high, table_low = hartley_parts(length)
    anywhere = pl.BlockSpec(memory_space=pltpu.HBM)
    vmem = pl.BlockSpec(memory_space=pltpu.VMEM)
    dma = pltpu.SemaphoreType.DMA
    operands = [
        pltpu.with_memory_space_constraint(value, pltpu.HBM)
        for value in (
            gas_init, transport, heat_coef, bed_mask, wall_init.reshape(layers, length), interface_init,
            jnp.transpose(inverse_blocks, (1, 2, 0)),
            jnp.asarray(table_high), jnp.asarray(table_low), jnp.asarray(selector()),
        )
    ]
    gas_now, wall_now, theta = pl.pallas_call(
        functools.partial(kernel, nax, naz),
        out_shape=(
            jax.ShapeDtypeStruct(gas_init.shape, F32),
            jax.ShapeDtypeStruct((layers, length), F32),
            jax.ShapeDtypeStruct((1, length), F32),
        ),
        in_specs=[anywhere] * 7 + [pl.BlockSpec(memory_space=pltpu.SMEM)] + [anywhere] * 3,
        out_specs=(vmem,) * 3,
        scratch_shapes=[
            pltpu.VMEM((3, rows + 2, SECTOR + 2 * TOP, 128), F32),
            pltpu.VMEM(transport.shape, BF16),
            pltpu.VMEM(heat_coef.shape, F32),
            pltpu.VMEM(bed_mask.shape, jnp.int32),
            pltpu.VMEM((layers, length), F32),
            pltpu.VMEM((1, length), F32),
            pltpu.VMEM((layers, layers, length), F32),
            pltpu.VMEM((length, length), BF16),
            pltpu.VMEM((length, length), BF16),
            pltpu.VMEM((NFIELD, 5 * 128), BF16),
            pltpu.VMEM((rows, NFIELD, 128), BF16),
            pltpu.VMEM((naz, NFIELD, 128), BF16),
            pltpu.VMEM((naz, 32, 128), BF16),
            pltpu.VMEM((naz * NFIELD, 128), F32),
            pltpu.VMEM((16, length), F32),
            pltpu.VMEM((8, length), F32),
            pltpu.VMEM((naz, 128), F32),
            pltpu.VMEM((rows + 2 * TOP, 128), F32),
            pltpu.VMEM((2, rows, 128), F32),
            pltpu.VMEM((4, 2, rows, 128), F32),
            pltpu.VMEM((3, 2, rows, 128), F32),
            pltpu.VMEM((3, 2, rows, 128), F32),
            pltpu.VMEM((layers, length), F32),
            pltpu.VMEM((2, 128), F32),
            pltpu.VMEM((2, max(nax, naz), 128), F32),
            dma((10,)),
            dma((2,)),
            dma((2,)),
            dma((2,)),
            dma((2,)),
            dma((4,)),
            dma((3, 4)),
            dma((3, 4)),
            dma((4,)),
            dma((4,)),
            dma((4,)),
        ],
        compiler_params=pltpu.CompilerParams(
            collective_id=0, has_side_effects=True, vmem_limit_bytes=48 * 1024 * 1024
        ),
        name="kiln_step",
    )(
        *operands[:7], rotation, *operands[7:],
    )
    gas_now, wall_now, theta = pl.pallas_call(
        write_out,
        out_shape=[jax.ShapeDtypeStruct(value.shape, F32) for value in (gas_now, wall_now, theta)],
        in_specs=[vmem] * 3,
        out_specs=[anywhere] * 3,
        scratch_shapes=[dma((3,))],
        compiler_params=pltpu.CompilerParams(vmem_limit_bytes=1024 * 1024),
        name="write_out",
    )(gas_now, wall_now, theta)
    return gas_now, wall_now.reshape(1, layers, length), theta


def solution(mesh):
    return jax.shard_map(
        functools.partial(on_device, mesh.shape["ax"], mesh.shape["az"]),
        mesh=mesh,
        in_specs=(
            P("ax", "az", None),
            P(None, "ax", "az", None),
            P("ax", "az"),
            P("ax", "az"),
            P(("ax", "az"), None, None),
            P(("ax", "az"), None),
            P(),
            P(),
        ),
        out_specs=(P("ax", "az", None), P(("ax", "az"), None, None), P(("ax", "az"), None)),
        check_vma=False,
    )
```

```python
import functools

import jax
import jax.numpy as jnp
import ml_dtypes
import numpy as np
from jax import lax
from jax.experimental import pallas as pl
from jax.experimental.pallas import tpu as pltpu
from jax.sharding import PartitionSpec as P

DIFFUSE = 0.04
RADIAL = 0.06
BED_COEF = 0.8
FIRST_RELAX = 0.5
TINY = 1e-06
MESH = pl.DeviceIdType.MESH
F32 = jnp.float32
BF16 = jnp.bfloat16
SECTOR = 32
TOP = 8
COUPLING, LOW = "coupling", "low"
GAS = [(part, r) for part in (0, 1) for r in (124, 125, 126, 127)]
WALLSIDE = [(2, 127), (3, 127), (4, 127), (2, 126), (3, 126), (4, 126), COUPLING, LOW]
FIELDS = (
    GAS
    + WALLSIDE
    + GAS
    + [(2, 125), (3, 125), (4, 125)] * 2 + [(4, 127), None]
    + [(part, r) for part in (0, 1) for r in (125, 126, 127)] + [(2, 127), (3, 127)]
    + WALLSIDE
)
NFIELD = len(FIELDS)
FIRSTS = [-5] * 8 + [-4] * 8 + [-1] * 8 + [-4] * 3 + [0] * 3 + [2] * 2 + [2] * 8 + [0] * 8
REACH = 5


def hartley_parts(length):
    positions = np.arange(length, dtype=np.int64)
    phases = 2.0 * np.pi / length * ((positions[:, None] * positions[None, :]) % length)
    table = ((np.cos(phases) + np.sin(phases)) / np.sqrt(length)).astype(np.float32)
    high = table.astype(ml_dtypes.bfloat16)
    low = (table - high.astype(np.float32)).astype(ml_dtypes.bfloat16)
    return high, low


def selector():
    table = np.zeros((NFIELD, 5 * 128), np.float32)
    for row, field in enumerate(FIELDS):
        if isinstance(field, tuple):
            table[row, field[0] * 128 + field[1]] = 1.0
    return table.astype(ml_dtypes.bfloat16)


def split(value):
    high = value.astype(BF16)
    return high, (value - high.astype(F32)).astype(BF16)


def roll_lanes(value, amount):
    amount = amount % value.shape[1]
    return pltpu.roll(value, amount, 1) if amount else value


def kernel(
    nax, naz,
    gas_hbm, tr_hbm, heat_hbm, bed_hbm, wall_hbm, th_hbm, inv_hbm, rot_ref, hh_hbm, hl_hbm, sel_hbm,
    gas_res, wall_res, th_res,
    pad, tr, heat, bed, wall, th, inv, hh, hl, sel,
    msg, recv, recv_nb, fields, th_rows, base_rows, window, edge, coef_out, coef_in, col_out, col_in, blend,
    redsrc, redbuf,
    load_sem, msg_sem, nb_sem, th_sem, base_sem, edge_sem, halo_ss, halo_rs, coef_ss, coef_rs, red_sem,
):
    ax, az = lax.axis_index("ax"), lax.axis_index("az")
    rows = naz
    length = SECTOR * naz
    quads = length // 128
    total = nax * rows
    flat = ax * naz + az
    up_ax, down_ax = lax.rem(ax + 1, nax), lax.rem(ax + nax - 1, nax)
    up_az, down_az = lax.rem(az + 1, naz), lax.rem(az + naz - 1, naz)
    inside = pl.ds(TOP, SECTOR)

    loads = {}
    for index, (name, source, target) in enumerate((
        ("gas", gas_hbm, pad.at[0, pl.ds(1, rows), inside]),
        ("tr", tr_hbm, tr),
        ("heat", heat_hbm, heat),
        ("bed", bed_hbm, bed),
        ("sel", sel_hbm, sel),
        ("th", th_hbm, th),
        ("wall", wall_hbm, wall),
        ("hh", hh_hbm, hh),
        ("hl", hl_hbm, hl),
        ("inv", inv_hbm, inv),
    )):
        loads[name] = pltpu.make_async_copy(source, target, load_sem.at[index])
        loads[name].start()

    barrier = pltpu.get_barrier_semaphore()

    def greet(to_ax, to_az):
        pl.semaphore_signal(barrier, inc=1, device_id=(to_ax, to_az), device_id_type=MESH)

    @pl.loop(1, naz)
    def _(k):
        greet(ax, lax.rem(az + k, naz))

    @pl.loop(1, nax)
    def _(k):
        greet(lax.rem(ax + k, nax), az)

    low_edge, high_edge = az < REACH, az >= naz - REACH
    at_edge = jnp.logical_or(low_edge, high_edge)
    beside = jnp.where(low_edge, down_ax, up_ax)
    at_rim = jnp.logical_or(az < 2, az >= naz - 2)

    @pl.when(at_edge)
    def _():
        @pl.loop(0, naz)
        def _(k):
            greet(beside, k)

    for k in range(2):
        greet(up_ax, k)
        greet(down_ax, naz - 2 + k)

    lane = lax.broadcasted_iota(jnp.int32, (naz, 128), 1)
    sector = lax.broadcasted_iota(jnp.int32, (naz, 128), 0)
    cell = lane % SECTOR
    group = lane // SECTOR
    turn = sector % 4

    def tile_rows(values):
        result = jnp.zeros((naz, 128), F32)
        for g, row in enumerate(values):
            if row is None:
                continue
            wide = jnp.concatenate(
                [jnp.broadcast_to(row[:, 128 * q : 128 * q + 128], (4, 128)) for q in range(quads)], axis=0
            )
            for p in range(4):
                here = jnp.logical_and(turn == p, group == g)
                result = jnp.where(here, roll_lanes(wide, SECTOR * (g - p)), result)
        return result

    def flatten(value, groups):
        moved = [roll_lanes(value, SECTOR * k) for k in range(4)]
        found = []
        for g in groups:
            result = jnp.zeros_like(value)
            for p in range(4):
                result = jnp.where(jnp.logical_and(turn == p, group == p), moved[(p - g) % 4], result)
            parts = [jnp.sum(result[4 * q : 4 * q + 4], axis=0, keepdims=True) for q in range(quads)]
            found.append(jnp.concatenate(parts, axis=1))
        return found

    def four_times(value):
        return jnp.concatenate([value] * 4, axis=1)

    loads["th"].wait()
    theta0 = th[...]
    th_rows[4:5, :] = theta0

    for name in ("gas", "tr", "heat", "bed", "sel"):
        loads[name].wait()
    gas = pad[0, 1 : rows + 1, TOP : TOP + SECTOR, :].reshape(rows * SECTOR, 128)
    gas_high, gas_low = split(gas)
    stacked = jnp.concatenate(
        [gas_high, gas_low] + [tr[j].reshape(rows * SECTOR, 128) for j in range(3)], axis=1
    )
    near = lax.dot_general(
        sel[...], stacked, (((1,), (1,)), ((), ())), preferred_element_type=F32
    )
    coded = four_times(jnp.where(bed[...] == 1, -heat[...], heat[...]))
    coded, = flatten(coded, (0,))
    coded_high = coded.astype(BF16).astype(F32)
    field_row = lax.broadcasted_iota(jnp.int32, (NFIELD, rows * SECTOR), 0)
    for index, one in enumerate(FIELDS):
        if one == COUPLING:
            near = jnp.where(field_row == index, coded_high, near)
        if one == LOW:
            near = jnp.where(field_row == index, coded - coded_high, near)
    turned = [near] + [roll_lanes(near, -SECTOR * k) for k in range(1, 4)]
    field8 = lax.broadcasted_iota(jnp.int32, (8, 128), 0)
    for i in range(rows):
        parts = []
        for part in range(NFIELD // 8):
            value = None
            for j in range(8):
                first = FIRSTS[8 * part + j]
                if j and first == FIRSTS[8 * part + j - 1]:
                    continue
                start = (i + first) % rows
                piece = turned[start % 4][8 * part : 8 * part + 8, 128 * (start // 4) : 128 * (start // 4) + 128]
                value = piece if value is None else jnp.where(field8 >= j, piece, value)
            parts.append(value)
        msg[i] = jnp.concatenate(parts, axis=0).astype(BF16)

    def stage_columns(step):
        col_out[step, 0] = pad[step, 1 : rows + 1, TOP, :]
        col_out[step, 1] = pad[step, 1 : rows + 1, TOP + SECTOR - 1, :]

    stage_columns(0)
    courant = [tile_rows([near[index : index + 1]] * 4) for index in (8, 9, 11, 12)]
    coef_out[0] = courant[0]
    coef_out[1] = courant[1]

    pl.semaphore_wait(barrier, naz - 1 + nax - 1 + 2 * REACH + jnp.where(at_rim, naz, 0))

    def remote(source, target, send, receive, to_ax, to_az):
        return pltpu.make_async_remote_copy(
            src_ref=source, dst_ref=target, send_sem=send, recv_sem=receive,
            device_id=(to_ax, to_az), device_id_type=MESH,
        )

    def wait_bytes(ref, sem):
        pltpu.make_async_copy(ref, ref, sem).wait()

    def send_row(ref, slot, reach, sems):
        for offset in range(-reach, reach + 1):
            if offset:
                to = lax.rem(flat + offset + total, total)
                remote(
                    ref.at[pl.ds(slot, 1)], ref.at[pl.ds(slot - offset, 1)], sems.at[0], sems.at[1],
                    lax.div(to, naz), lax.rem(to, naz),
                ).start()

    send_row(th_rows, 4, 4, th_sem)

    def halo_copies(step):
        return (
            remote(pad.at[step, rows, inside], pad.at[step, 0, inside],
                   halo_ss.at[step, 0], halo_rs.at[step, 0], up_ax, az),
            remote(pad.at[step, 1, inside], pad.at[step, rows + 1, inside],
                   halo_ss.at[step, 1], halo_rs.at[step, 1], down_ax, az),
            remote(col_out.at[step, 1], col_in.at[step, 0],
                   halo_ss.at[step, 2], halo_rs.at[step, 2], ax, up_az),
            remote(col_out.at[step, 0], col_in.at[step, 1],
                   halo_ss.at[step, 3], halo_rs.at[step, 3], ax, down_az),
        )

    def send_halo(step):
        for copy in halo_copies(step):
            copy.start()

    send_halo(0)

    @pl.loop(0, REACH)
    def _(k):
        remote(msg.at[k, pl.ds(0, 32)], recv_nb.at[az], nb_sem.at[0], nb_sem.at[1], up_ax, k).start()
        high = naz - REACH + k
        remote(msg.at[high, pl.ds(16, 32)], recv_nb.at[az], nb_sem.at[0], nb_sem.at[1], down_ax, high).start()

    @pl.loop(1, naz)
    def _(k):
        to = lax.rem(az + k, naz)
        remote(msg.at[to], recv.at[az], msg_sem.at[0], msg_sem.at[1], ax, to).start()

    def times_table(value):
        high, low = split(value)
        count = value.shape[0]
        both = jnp.dot(jnp.concatenate([high, low], axis=0), hh[...], preferred_element_type=F32)
        return both[:count] + both[count:] + jnp.dot(high, hl[...], preferred_element_type=F32)

    def rows_times_table(value):
        count = value.shape[0]
        value = jnp.concatenate([value, jnp.zeros((8 - count, length), F32)], axis=0)
        high = value.astype(BF16).astype(F32)
        both = jnp.concatenate([high, value - high], axis=0).astype(BF16)
        first = jnp.dot(both, hh[...], preferred_element_type=F32)
        second = jnp.dot(both, hl[...], preferred_element_type=F32)
        return (first[0:8] + first[8:16] + second[0:8])[:count]

    loads["wall"].wait()
    loads["hh"].wait()
    loads["hl"].wait()
    layers = wall.shape[0]
    spectral = times_table(wall[...])
    loads["inv"].wait()
    mode_gain = inv[0, 0:1, :]
    mode_base = jnp.sum(inv[0] * spectral, axis=0, keepdims=True)
    base_rows[2:3, :] = mode_base
    send_row(base_rows, 2, 2, base_sem)

    def take_halo(step):
        for copy in halo_copies(step):
            copy.wait()

        @pl.when(ax == 0)
        def _():
            pad[step, 0, inside, :] = jnp.zeros((SECTOR, 128), F32)

        @pl.when(ax == nax - 1)
        def _():
            pad[step, rows + 1, inside, :] = jnp.zeros((SECTOR, 128), F32)

        pad[step, 1 : rows + 1, TOP - 1, :] = col_in[step, 0]
        pad[step, 1 : rows + 1, TOP + SECTOR, :] = col_in[step, 1]

    coef_copies = [
        remote(coef_out, coef_in.at[slot], coef_ss.at[slot], coef_rs.at[slot], to_ax, to_az)
        for slot, (to_ax, to_az) in enumerate(((up_ax, az), (down_ax, az), (ax, up_az), (ax, down_az)))
    ]
    for copy in coef_copies:
        copy.start()
    recv[az] = msg[az]

    @pl.loop(0, layers // 2)
    def _(pair):
        for j in range(2):
            layer = 2 * pair + j
            blend[pl.ds(layer, 1), :] = jnp.sum(inv[layer] * spectral, axis=0, keepdims=True)

    lane_row = lax.broadcasted_iota(jnp.int32, (SECTOR, 128), 1)

    def sweep(step, store):
        @pl.loop(0, rows)
        def _(x):
            centre = pad[step, x + 1, inside, :]
            west = pad[step, x, inside, :]
            east = pad[step, x + 2, inside, :]
            south = pad[step, x + 1, pl.ds(TOP - 1, SECTOR), :]
            north = pad[step, x + 1, pl.ds(TOP + 1, SECTOR), :]
            inner = jnp.where(lane_row == 0, centre, roll_lanes(centre, 1))
            outer = jnp.where(lane_row == 127, 0.0, roll_lanes(centre, -1))
            store(x, (
                centre
                + tr[0, x].astype(F32) * (west - centre)
                + tr[1, x].astype(F32) * (south - centre)
                + DIFFUSE * (west + east + south + north - 4.0 * centre)
                + RADIAL * (inner + outer - 2.0 * centre)
                + tr[2, x].astype(F32)
            ))

    def store_pad(step):
        def store(x, value):
            pad[step, x + 1, inside, :] = value
        return store

    take_halo(0)
    sweep(0, store_pad(1))
    stage_columns(1)
    send_halo(1)

    wait_bytes(recv.at[pl.ds(0, naz - 1)], msg_sem.at[1])

    @pl.loop(0, naz, unroll=True)
    def _(source):
        fields[pl.ds(pl.multiple_of(source * NFIELD, NFIELD), NFIELD), :] = recv[source].astype(F32)

    def merge(start):
        firsts = jnp.zeros((32, 128), jnp.int32)
        index = lax.broadcasted_iota(jnp.int32, (32, 128), 0)
        for j in range(32):
            if j == 0 or FIRSTS[start + j] != FIRSTS[start + j - 1]:
                firsts = jnp.where(index >= j, FIRSTS[start + j], firsts)
        place = az + firsts + lax.broadcasted_iota(jnp.int32, (32, 128), 1) // SECTOR
        own = jnp.logical_and(place >= 0, place < rows)

        @pl.loop(0, naz, unroll=4)
        def _(source):
            here = pl.ds(pl.multiple_of(source * NFIELD + start, 16), 32)
            fields[here, :] = jnp.where(own, fields[here, :], recv_nb[source].astype(F32))

    @pl.when(low_edge)
    def _():
        wait_bytes(recv_nb, nb_sem.at[1])
        merge(0)

    @pl.when(high_edge)
    def _():
        wait_bytes(recv_nb, nb_sem.at[1])
        merge(16)

    def field(index):
        return fields[pl.ds(index, naz, stride=NFIELD), :]

    def in_domain(first):
        place = flat + first + group
        return jnp.logical_and(place >= 0, place < total)

    def masked(first, value):
        return jnp.where(in_domain(first), value, 0.0)

    gas_p = [masked(-5, field(j) + field(4 + j)) for j in range(4)]
    gas_q = [masked(-1, field(16 + j) + field(20 + j)) for j in range(4)]
    gas_r = [None] + [masked(2, field(32 + j) + field(35 + j)) for j in range(3)]
    coef_127 = [[field(8 + j) for j in range(3)], [field(40 + j) for j in range(3)]]
    coef_127.append([roll_lanes(field(j), -64) for j in (38, 39, 30)])
    coef_126 = [[field(11 + j) for j in range(3)], [field(43 + j) for j in range(3)]]
    coef_125 = [[field(24 + j) for j in range(3)], [field(27 + j) for j in range(3)]]
    coupling = [field(14) + field(15), field(46) + field(47)]

    def stencil(coef, centre, west, east, inner, outer):
        south = jnp.where(cell == 0, pltpu.roll(roll_lanes(centre, -31), 1, 0), roll_lanes(centre, 1))
        north = jnp.where(
            cell == SECTOR - 1, pltpu.roll(roll_lanes(centre, 31), naz - 1, 0), roll_lanes(centre, -1)
        )
        return (
            centre
            + coef[0] * (west - centre)
            + coef[1] * (south - centre)
            + DIFFUSE * (west + east + south + north - 4.0 * centre)
            + RADIAL * (inner + outer - 2.0 * centre)
            + coef[2]
        )

    def windows(p, q, r):
        if r is None:
            r = jnp.zeros_like(q)
        centres = (
            jnp.where(group == 3, roll_lanes(q, 96), roll_lanes(p, -32)),
            jnp.where(group == 3, roll_lanes(r, 64), roll_lanes(q, -32)),
        )
        easts = (
            jnp.where(group >= 2, roll_lanes(q, 64), roll_lanes(p, -64)),
            jnp.where(group >= 2, roll_lanes(r, 32), roll_lanes(q, -64)),
        )
        return centres, (p, q), easts

    def shifted(zero, one, two=None):
        west = (roll_lanes(zero, 32), jnp.where(group == 0, roll_lanes(zero, 32), roll_lanes(one, 32)))
        last = roll_lanes(one, -32)
        if two is not None:
            last = jnp.where(group == 3, roll_lanes(two, 96), last)
        east = (jnp.where(group == 3, roll_lanes(one, -32), roll_lanes(zero, -32)), last)
        return west, east

    none = jnp.zeros((naz, 128), F32)
    centre_124 = windows(gas_p[0], gas_q[0], None)[0]
    centre_125, west_125, east_125 = windows(gas_p[1], gas_q[1], gas_r[1])
    centre_126, west_126, east_126 = windows(gas_p[2], gas_q[2], gas_r[2])
    centre_127, west_127, east_127 = windows(gas_p[3], gas_q[3], gas_r[3])
    firsts = (-4, 0, 4)
    base = [
        masked(firsts[w], stencil(coef_127[w], centre_127[w], west_127[w], east_127[w], centre_126[w], none))
        for w in range(2)
    ]
    base.append(masked(4, stencil(
        coef_127[2], roll_lanes(gas_r[3], -64), roll_lanes(gas_r[3], -32), roll_lanes(gas_r[3], -96),
        roll_lanes(gas_r[2], -64), none,
    )))
    one_126 = [
        masked(firsts[w], stencil(coef_126[w], centre_126[w], west_126[w], east_126[w], centre_125[w], centre_127[w]))
        for w in range(2)
    ]
    one_125 = [
        stencil(coef_125[w], centre_125[w], west_125[w], east_125[w], centre_124[w], centre_126[w]) for w in range(2)
    ]
    west_one_126, east_one_126 = shifted(*one_126)

    def near_flux(edges, wanted):
        one = [base[w] + masked(firsts[w], RADIAL * edges[w]) for w in range(3)]
        west, east = shifted(*one)
        two = [
            masked(firsts[w], stencil(coef_127[w], one[w], west[w], east[w], one_126[w], edges[w])) for w in range(2)
        ]
        west, east = shifted(*two)
        result = []
        for w in wanted:
            two_126 = stencil(coef_126[w], one_126[w], west_one_126[w], east_one_126[w], one_125[w], one[w])
            three = stencil(coef_127[w], two[w], west[w], east[w], two_126, edges[w])
            result.append(jnp.where(
                coupling[w] < 0, -BED_COEF * edges[w], coupling[w] * (three - edges[w])
            ))
        return result

    shift = rot_ref[0]
    shift_back = length - shift

    def wall_face(flux, without):
        modes = rows_times_table(pltpu.roll(flux, shift_back, 1))
        face = rows_times_table(modes * mode_gain + without)
        return modes, pltpu.roll(face, shift, 1)

    wait_bytes(th_rows.at[pl.ds(0, 8)], th_sem.at[1])
    start = th_rows[0:9, :]
    rows_of = lambda values, *picks: tile_rows([None if k is None else values[k : k + 1] for k in picks])
    flux = near_flux(
        [rows_of(start, 0, 1, 2, 3), rows_of(start, 4, 5, 6, 7), rows_of(start, 8, None, None, None)], (0, 1)
    )
    flux = jnp.concatenate(flatten(flux[0], (2, 3)) + flatten(flux[1], (0, 1, 2)), axis=0)
    wait_bytes(base_rows.at[pl.ds(0, 4)], base_sem.at[1])
    _, face = wall_face(flux, base_rows[0:5, :])
    residual1 = face - start[2:7]
    theta1 = start[2:7] + FIRST_RELAX * residual1
    flux = near_flux(
        [rows_of(theta1, None, None, 0, 1), rows_of(theta1, 2, 3, 4, None), none], (1,)
    )
    modes, face = wall_face(flatten(flux[0], (0,))[0], mode_base)
    residual1 = residual1[2:3]
    theta1 = theta1[2:3]
    residual2 = face - theta1
    change = residual2 - residual1
    top = jnp.sum(residual1 * change, axis=1, keepdims=True)
    bottom = jnp.sum(change * change, axis=1, keepdims=True)
    lane1 = lax.broadcasted_iota(jnp.int32, (1, 128), 1)
    redsrc[0:1] = jnp.where(lane1 == 0, top, jnp.where(lane1 == 1, bottom, 0.0))

    @pl.loop(1, naz)
    def _(k):
        to = lax.rem(az + k, naz)
        remote(redsrc.at[pl.ds(0, 1)], redbuf.at[0, pl.ds(az, 1)], red_sem.at[0], red_sem.at[1], ax, to).start()

    redbuf[0, pl.ds(az, 1), :] = redsrc[0:1]

    turned = [roll_lanes(theta1, -SECTOR * (p - 1)) for p in range(4)]
    window[...] = jnp.concatenate(
        [turned[k % 4][:, 128 * (k // 4) : 128 * (k // 4) + 128] for k in range(naz)], axis=0
    )

    @pl.loop(1, naz)
    def _(k):
        to = lax.rem(az + k, naz)
        remote(
            window.at[pl.ds(to, 1)], edge.at[pl.ds(TOP + az, 1)], edge_sem.at[0], edge_sem.at[1], ax, to
        ).start()

    rim_ax = jnp.where(az < 2, down_ax, up_ax)
    rim_row = jnp.where(az < 2, TOP + rows + az, TOP - naz + az)

    @pl.when(at_rim)
    def _():
        @pl.loop(0, naz)
        def _(k):
            remote(
                window.at[pl.ds(k, 1)], edge.at[pl.ds(rim_row, 1)], edge_sem.at[2], edge_sem.at[3], rim_ax, k
            ).start()

    edge[pl.ds(TOP + az, 1), :] = window[pl.ds(az, 1), :]

    wall_res[...] = times_table(blend[...] + inv[:, 0, :] * modes)

    take_halo(1)
    sweep(1, store_pad(2))
    stage_columns(2)
    send_halo(2)

    wait_bytes(redbuf.at[0, pl.ds(0, naz - 1)], red_sem.at[1])
    redsrc[1:2] = jnp.sum(redbuf[0, 0:naz], axis=0, keepdims=True)

    @pl.loop(1, nax)
    def _(k):
        to = lax.rem(ax + k, nax)
        remote(redsrc.at[pl.ds(1, 1)], redbuf.at[1, pl.ds(ax, 1)], red_sem.at[2], red_sem.at[3], to, az).start()

    redbuf[1, pl.ds(ax, 1), :] = redsrc[1:2]

    take_halo(2)

    def store_result(x, value):
        gas_res[x] = value

    sweep(2, store_result)

    for copy in coef_copies:
        copy.wait()
    wait_bytes(edge.at[pl.ds(0, naz - 1)], edge_sem.at[1])
    wait_bytes(edge.at[pl.ds(0, 4)], edge_sem.at[3])
    tall = rows + 2 * TOP
    place = lax.broadcasted_iota(jnp.int32, (tall, 128), 0)
    row_x = ax * rows + place - TOP
    valid = jnp.logical_and(jnp.logical_and(row_x >= 0, row_x < total),
                            jnp.logical_and(place >= TOP - 2, place < TOP + rows + 2))
    theta = jnp.where(valid, edge[...], 0.0)

    def tall_coef(j):
        middle = jnp.where(group == 0, coef_in[2, j], jnp.where(group == 2, coef_in[3, j], courant[j]))
        below = jnp.broadcast_to(coef_in[0, j, rows - 1 : rows, :], (TOP, 128))
        above = jnp.broadcast_to(coef_in[1, j, 0:1, :], (TOP, 128))
        return jnp.concatenate([below, middle, above], axis=0)

    def tall_only(value):
        return jnp.concatenate([jnp.zeros((TOP, 128), F32), value, jnp.zeros((TOP, 128), F32)], axis=0)

    def answer(coef_x, coef_a, centre):
        west, east = pltpu.roll(centre, 1, 0), pltpu.roll(centre, tall - 1, 0)
        south, north = roll_lanes(centre, 1), roll_lanes(centre, -1)
        return (
            centre + coef_x * (west - centre) + coef_a * (south - centre)
            + DIFFUSE * (west + east + south + north - 4.0 * centre)
        )

    coef_x, coef_a = tall_coef(0), tall_coef(1)
    first = RADIAL * theta
    second = jnp.where(valid, answer(coef_x, coef_a, first) + RADIAL * (theta - 2.0 * first), 0.0)
    second_126 = RADIAL * first
    third = answer(coef_x, coef_a, second) + RADIAL * (second_126 + theta - 2.0 * second)
    third_126 = answer(tall_only(courant[2]), tall_only(courant[3]), second_126) + RADIAL * (second - 2.0 * second_126)
    third_125 = RADIAL * second_126
    added = [flatten(value[TOP : TOP + rows], (1,))[0] for value in (third_125, third_126, third)]
    added = jnp.concatenate(added + [jnp.zeros((5, length), F32)], axis=0)
    added_high = added.astype(BF16).astype(F32)
    added = jnp.concatenate([added_high, added - added_high], axis=0).astype(BF16)
    radius = lax.broadcasted_iota(jnp.int32, (16, 128), 1) - 125
    which = lax.broadcasted_iota(jnp.int32, (16, 128), 0) % 8
    spread = jnp.where(jnp.logical_and(radius == which, which < 3), 1.0, 0.0).astype(BF16)
    added = lax.dot_general(added, spread, (((0,), (0,)), ((), ())), preferred_element_type=F32)
    gas_res[...] = gas_res[...] + added.reshape(rows, SECTOR, 128)

    wait_bytes(redbuf.at[1, pl.ds(0, nax - 1)], red_sem.at[3])
    sums = jnp.sum(redbuf[1, 0:nax], axis=0, keepdims=True)
    top = jnp.sum(jnp.where(lane1 == 0, sums, 0.0), axis=1, keepdims=True)
    bottom = jnp.sum(jnp.where(lane1 == 1, sums, 0.0), axis=1, keepdims=True)
    relax = -FIRST_RELAX * top / (bottom + TINY)
    th_res[...] = theta1 + relax * residual2

    wait_bytes(msg.at[pl.ds(0, naz - 1)], msg_sem.at[0])
    wait_bytes(msg.at[pl.ds(0, 2 * REACH), pl.ds(0, 32)], nb_sem.at[0])
    wait_bytes(th_rows.at[pl.ds(0, 8)], th_sem.at[0])
    wait_bytes(base_rows.at[pl.ds(0, 4)], base_sem.at[0])
    wait_bytes(edge.at[pl.ds(0, naz - 1)], edge_sem.at[0])

    @pl.when(at_rim)
    def _():
        wait_bytes(edge.at[pl.ds(0, naz)], edge_sem.at[2])

    wait_bytes(redbuf.at[0, pl.ds(0, naz - 1)], red_sem.at[0])
    wait_bytes(redbuf.at[1, pl.ds(0, nax - 1)], red_sem.at[2])


def write_out(gas_res, wall_res, th_res, gas_out, wall_out, th_out, sem):
    copies = [
        pltpu.make_async_copy(source, target, sem.at[index])
        for index, (source, target) in enumerate(((gas_res, gas_out), (wall_res, wall_out), (th_res, th_out)))
    ]
    for copy in copies:
        copy.start()
    for copy in copies:
        copy.wait()


def on_device(
    nax, naz, gas_init, transport, heat_coef, bed_mask, wall_init, interface_init, inverse_blocks, rotation
):
    rows = gas_init.shape[0]
    layers, length = wall_init.shape[1:]
    table_high, table_low = hartley_parts(length)
    anywhere = pl.BlockSpec(memory_space=pltpu.HBM)
    vmem = pl.BlockSpec(memory_space=pltpu.VMEM)
    dma = pltpu.SemaphoreType.DMA
    operands = [
        pltpu.with_memory_space_constraint(value, pltpu.HBM)
        for value in (
            gas_init, transport, heat_coef, bed_mask, wall_init.reshape(layers, length), interface_init,
            jnp.transpose(inverse_blocks, (1, 2, 0)),
            jnp.asarray(table_high), jnp.asarray(table_low), jnp.asarray(selector()),
        )
    ]
    gas_now, wall_now, theta = pl.pallas_call(
        functools.partial(kernel, nax, naz),
        out_shape=(
            jax.ShapeDtypeStruct(gas_init.shape, F32),
            jax.ShapeDtypeStruct((layers, length), F32),
            jax.ShapeDtypeStruct((1, length), F32),
        ),
        in_specs=[anywhere] * 7 + [pl.BlockSpec(memory_space=pltpu.SMEM)] + [anywhere] * 3,
        out_specs=(vmem,) * 3,
        scratch_shapes=[
            pltpu.VMEM((3, rows + 2, SECTOR + 2 * TOP, 128), F32),
            pltpu.VMEM(transport.shape, BF16),
            pltpu.VMEM(heat_coef.shape, F32),
            pltpu.VMEM(bed_mask.shape, jnp.int32),
            pltpu.VMEM((layers, length), F32),
            pltpu.VMEM((1, length), F32),
            pltpu.VMEM((layers, layers, length), F32),
            pltpu.VMEM((length, length), BF16),
            pltpu.VMEM((length, length), BF16),
            pltpu.VMEM((NFIELD, 5 * 128), BF16),
            pltpu.VMEM((rows, NFIELD, 128), BF16),
            pltpu.VMEM((naz, NFIELD, 128), BF16),
            pltpu.VMEM((naz, 32, 128), BF16),
            pltpu.VMEM((naz * NFIELD, 128), F32),
            pltpu.VMEM((16, length), F32),
            pltpu.VMEM((8, length), F32),
            pltpu.VMEM((naz, 128), F32),
            pltpu.VMEM((rows + 2 * TOP, 128), F32),
            pltpu.VMEM((2, rows, 128), F32),
            pltpu.VMEM((4, 2, rows, 128), F32),
            pltpu.VMEM((3, 2, rows, 128), F32),
            pltpu.VMEM((3, 2, rows, 128), F32),
            pltpu.VMEM((layers, length), F32),
            pltpu.VMEM((2, 128), F32),
            pltpu.VMEM((2, max(nax, naz), 128), F32),
            dma((10,)),
            dma((2,)),
            dma((2,)),
            dma((2,)),
            dma((2,)),
            dma((4,)),
            dma((3, 4)),
            dma((3, 4)),
            dma((4,)),
            dma((4,)),
            dma((4,)),
        ],
        compiler_params=pltpu.CompilerParams(
            collective_id=0, has_side_effects=True, vmem_limit_bytes=48 * 1024 * 1024
        ),
        name="kiln_step",
    )(
        *operands[:7], rotation, *operands[7:],
    )
    gas_now, wall_now, theta = pl.pallas_call(
        write_out,
        out_shape=[jax.ShapeDtypeStruct(value.shape, F32) for value in (gas_now, wall_now, theta)],
        in_specs=[vmem] * 3,
        out_specs=[anywhere] * 3,
        scratch_shapes=[dma((3,))],
        compiler_params=pltpu.CompilerParams(vmem_limit_bytes=1024 * 1024),
        name="write_out",
    )(gas_now, wall_now, theta)
    return gas_now, wall_now.reshape(1, layers, length), theta


def solution(mesh):
    return jax.shard_map(
        functools.partial(on_device, mesh.shape["ax"], mesh.shape["az"]),
        mesh=mesh,
        in_specs=(
            P("ax", "az", None),
            P(None, "ax", "az", None),
            P("ax", "az"),
            P("ax", "az"),
            P(("ax", "az"), None, None),
            P(("ax", "az"), None),
            P(),
            P(),
        ),
        out_specs=(P("ax", "az", None), P(("ax", "az"), None, None), P(("ax", "az"), None)),
        check_vma=False,
    )
```

```python
import functools

import jax
import jax.numpy as jnp
import ml_dtypes
import numpy as np
from jax import lax
from jax.experimental import pallas as pl
from jax.experimental.pallas import tpu as pltpu
from jax.sharding import PartitionSpec as P

DIFFUSE = 0.04
RADIAL = 0.06
BED_COEF = 0.8
FIRST_RELAX = 0.5
TINY = 1e-06
MESH = pl.DeviceIdType.MESH
F32 = jnp.float32
BF16 = jnp.bfloat16
SECTOR = 32
TOP = 8
COUPLING, LOW = "coupling", "low"
GAS = [(part, r) for part in (0, 1) for r in (124, 125, 126, 127)]
WALLSIDE = [(2, 127), (3, 127), (4, 127), (2, 126), (3, 126), (4, 126), COUPLING, LOW]
FIELDS = (
    GAS
    + WALLSIDE
    + GAS
    + [(2, 125), (3, 125), (4, 125)] * 2 + [(4, 127), None]
    + [(part, r) for part in (0, 1) for r in (125, 126, 127)] + [(2, 127), (3, 127)]
    + WALLSIDE
)
NFIELD = len(FIELDS)
FIRSTS = [-5] * 8 + [-4] * 8 + [-1] * 8 + [-4] * 3 + [0] * 3 + [2] * 2 + [2] * 8 + [0] * 8
REACH = 5


def hartley_parts(length):
    positions = np.arange(length, dtype=np.int64)
    phases = 2.0 * np.pi / length * ((positions[:, None] * positions[None, :]) % length)
    table = ((np.cos(phases) + np.sin(phases)) / np.sqrt(length)).astype(np.float32)
    high = table.astype(ml_dtypes.bfloat16)
    low = (table - high.astype(np.float32)).astype(ml_dtypes.bfloat16)
    return high, low


def selector():
    table = np.zeros((NFIELD, 5 * 128), np.float32)
    for row, field in enumerate(FIELDS):
        if isinstance(field, tuple):
            table[row, field[0] * 128 + field[1]] = 1.0
    return table.astype(ml_dtypes.bfloat16)


def split(value):
    high = value.astype(BF16)
    return high, (value - high.astype(F32)).astype(BF16)


def roll_lanes(value, amount):
    amount = amount % value.shape[1]
    return pltpu.roll(value, amount, 1) if amount else value


def kernel(
    nax, naz,
    gas_hbm, tr_hbm, heat_hbm, bed_hbm, wall_hbm, th_hbm, inv_hbm, rot_ref, hh_hbm, hl_hbm, sel_hbm,
    gas_res, wall_res, th_res,
    pad, tr, heat, bed, wall, th, inv, hh, hl, sel,
    msg, recv, recv_nb, fields, th_rows, base_rows, window, edge, coef_out, coef_in, col_out, col_in, blend,
    redsrc, redbuf,
    load_sem, msg_sem, nb_sem, th_sem, base_sem, edge_sem, halo_ss, halo_rs, coef_ss, coef_rs, red_sem,
):
    ax, az = lax.axis_index("ax"), lax.axis_index("az")
    rows = naz
    length = SECTOR * naz
    quads = length // 128
    total = nax * rows
    flat = ax * naz + az
    up_ax, down_ax = lax.rem(ax + 1, nax), lax.rem(ax + nax - 1, nax)
    up_az, down_az = lax.rem(az + 1, naz), lax.rem(az + naz - 1, naz)
    inside = pl.ds(TOP, SECTOR)

    barrier = pltpu.get_barrier_semaphore()

    def greet(to_ax, to_az):
        pl.semaphore_signal(barrier, inc=1, device_id=(to_ax, to_az), device_id_type=MESH)

    low_edge, high_edge = az < REACH, az >= naz - REACH
    at_edge = jnp.logical_or(low_edge, high_edge)
    beside = jnp.where(low_edge, down_ax, up_ax)
    at_rim = jnp.logical_or(az < 2, az >= naz - 2)

    @pl.when(at_edge)
    def _():
        @pl.loop(0, naz)
        def _(k):
            greet(beside, k)

    for k in range(2):
        greet(up_ax, k)
        greet(down_ax, naz - 2 + k)

    for k in sorted(range(1, max(nax, naz)), key=lambda k: -min(k, max(nax, naz) - k)):
        if k < nax:
            greet(lax.rem(ax + k, nax), az)
        if k < naz:
            greet(ax, lax.rem(az + k, naz))

    loads = {}
    for index, (name, source, target) in enumerate((
        ("gas", gas_hbm, pad.at[0, pl.ds(1, rows), inside]),
        ("tr", tr_hbm, tr),
        ("heat", heat_hbm, heat),
        ("bed", bed_hbm, bed),
        ("sel", sel_hbm, sel),
        ("th", th_hbm, th),
        ("wall", wall_hbm, wall),
        ("hh", hh_hbm, hh),
        ("hl", hl_hbm, hl),
        ("inv", inv_hbm, inv),
    )):
        loads[name] = pltpu.make_async_copy(source, target, load_sem.at[index])
        loads[name].start()

    lane = lax.broadcasted_iota(jnp.int32, (naz, 128), 1)
    sector = lax.broadcasted_iota(jnp.int32, (naz, 128), 0)
    cell = lane % SECTOR
    group = lane // SECTOR
    turn = sector % 4

    def tile_rows(values):
        result = jnp.zeros((naz, 128), F32)
        for g, row in enumerate(values):
            if row is None:
                continue
            wide = jnp.concatenate(
                [jnp.broadcast_to(row[:, 128 * q : 128 * q + 128], (4, 128)) for q in range(quads)], axis=0
            )
            for p in range(4):
                here = jnp.logical_and(turn == p, group == g)
                result = jnp.where(here, roll_lanes(wide, SECTOR * (g - p)), result)
        return result

    def flatten(value, groups):
        moved = [roll_lanes(value, SECTOR * k) for k in range(4)]
        found = []
        for g in groups:
            result = jnp.zeros_like(value)
            for p in range(4):
                result = jnp.where(jnp.logical_and(turn == p, group == p), moved[(p - g) % 4], result)
            parts = [jnp.sum(result[4 * q : 4 * q + 4], axis=0, keepdims=True) for q in range(quads)]
            found.append(jnp.concatenate(parts, axis=1))
        return found

    def four_times(value):
        return jnp.concatenate([value] * 4, axis=1)

    loads["th"].wait()
    theta0 = th[...]
    th_rows[4:5, :] = theta0

    for name in ("gas", "tr", "heat", "bed", "sel"):
        loads[name].wait()
    gas = pad[0, 1 : rows + 1, TOP : TOP + SECTOR, :].reshape(rows * SECTOR, 128)
    gas_high, gas_low = split(gas)
    stacked = jnp.concatenate(
        [gas_high, gas_low] + [tr[j].reshape(rows * SECTOR, 128) for j in range(3)], axis=1
    )
    near = lax.dot_general(
        sel[...], stacked, (((1,), (1,)), ((), ())), preferred_element_type=F32
    )
    coded = four_times(jnp.where(bed[...] == 1, -heat[...], heat[...]))
    coded, = flatten(coded, (0,))
    coded_high = coded.astype(BF16).astype(F32)
    field_row = lax.broadcasted_iota(jnp.int32, (NFIELD, rows * SECTOR), 0)
    for index, one in enumerate(FIELDS):
        if one == COUPLING:
            near = jnp.where(field_row == index, coded_high, near)
        if one == LOW:
            near = jnp.where(field_row == index, coded - coded_high, near)
    turned = [near] + [roll_lanes(near, -SECTOR * k) for k in range(1, 4)]
    field8 = lax.broadcasted_iota(jnp.int32, (8, 128), 0)
    for i in range(rows):
        parts = []
        for part in range(NFIELD // 8):
            value = None
            for j in range(8):
                first = FIRSTS[8 * part + j]
                if j and first == FIRSTS[8 * part + j - 1]:
                    continue
                start = (i + first) % rows
                piece = turned[start % 4][8 * part : 8 * part + 8, 128 * (start // 4) : 128 * (start // 4) + 128]
                value = piece if value is None else jnp.where(field8 >= j, piece, value)
            parts.append(value)
        msg[i] = jnp.concatenate(parts, axis=0).astype(BF16)

    def stage_columns(step):
        col_out[step, 0] = pad[step, 1 : rows + 1, TOP, :]
        col_out[step, 1] = pad[step, 1 : rows + 1, TOP + SECTOR - 1, :]

    stage_columns(0)
    courant = [tile_rows([near[index : index + 1]] * 4) for index in (8, 9, 11, 12)]
    coef_out[0] = courant[0]
    coef_out[1] = courant[1]

    pl.semaphore_wait(barrier, naz - 1 + nax - 1 + 2 * REACH + jnp.where(at_rim, naz, 0))

    def remote(source, target, send, receive, to_ax, to_az):
        return pltpu.make_async_remote_copy(
            src_ref=source, dst_ref=target, send_sem=send, recv_sem=receive,
            device_id=(to_ax, to_az), device_id_type=MESH,
        )

    def wait_bytes(ref, sem):
        pltpu.make_async_copy(ref, ref, sem).wait()

    def edge_part(row):
        if row < REACH:
            return pl.ds(0, 32 if row < 2 else 16)
        return pl.ds(16, 32) if row > naz - REACH else pl.ds(32, 16)

    def send_row(ref, slot, reach, sems):
        for offset in range(-reach, reach + 1):
            if offset:
                to = lax.rem(flat + offset + total, total)
                remote(
                    ref.at[pl.ds(slot, 1)], ref.at[pl.ds(slot - offset, 1)], sems.at[0], sems.at[1],
                    lax.div(to, naz), lax.rem(to, naz),
                ).start()

    send_row(th_rows, 4, 4, th_sem)

    def halo_copies(step):
        return (
            remote(pad.at[step, rows, inside], pad.at[step, 0, inside],
                   halo_ss.at[step, 0], halo_rs.at[step, 0], up_ax, az),
            remote(pad.at[step, 1, inside], pad.at[step, rows + 1, inside],
                   halo_ss.at[step, 1], halo_rs.at[step, 1], down_ax, az),
            remote(col_out.at[step, 1], col_in.at[step, 0],
                   halo_ss.at[step, 2], halo_rs.at[step, 2], ax, up_az),
            remote(col_out.at[step, 0], col_in.at[step, 1],
                   halo_ss.at[step, 3], halo_rs.at[step, 3], ax, down_az),
        )

    def send_halo(step):
        for copy in halo_copies(step):
            copy.start()

    send_halo(0)

    for k in sorted(range(1, naz), key=lambda k: -min(k // 4, 4 - k // 4) - min(k % 4, 4 - k % 4)):
        to = lax.rem(az + k, naz)
        remote(msg.at[to], recv.at[az], msg_sem.at[0], msg_sem.at[1], ax, to).start()

    for k in range(REACH):
        part = edge_part(k)
        remote(msg.at[k, part], recv_nb.at[az, pl.ds(0, part.size)], nb_sem.at[0], nb_sem.at[1], up_ax, k).start()
        high = naz - REACH + k
        part = edge_part(high)
        remote(
            msg.at[high, part], recv_nb.at[az, pl.ds(0, part.size)], nb_sem.at[0], nb_sem.at[1], down_ax, high
        ).start()

    def times_table(value):
        high, low = split(value)
        count = value.shape[0]
        both = jnp.dot(jnp.concatenate([high, low], axis=0), hh[...], preferred_element_type=F32)
        return both[:count] + both[count:] + jnp.dot(high, hl[...], preferred_element_type=F32)

    def rows_times_table(value):
        count = value.shape[0]
        value = jnp.concatenate([value, jnp.zeros((8 - count, length), F32)], axis=0)
        high = value.astype(BF16).astype(F32)
        both = jnp.concatenate([high, value - high], axis=0).astype(BF16)
        first = jnp.dot(both, hh[...], preferred_element_type=F32)
        second = jnp.dot(both, hl[...], preferred_element_type=F32)
        return (first[0:8] + first[8:16] + second[0:8])[:count]

    loads["wall"].wait()
    loads["hh"].wait()
    loads["hl"].wait()
    layers = wall.shape[0]
    spectral = times_table(wall[...])
    loads["inv"].wait()
    mode_gain = inv[0, 0:1, :]
    mode_base = jnp.sum(inv[0] * spectral, axis=0, keepdims=True)
    base_rows[2:3, :] = mode_base
    send_row(base_rows, 2, 2, base_sem)

    def take_halo(step):
        for copy in halo_copies(step):
            copy.wait()

        @pl.when(ax == 0)
        def _():
            pad[step, 0, inside, :] = jnp.zeros((SECTOR, 128), F32)

        @pl.when(ax == nax - 1)
        def _():
            pad[step, rows + 1, inside, :] = jnp.zeros((SECTOR, 128), F32)

        pad[step, 1 : rows + 1, TOP - 1, :] = col_in[step, 0]
        pad[step, 1 : rows + 1, TOP + SECTOR, :] = col_in[step, 1]

    coef_copies = [
        remote(coef_out, coef_in.at[slot], coef_ss.at[slot], coef_rs.at[slot], to_ax, to_az)
        for slot, (to_ax, to_az) in enumerate(((up_ax, az), (down_ax, az), (ax, up_az), (ax, down_az)))
    ]
    for copy in coef_copies:
        copy.start()
    recv[az] = msg[az]

    @pl.loop(0, layers // 2)
    def _(pair):
        for j in range(2):
            layer = 2 * pair + j
            blend[pl.ds(layer, 1), :] = jnp.sum(inv[layer] * spectral, axis=0, keepdims=True)

    lane_row = lax.broadcasted_iota(jnp.int32, (SECTOR, 128), 1)

    def sweep(step, store):
        @pl.loop(0, rows, unroll=2)
        def _(x):
            centre = pad[step, x + 1, inside, :]
            west = pad[step, x, inside, :]
            east = pad[step, x + 2, inside, :]
            south = pad[step, x + 1, pl.ds(TOP - 1, SECTOR), :]
            north = pad[step, x + 1, pl.ds(TOP + 1, SECTOR), :]
            inner = jnp.where(lane_row == 0, centre, roll_lanes(centre, 1))
            outer = jnp.where(lane_row == 127, 0.0, roll_lanes(centre, -1))
            store(x, (
                centre
                + tr[0, x].astype(F32) * (west - centre)
                + tr[1, x].astype(F32) * (south - centre)
                + DIFFUSE * (west + east + south + north - 4.0 * centre)
                + RADIAL * (inner + outer - 2.0 * centre)
                + tr[2, x].astype(F32)
            ))

    def store_pad(step):
        def store(x, value):
            pad[step, x + 1, inside, :] = value
        return store

    wait_bytes(th_rows.at[pl.ds(0, 8)], th_sem.at[1])
    start = th_rows[0:9, :]
    rows_of = lambda values, *picks: tile_rows([None if k is None else values[k : k + 1] for k in picks])
    start_edges = [rows_of(start, 0, 1, 2, 3), rows_of(start, 4, 5, 6, 7), rows_of(start, 8, None, None, None)]

    take_halo(0)
    sweep(0, store_pad(1))
    stage_columns(1)
    send_halo(1)

    wait_bytes(recv.at[pl.ds(0, naz - 1)], msg_sem.at[1])

    @pl.loop(0, naz, unroll=True)
    def _(source):
        fields[pl.ds(pl.multiple_of(source * NFIELD, NFIELD), NFIELD), :] = recv[source].astype(F32)

    def merge(start, count):
        wait_bytes(recv_nb.at[pl.ds(0, naz), pl.ds(0, count)], nb_sem.at[1])
        firsts = jnp.zeros((count, 128), jnp.int32)
        index = lax.broadcasted_iota(jnp.int32, (count, 128), 0)
        for j in range(count):
            if j == 0 or FIRSTS[start + j] != FIRSTS[start + j - 1]:
                firsts = jnp.where(index >= j, FIRSTS[start + j], firsts)
        place = az + firsts + lax.broadcasted_iota(jnp.int32, (count, 128), 1) // SECTOR
        own = jnp.logical_and(place >= 0, place < rows)

        @pl.loop(0, naz, unroll=4)
        def _(source):
            here = pl.ds(pl.multiple_of(source * NFIELD + start, 16), count)
            fields[here, :] = jnp.where(own, fields[here, :], recv_nb[source, 0:count].astype(F32))

    for chosen, row in (
        (az < 2, 0),
        (jnp.logical_and(az >= 2, low_edge), 2),
        (az == naz - REACH, naz - REACH),
        (az > naz - REACH, naz - 1),
    ):
        part = edge_part(row)
        pl.when(chosen)(functools.partial(merge, part.start, part.size))

    def field(index):
        return fields[pl.ds(index, naz, stride=NFIELD), :]

    def in_domain(first):
        place = flat + first + group
        return jnp.logical_and(place >= 0, place < total)

    def masked(first, value):
        return jnp.where(in_domain(first), value, 0.0)

    gas_p = [masked(-5, field(j) + field(4 + j)) for j in range(4)]
    gas_q = [masked(-1, field(16 + j) + field(20 + j)) for j in range(4)]
    gas_r = [None] + [masked(2, field(32 + j) + field(35 + j)) for j in range(3)]
    coef_127 = [[field(8 + j) for j in range(3)], [field(40 + j) for j in range(3)]]
    coef_127.append([roll_lanes(field(j), -64) for j in (38, 39, 30)])
    coef_126 = [[field(11 + j) for j in range(3)], [field(43 + j) for j in range(3)]]
    coef_125 = [[field(24 + j) for j in range(3)], [field(27 + j) for j in range(3)]]
    coupling = [field(14) + field(15), field(46) + field(47)]

    def stencil(coef, centre, west, east, inner, outer):
        south = jnp.where(cell == 0, pltpu.roll(roll_lanes(centre, -31), 1, 0), roll_lanes(centre, 1))
        north = jnp.where(
            cell == SECTOR - 1, pltpu.roll(roll_lanes(centre, 31), naz - 1, 0), roll_lanes(centre, -1)
        )
        return (
            centre
            + coef[0] * (west - centre)
            + coef[1] * (south - centre)
            + DIFFUSE * (west + east + south + north - 4.0 * centre)
            + RADIAL * (inner + outer - 2.0 * centre)
            + coef[2]
        )

    def windows(p, q, r):
        if r is None:
            r = jnp.zeros_like(q)
        centres = (
            jnp.where(group == 3, roll_lanes(q, 96), roll_lanes(p, -32)),
            jnp.where(group == 3, roll_lanes(r, 64), roll_lanes(q, -32)),
        )
        easts = (
            jnp.where(group >= 2, roll_lanes(q, 64), roll_lanes(p, -64)),
            jnp.where(group >= 2, roll_lanes(r, 32), roll_lanes(q, -64)),
        )
        return centres, (p, q), easts

    def shifted(zero, one, two=None):
        west = (roll_lanes(zero, 32), jnp.where(group == 0, roll_lanes(zero, 32), roll_lanes(one, 32)))
        last = roll_lanes(one, -32)
        if two is not None:
            last = jnp.where(group == 3, roll_lanes(two, 96), last)
        east = (jnp.where(group == 3, roll_lanes(one, -32), roll_lanes(zero, -32)), last)
        return west, east

    none = jnp.zeros((naz, 128), F32)
    centre_124 = windows(gas_p[0], gas_q[0], None)[0]
    centre_125, west_125, east_125 = windows(gas_p[1], gas_q[1], gas_r[1])
    centre_126, west_126, east_126 = windows(gas_p[2], gas_q[2], gas_r[2])
    centre_127, west_127, east_127 = windows(gas_p[3], gas_q[3], gas_r[3])
    firsts = (-4, 0, 4)
    base = [
        masked(firsts[w], stencil(coef_127[w], centre_127[w], west_127[w], east_127[w], centre_126[w], none))
        for w in range(2)
    ]
    base.append(masked(4, stencil(
        coef_127[2], roll_lanes(gas_r[3], -64), roll_lanes(gas_r[3], -32), roll_lanes(gas_r[3], -96),
        roll_lanes(gas_r[2], -64), none,
    )))
    one_126 = [
        masked(firsts[w], stencil(coef_126[w], centre_126[w], west_126[w], east_126[w], centre_125[w], centre_127[w]))
        for w in range(2)
    ]
    one_125 = [
        stencil(coef_125[w], centre_125[w], west_125[w], east_125[w], centre_124[w], centre_126[w]) for w in range(2)
    ]
    west_one_126, east_one_126 = shifted(*one_126)

    def near_flux(edges, wanted):
        one = [base[w] + masked(firsts[w], RADIAL * edges[w]) for w in range(3)]
        west, east = shifted(*one)
        two = [
            masked(firsts[w], stencil(coef_127[w], one[w], west[w], east[w], one_126[w], edges[w])) for w in range(2)
        ]
        west, east = shifted(*two)
        result = []
        for w in wanted:
            two_126 = stencil(coef_126[w], one_126[w], west_one_126[w], east_one_126[w], one_125[w], one[w])
            three = stencil(coef_127[w], two[w], west[w], east[w], two_126, edges[w])
            result.append(jnp.where(
                coupling[w] < 0, -BED_COEF * edges[w], coupling[w] * (three - edges[w])
            ))
        return result

    shift = rot_ref[0]
    shift_back = length - shift

    def wall_face(flux, without):
        modes = rows_times_table(pltpu.roll(flux, shift_back, 1))
        face = rows_times_table(modes * mode_gain + without)
        return modes, pltpu.roll(face, shift, 1)

    flux = near_flux(start_edges, (0, 1))
    flux = jnp.concatenate(flatten(flux[0], (2, 3)) + flatten(flux[1], (0, 1, 2)), axis=0)
    wait_bytes(base_rows.at[pl.ds(0, 4)], base_sem.at[1])
    _, face = wall_face(flux, base_rows[0:5, :])
    residual1 = face - start[2:7]
    theta1 = start[2:7] + FIRST_RELAX * residual1
    flux = near_flux(
        [rows_of(theta1, None, None, 0, 1), rows_of(theta1, 2, 3, 4, None), none], (1,)
    )
    modes, face = wall_face(flatten(flux[0], (0,))[0], mode_base)
    residual1 = residual1[2:3]
    theta1 = theta1[2:3]
    residual2 = face - theta1
    change = residual2 - residual1
    top = jnp.sum(residual1 * change, axis=1, keepdims=True)
    bottom = jnp.sum(change * change, axis=1, keepdims=True)
    lane1 = lax.broadcasted_iota(jnp.int32, (1, 128), 1)
    redsrc[0:1] = jnp.where(lane1 == 0, top, jnp.where(lane1 == 1, bottom, 0.0))

    @pl.loop(1, naz)
    def _(k):
        to = lax.rem(az + k, naz)
        remote(redsrc.at[pl.ds(0, 1)], redbuf.at[0, pl.ds(az, 1)], red_sem.at[0], red_sem.at[1], ax, to).start()

    redbuf[0, pl.ds(az, 1), :] = redsrc[0:1]

    turned = [roll_lanes(theta1, -SECTOR * (p - 1)) for p in range(4)]
    window[...] = jnp.concatenate(
        [turned[k % 4][:, 128 * (k // 4) : 128 * (k // 4) + 128] for k in range(naz)], axis=0
    )

    @pl.loop(1, naz)
    def _(k):
        to = lax.rem(az + k, naz)
        remote(
            window.at[pl.ds(to, 1)], edge.at[pl.ds(TOP + az, 1)], edge_sem.at[0], edge_sem.at[1], ax, to
        ).start()

    rim_ax = jnp.where(az < 2, down_ax, up_ax)
    rim_row = jnp.where(az < 2, TOP + rows + az, TOP - naz + az)

    @pl.when(at_rim)
    def _():
        @pl.loop(0, naz)
        def _(k):
            remote(
                window.at[pl.ds(k, 1)], edge.at[pl.ds(rim_row, 1)], edge_sem.at[2], edge_sem.at[3], rim_ax, k
            ).start()

    edge[pl.ds(TOP + az, 1), :] = window[pl.ds(az, 1), :]

    wall_res[...] = times_table(blend[...] + inv[:, 0, :] * modes)

    take_halo(1)
    sweep(1, store_pad(2))
    stage_columns(2)
    send_halo(2)

    wait_bytes(redbuf.at[0, pl.ds(0, naz - 1)], red_sem.at[1])
    redsrc[1:2] = jnp.sum(redbuf[0, 0:naz], axis=0, keepdims=True)

    @pl.loop(1, nax)
    def _(k):
        to = lax.rem(ax + k, nax)
        remote(redsrc.at[pl.ds(1, 1)], redbuf.at[1, pl.ds(ax, 1)], red_sem.at[2], red_sem.at[3], to, az).start()

    redbuf[1, pl.ds(ax, 1), :] = redsrc[1:2]

    take_halo(2)

    def store_result(x, value):
        gas_res[x] = value

    sweep(2, store_result)

    for copy in coef_copies:
        copy.wait()
    wait_bytes(edge.at[pl.ds(0, naz - 1)], edge_sem.at[1])
    wait_bytes(edge.at[pl.ds(0, 4)], edge_sem.at[3])
    tall = rows + 2 * TOP
    place = lax.broadcasted_iota(jnp.int32, (tall, 128), 0)
    row_x = ax * rows + place - TOP
    valid = jnp.logical_and(jnp.logical_and(row_x >= 0, row_x < total),
                            jnp.logical_and(place >= TOP - 2, place < TOP + rows + 2))
    theta = jnp.where(valid, edge[...], 0.0)

    def tall_coef(j):
        middle = jnp.where(group == 0, coef_in[2, j], jnp.where(group == 2, coef_in[3, j], courant[j]))
        below = jnp.broadcast_to(coef_in[0, j, rows - 1 : rows, :], (TOP, 128))
        above = jnp.broadcast_to(coef_in[1, j, 0:1, :], (TOP, 128))
        return jnp.concatenate([below, middle, above], axis=0)

    def tall_only(value):
        return jnp.concatenate([jnp.zeros((TOP, 128), F32), value, jnp.zeros((TOP, 128), F32)], axis=0)

    def answer(coef_x, coef_a, centre):
        west, east = pltpu.roll(centre, 1, 0), pltpu.roll(centre, tall - 1, 0)
        south, north = roll_lanes(centre, 1), roll_lanes(centre, -1)
        return (
            centre + coef_x * (west - centre) + coef_a * (south - centre)
            + DIFFUSE * (west + east + south + north - 4.0 * centre)
        )

    coef_x, coef_a = tall_coef(0), tall_coef(1)
    first = RADIAL * theta
    second = jnp.where(valid, answer(coef_x, coef_a, first) + RADIAL * (theta - 2.0 * first), 0.0)
    second_126 = RADIAL * first
    third = answer(coef_x, coef_a, second) + RADIAL * (second_126 + theta - 2.0 * second)
    third_126 = answer(tall_only(courant[2]), tall_only(courant[3]), second_126) + RADIAL * (second - 2.0 * second_126)
    third_125 = RADIAL * second_126
    added = [flatten(value[TOP : TOP + rows], (1,))[0] for value in (third_125, third_126, third)]
    added = jnp.concatenate(added + [jnp.zeros((5, length), F32)], axis=0)
    added_high = added.astype(BF16).astype(F32)
    added = jnp.concatenate([added_high, added - added_high], axis=0).astype(BF16)
    radius = lax.broadcasted_iota(jnp.int32, (16, 128), 1) - 125
    which = lax.broadcasted_iota(jnp.int32, (16, 128), 0) % 8
    spread = jnp.where(jnp.logical_and(radius == which, which < 3), 1.0, 0.0).astype(BF16)
    added = lax.dot_general(added, spread, (((0,), (0,)), ((), ())), preferred_element_type=F32)
    gas_res[...] = gas_res[...] + added.reshape(rows, SECTOR, 128)

    wait_bytes(redbuf.at[1, pl.ds(0, nax - 1)], red_sem.at[3])
    sums = jnp.sum(redbuf[1, 0:nax], axis=0, keepdims=True)
    top = jnp.sum(jnp.where(lane1 == 0, sums, 0.0), axis=1, keepdims=True)
    bottom = jnp.sum(jnp.where(lane1 == 1, sums, 0.0), axis=1, keepdims=True)
    relax = -FIRST_RELAX * top / (bottom + TINY)
    th_res[...] = theta1 + relax * residual2

    wait_bytes(msg.at[pl.ds(0, naz - 1)], msg_sem.at[0])
    wait_bytes(msg.at[pl.ds(0, 8), pl.ds(0, 32)], nb_sem.at[0])
    wait_bytes(th_rows.at[pl.ds(0, 8)], th_sem.at[0])
    wait_bytes(base_rows.at[pl.ds(0, 4)], base_sem.at[0])
    wait_bytes(edge.at[pl.ds(0, naz - 1)], edge_sem.at[0])

    @pl.when(at_rim)
    def _():
        wait_bytes(edge.at[pl.ds(0, naz)], edge_sem.at[2])

    wait_bytes(redbuf.at[0, pl.ds(0, naz - 1)], red_sem.at[0])
    wait_bytes(redbuf.at[1, pl.ds(0, nax - 1)], red_sem.at[2])


def write_out(gas_res, wall_res, th_res, gas_out, wall_out, th_out, sem):
    copies = [
        pltpu.make_async_copy(source, target, sem.at[index])
        for index, (source, target) in enumerate(((gas_res, gas_out), (wall_res, wall_out), (th_res, th_out)))
    ]
    for copy in copies:
        copy.start()
    for copy in copies:
        copy.wait()


def on_device(
    nax, naz, gas_init, transport, heat_coef, bed_mask, wall_init, interface_init, inverse_blocks, rotation
):
    rows = gas_init.shape[0]
    layers, length = wall_init.shape[1:]
    table_high, table_low = hartley_parts(length)
    anywhere = pl.BlockSpec(memory_space=pltpu.HBM)
    vmem = pl.BlockSpec(memory_space=pltpu.VMEM)
    dma = pltpu.SemaphoreType.DMA
    operands = [
        pltpu.with_memory_space_constraint(value, pltpu.HBM)
        for value in (
            gas_init, transport, heat_coef, bed_mask, wall_init.reshape(layers, length), interface_init,
            jnp.transpose(inverse_blocks, (1, 2, 0)),
            jnp.asarray(table_high), jnp.asarray(table_low), jnp.asarray(selector()),
        )
    ]
    gas_now, wall_now, theta = pl.pallas_call(
        functools.partial(kernel, nax, naz),
        out_shape=(
            jax.ShapeDtypeStruct(gas_init.shape, F32),
            jax.ShapeDtypeStruct((layers, length), F32),
            jax.ShapeDtypeStruct((1, length), F32),
        ),
        in_specs=[anywhere] * 7 + [pl.BlockSpec(memory_space=pltpu.SMEM)] + [anywhere] * 3,
        out_specs=(vmem,) * 3,
        scratch_shapes=[
            pltpu.VMEM((3, rows + 2, SECTOR + 2 * TOP, 128), F32),
            pltpu.VMEM(transport.shape, BF16),
            pltpu.VMEM(heat_coef.shape, F32),
            pltpu.VMEM(bed_mask.shape, jnp.int32),
            pltpu.VMEM((layers, length), F32),
            pltpu.VMEM((1, length), F32),
            pltpu.VMEM((layers, layers, length), F32),
            pltpu.VMEM((length, length), BF16),
            pltpu.VMEM((length, length), BF16),
            pltpu.VMEM((NFIELD, 5 * 128), BF16),
            pltpu.VMEM((rows, NFIELD, 128), BF16),
            pltpu.VMEM((naz, NFIELD, 128), BF16),
            pltpu.VMEM((naz, 32, 128), BF16),
            pltpu.VMEM((naz * NFIELD, 128), F32),
            pltpu.VMEM((16, length), F32),
            pltpu.VMEM((8, length), F32),
            pltpu.VMEM((naz, 128), F32),
            pltpu.VMEM((rows + 2 * TOP, 128), F32),
            pltpu.VMEM((2, rows, 128), F32),
            pltpu.VMEM((4, 2, rows, 128), F32),
            pltpu.VMEM((3, 2, rows, 128), F32),
            pltpu.VMEM((3, 2, rows, 128), F32),
            pltpu.VMEM((layers, length), F32),
            pltpu.VMEM((2, 128), F32),
            pltpu.VMEM((2, max(nax, naz), 128), F32),
            dma((10,)),
            dma((2,)),
            dma((2,)),
            dma((2,)),
            dma((2,)),
            dma((4,)),
            dma((3, 4)),
            dma((3, 4)),
            dma((4,)),
            dma((4,)),
            dma((4,)),
        ],
        compiler_params=pltpu.CompilerParams(
            collective_id=0, has_side_effects=True, vmem_limit_bytes=48 * 1024 * 1024
        ),
        name="kiln_step",
    )(
        *operands[:7], rotation, *operands[7:],
    )
    gas_now, wall_now, theta = pl.pallas_call(
        write_out,
        out_shape=[jax.ShapeDtypeStruct(value.shape, F32) for value in (gas_now, wall_now, theta)],
        in_specs=[vmem] * 3,
        out_specs=[anywhere] * 3,
        scratch_shapes=[dma((3,))],
        compiler_params=pltpu.CompilerParams(vmem_limit_bytes=1024 * 1024),
        name="write_out",
    )(gas_now, wall_now, theta)
    return gas_now, wall_now.reshape(1, layers, length), theta


def solution(mesh):
    return jax.shard_map(
        functools.partial(on_device, mesh.shape["ax"], mesh.shape["az"]),
        mesh=mesh,
        in_specs=(
            P("ax", "az", None),
            P(None, "ax", "az", None),
            P("ax", "az"),
            P("ax", "az"),
            P(("ax", "az"), None, None),
            P(("ax", "az"), None),
            P(),
            P(),
        ),
        out_specs=(P("ax", "az", None), P(("ax", "az"), None, None), P(("ax", "az"), None)),
        check_vma=False,
    )
```

```python
import functools

import jax
import jax.numpy as jnp
import ml_dtypes
import numpy as np
from jax import lax
from jax.experimental import pallas as pl
from jax.experimental.pallas import tpu as pltpu
from jax.sharding import PartitionSpec as P

DIFFUSE = 0.04
RADIAL = 0.06
BED_COEF = 0.8
FIRST_RELAX = 0.5
TINY = 1e-06
MESH = pl.DeviceIdType.MESH
F32 = jnp.float32
BF16 = jnp.bfloat16
SECTOR = 32
TOP = 8
COUPLING, LOW = "coupling", "low"
GAS = [(part, r) for part in (0, 1) for r in (124, 125, 126, 127)]
WALLSIDE = [(2, 127), (3, 127), (4, 127), (2, 126), (3, 126), (4, 126), COUPLING, LOW]
FIELDS = (
    GAS
    + WALLSIDE
    + GAS
    + [(2, 125), (3, 125), (4, 125)] * 2 + [(4, 127), None]
    + [(part, r) for part in (0, 1) for r in (125, 126, 127)] + [(2, 127), (3, 127)]
    + WALLSIDE
)
NFIELD = len(FIELDS)
FIRSTS = [-5] * 8 + [-4] * 8 + [-1] * 8 + [-4] * 3 + [0] * 3 + [2] * 2 + [2] * 8 + [0] * 8
REACH = 5


def hartley_parts(length):
    positions = np.arange(length, dtype=np.int64)
    phases = 2.0 * np.pi / length * ((positions[:, None] * positions[None, :]) % length)
    table = ((np.cos(phases) + np.sin(phases)) / np.sqrt(length)).astype(np.float32)
    high = table.astype(ml_dtypes.bfloat16)
    low = (table - high.astype(np.float32)).astype(ml_dtypes.bfloat16)
    return high, low


def selector():
    table = np.zeros((NFIELD, 5 * 128), np.float32)
    for row, field in enumerate(FIELDS):
        if isinstance(field, tuple):
            table[row, field[0] * 128 + field[1]] = 1.0
    return table.astype(ml_dtypes.bfloat16)


def split(value):
    high = value.astype(BF16)
    return high, (value - high.astype(F32)).astype(BF16)


def roll_lanes(value, amount):
    amount = amount % value.shape[1]
    return pltpu.roll(value, amount, 1) if amount else value


def kernel(
    nax, naz,
    gas_hbm, tr_hbm, heat_hbm, bed_hbm, wall_hbm, th_hbm, inv_hbm, rot_ref, hh_hbm, hl_hbm, sel_hbm,
    gas_res, wall_res, th_res,
    pad, tr, heat, bed, wall, th, inv, hh, hl, gh, gl, sel,
    msg, recv, recv_nb, fields, th_rows, base_rows, window, edge, coef_out, coef_in, col_out, col_in, blend,
    redsrc, redbuf,
    load_sem, msg_sem, nb_sem, th_sem, base_sem, edge_sem, halo_ss, halo_rs, coef_ss, coef_rs, red_sem,
):
    ax, az = lax.axis_index("ax"), lax.axis_index("az")
    rows = naz
    length = SECTOR * naz
    quads = length // 128
    total = nax * rows
    flat = ax * naz + az
    up_ax, down_ax = lax.rem(ax + 1, nax), lax.rem(ax + nax - 1, nax)
    up_az, down_az = lax.rem(az + 1, naz), lax.rem(az + naz - 1, naz)
    inside = pl.ds(TOP, SECTOR)

    barrier = pltpu.get_barrier_semaphore()

    def greet(to_ax, to_az):
        pl.semaphore_signal(barrier, inc=1, device_id=(to_ax, to_az), device_id_type=MESH)

    low_edge, high_edge = az < REACH, az >= naz - REACH
    at_edge = jnp.logical_or(low_edge, high_edge)
    beside = jnp.where(low_edge, down_ax, up_ax)
    at_rim = jnp.logical_or(az < 2, az >= naz - 2)

    @pl.when(at_edge)
    def _():
        @pl.loop(0, naz)
        def _(k):
            greet(beside, k)

    for k in range(2):
        greet(up_ax, k)
        greet(down_ax, naz - 2 + k)

    for k in sorted(range(1, max(nax, naz)), key=lambda k: -min(k, max(nax, naz) - k)):
        if k < nax:
            greet(lax.rem(ax + k, nax), az)
        if k < naz:
            greet(ax, lax.rem(az + k, naz))

    loads = {}
    for index, (name, source, target) in enumerate((
        ("gas", gas_hbm, pad.at[0, pl.ds(1, rows), inside]),
        ("tr", tr_hbm, tr),
        ("heat", heat_hbm, heat),
        ("bed", bed_hbm, bed),
        ("sel", sel_hbm, sel),
        ("th", th_hbm, th),
        ("wall", wall_hbm, wall),
        ("hh", hh_hbm, hh),
        ("hl", hl_hbm, hl),
        ("inv", inv_hbm, inv),
    )):
        loads[name] = pltpu.make_async_copy(source, target, load_sem.at[index])
        loads[name].start()

    lane = lax.broadcasted_iota(jnp.int32, (naz, 128), 1)
    sector = lax.broadcasted_iota(jnp.int32, (naz, 128), 0)
    cell = lane % SECTOR
    group = lane // SECTOR
    turn = sector % 4

    def tile_rows(values):
        result = jnp.zeros((naz, 128), F32)
        for g, row in enumerate(values):
            if row is None:
                continue
            wide = jnp.concatenate(
                [jnp.broadcast_to(row[:, 128 * q : 128 * q + 128], (4, 128)) for q in range(quads)], axis=0
            )
            for p in range(4):
                here = jnp.logical_and(turn == p, group == g)
                result = jnp.where(here, roll_lanes(wide, SECTOR * (g - p)), result)
        return result

    def flatten(value, groups):
        moved = [roll_lanes(value, SECTOR * k) for k in range(4)]
        found = []
        for g in groups:
            result = jnp.zeros_like(value)
            for p in range(4):
                result = jnp.where(jnp.logical_and(turn == p, group == p), moved[(p - g) % 4], result)
            parts = [jnp.sum(result[4 * q : 4 * q + 4], axis=0, keepdims=True) for q in range(quads)]
            found.append(jnp.concatenate(parts, axis=1))
        return found

    def four_times(value):
        return jnp.concatenate([value] * 4, axis=1)

    loads["th"].wait()
    theta0 = th[...]
    th_rows[4:5, :] = theta0

    for name in ("gas", "tr", "heat", "bed", "sel"):
        loads[name].wait()
    gas = pad[0, 1 : rows + 1, TOP : TOP + SECTOR, :].reshape(rows * SECTOR, 128)
    gas_high, gas_low = split(gas)
    stacked = jnp.concatenate(
        [gas_high, gas_low] + [tr[j].reshape(rows * SECTOR, 128) for j in range(3)], axis=1
    )
    near = lax.dot_general(
        sel[...], stacked, (((1,), (1,)), ((), ())), preferred_element_type=F32
    )
    coded = four_times(jnp.where(bed[...] == 1, -heat[...], heat[...]))
    coded, = flatten(coded, (0,))
    coded_high = coded.astype(BF16).astype(F32)
    field_row = lax.broadcasted_iota(jnp.int32, (NFIELD, rows * SECTOR), 0)
    for index, one in enumerate(FIELDS):
        if one == COUPLING:
            near = jnp.where(field_row == index, coded_high, near)
        if one == LOW:
            near = jnp.where(field_row == index, coded - coded_high, near)
    turned = [near] + [roll_lanes(near, -SECTOR * k) for k in range(1, 4)]
    field8 = lax.broadcasted_iota(jnp.int32, (8, 128), 0)
    for i in range(rows):
        parts = []
        for part in range(NFIELD // 8):
            value = None
            for j in range(8):
                first = FIRSTS[8 * part + j]
                if j and first == FIRSTS[8 * part + j - 1]:
                    continue
                start = (i + first) % rows
                piece = turned[start % 4][8 * part : 8 * part + 8, 128 * (start // 4) : 128 * (start // 4) + 128]
                value = piece if value is None else jnp.where(field8 >= j, piece, value)
            parts.append(value)
        msg[i] = jnp.concatenate(parts, axis=0).astype(BF16)

    def stage_columns(step):
        col_out[step, 0] = pad[step, 1 : rows + 1, TOP, :]
        col_out[step, 1] = pad[step, 1 : rows + 1, TOP + SECTOR - 1, :]

    stage_columns(0)
    courant = [tile_rows([near[index : index + 1]] * 4) for index in (8, 9, 11, 12)]
    coef_out[0] = courant[0]
    coef_out[1] = courant[1]

    pl.semaphore_wait(barrier, naz - 1 + nax - 1 + 2 * REACH + jnp.where(at_rim, naz, 0))

    def remote(source, target, send, receive, to_ax, to_az):
        return pltpu.make_async_remote_copy(
            src_ref=source, dst_ref=target, send_sem=send, recv_sem=receive,
            device_id=(to_ax, to_az), device_id_type=MESH,
        )

    def wait_bytes(ref, sem):
        pltpu.make_async_copy(ref, ref, sem).wait()

    def edge_part(row):
        if row < REACH:
            return pl.ds(0, 32 if row < 2 else 16)
        return pl.ds(16, 32) if row > naz - REACH else pl.ds(32, 16)

    def send_row(ref, slot, reach, sems):
        for offset in range(-reach, reach + 1):
            if offset:
                to = lax.rem(flat + offset + total, total)
                remote(
                    ref.at[pl.ds(slot, 1)], ref.at[pl.ds(slot - offset, 1)], sems.at[0], sems.at[1],
                    lax.div(to, naz), lax.rem(to, naz),
                ).start()

    send_row(th_rows, 4, 4, th_sem)

    def halo_copies(step):
        return (
            remote(pad.at[step, rows, inside], pad.at[step, 0, inside],
                   halo_ss.at[step, 0], halo_rs.at[step, 0], up_ax, az),
            remote(pad.at[step, 1, inside], pad.at[step, rows + 1, inside],
                   halo_ss.at[step, 1], halo_rs.at[step, 1], down_ax, az),
            remote(col_out.at[step, 1], col_in.at[step, 0],
                   halo_ss.at[step, 2], halo_rs.at[step, 2], ax, up_az),
            remote(col_out.at[step, 0], col_in.at[step, 1],
                   halo_ss.at[step, 3], halo_rs.at[step, 3], ax, down_az),
        )

    def send_halo(step):
        for copy in halo_copies(step):
            copy.start()

    send_halo(0)

    for k in sorted(range(1, naz), key=lambda k: -min(k // 4, 4 - k // 4) - min(k % 4, 4 - k % 4)):
        to = lax.rem(az + k, naz)
        remote(msg.at[to], recv.at[az], msg_sem.at[0], msg_sem.at[1], ax, to).start()

    for k in range(REACH):
        part = edge_part(k)
        remote(msg.at[k, part], recv_nb.at[az, pl.ds(0, part.size)], nb_sem.at[0], nb_sem.at[1], up_ax, k).start()
        high = naz - REACH + k
        part = edge_part(high)
        remote(
            msg.at[high, part], recv_nb.at[az, pl.ds(0, part.size)], nb_sem.at[0], nb_sem.at[1], down_ax, high
        ).start()

    def times_table(value):
        high, low = split(value)
        count = value.shape[0]
        both = jnp.dot(jnp.concatenate([high, low], axis=0), hh[...], preferred_element_type=F32)
        return both[:count] + both[count:] + jnp.dot(high, hl[...], preferred_element_type=F32)

    def rows_times_table(value, high_table=hh, low_table=hl):
        count = value.shape[0]
        value = jnp.concatenate([value, jnp.zeros((8 - count, length), F32)], axis=0)
        high = value.astype(BF16).astype(F32)
        both = jnp.concatenate([high, value - high], axis=0).astype(BF16)
        first = jnp.dot(both, high_table[...], preferred_element_type=F32)
        second = jnp.dot(both, low_table[...], preferred_element_type=F32)
        return (first[0:8] + first[8:16] + second[0:8])[:count]

    loads["wall"].wait()
    loads["hh"].wait()
    loads["hl"].wait()
    layers = wall.shape[0]
    spectral = times_table(wall[...])
    loads["inv"].wait()
    mode_gain = inv[0, 0:1, :]
    mode_base = jnp.sum(inv[0] * spectral, axis=0, keepdims=True)
    base_rows[2:3, :] = rows_times_table(mode_base)
    send_row(base_rows, 2, 2, base_sem)

    def take_halo(step):
        for copy in halo_copies(step):
            copy.wait()

        @pl.when(ax == 0)
        def _():
            pad[step, 0, inside, :] = jnp.zeros((SECTOR, 128), F32)

        @pl.when(ax == nax - 1)
        def _():
            pad[step, rows + 1, inside, :] = jnp.zeros((SECTOR, 128), F32)

        pad[step, 1 : rows + 1, TOP - 1, :] = col_in[step, 0]
        pad[step, 1 : rows + 1, TOP + SECTOR, :] = col_in[step, 1]

    coef_copies = [
        remote(coef_out, coef_in.at[slot], coef_ss.at[slot], coef_rs.at[slot], to_ax, to_az)
        for slot, (to_ax, to_az) in enumerate(((up_ax, az), (down_ax, az), (ax, up_az), (ax, down_az)))
    ]
    recv[az] = msg[az]

    @pl.loop(0, layers // 2)
    def _(pair):
        for j in range(2):
            layer = 2 * pair + j
            blend[pl.ds(layer, 1), :] = jnp.sum(inv[layer] * spectral, axis=0, keepdims=True)

    scaled_high, scaled_low = split((hh[...].astype(F32) + hl[...].astype(F32)) * mode_gain)
    both = (
        jnp.dot(scaled_high, hh[...], preferred_element_type=F32)
        + jnp.dot(scaled_low, hh[...], preferred_element_type=F32)
        + jnp.dot(scaled_high, hl[...], preferred_element_type=F32)
    )
    gh[...], gl[...] = split(both)

    lane_row = lax.broadcasted_iota(jnp.int32, (SECTOR, 128), 1)

    def sweep(step, store):
        @pl.loop(0, rows, unroll=2)
        def _(x):
            centre = pad[step, x + 1, inside, :]
            west = pad[step, x, inside, :]
            east = pad[step, x + 2, inside, :]
            south = pad[step, x + 1, pl.ds(TOP - 1, SECTOR), :]
            north = pad[step, x + 1, pl.ds(TOP + 1, SECTOR), :]
            inner = jnp.where(lane_row == 0, centre, roll_lanes(centre, 1))
            outer = jnp.where(lane_row == 127, 0.0, roll_lanes(centre, -1))
            store(x, (
                centre
                + tr[0, x].astype(F32) * (west - centre)
                + tr[1, x].astype(F32) * (south - centre)
                + DIFFUSE * (west + east + south + north - 4.0 * centre)
                + RADIAL * (inner + outer - 2.0 * centre)
                + tr[2, x].astype(F32)
            ))

    def store_pad(step):
        def store(x, value):
            pad[step, x + 1, inside, :] = value
        return store

    wait_bytes(th_rows.at[pl.ds(0, 8)], th_sem.at[1])
    start = th_rows[0:9, :]
    rows_of = lambda values, *picks: tile_rows([None if k is None else values[k : k + 1] for k in picks])
    start_edges = [rows_of(start, 0, 1, 2, 3), rows_of(start, 4, 5, 6, 7), rows_of(start, 8, None, None, None)]

    take_halo(0)
    sweep(0, store_pad(1))
    stage_columns(1)
    send_halo(1)

    wait_bytes(recv.at[pl.ds(0, naz - 1)], msg_sem.at[1])

    @pl.loop(0, naz, unroll=True)
    def _(source):
        fields[pl.ds(pl.multiple_of(source * NFIELD, NFIELD), NFIELD), :] = recv[source].astype(F32)

    def merge(start, count):
        wait_bytes(recv_nb.at[pl.ds(0, naz), pl.ds(0, count)], nb_sem.at[1])
        firsts = jnp.zeros((count, 128), jnp.int32)
        index = lax.broadcasted_iota(jnp.int32, (count, 128), 0)
        for j in range(count):
            if j == 0 or FIRSTS[start + j] != FIRSTS[start + j - 1]:
                firsts = jnp.where(index >= j, FIRSTS[start + j], firsts)
        place = az + firsts + lax.broadcasted_iota(jnp.int32, (count, 128), 1) // SECTOR
        own = jnp.logical_and(place >= 0, place < rows)

        @pl.loop(0, naz, unroll=4)
        def _(source):
            here = pl.ds(pl.multiple_of(source * NFIELD + start, 16), count)
            fields[here, :] = jnp.where(own, fields[here, :], recv_nb[source, 0:count].astype(F32))

    for chosen, row in (
        (az < 2, 0),
        (jnp.logical_and(az >= 2, low_edge), 2),
        (az == naz - REACH, naz - REACH),
        (az > naz - REACH, naz - 1),
    ):
        part = edge_part(row)
        pl.when(chosen)(functools.partial(merge, part.start, part.size))

    def field(index):
        return fields[pl.ds(index, naz, stride=NFIELD), :]

    def in_domain(first):
        place = flat + first + group
        return jnp.logical_and(place >= 0, place < total)

    def masked(first, value):
        return jnp.where(in_domain(first), value, 0.0)

    gas_p = [masked(-5, field(j) + field(4 + j)) for j in range(4)]
    gas_q = [masked(-1, field(16 + j) + field(20 + j)) for j in range(4)]
    gas_r = [None] + [masked(2, field(32 + j) + field(35 + j)) for j in range(3)]
    coef_127 = [[field(8 + j) for j in range(3)], [field(40 + j) for j in range(3)]]
    coef_127.append([roll_lanes(field(j), -64) for j in (38, 39, 30)])
    coef_126 = [[field(11 + j) for j in range(3)], [field(43 + j) for j in range(3)]]
    coef_125 = [[field(24 + j) for j in range(3)], [field(27 + j) for j in range(3)]]
    coupling = [field(14) + field(15), field(46) + field(47)]

    def stencil(coef, centre, west, east, inner, outer):
        south = jnp.where(cell == 0, pltpu.roll(roll_lanes(centre, -31), 1, 0), roll_lanes(centre, 1))
        north = jnp.where(
            cell == SECTOR - 1, pltpu.roll(roll_lanes(centre, 31), naz - 1, 0), roll_lanes(centre, -1)
        )
        return (
            centre
            + coef[0] * (west - centre)
            + coef[1] * (south - centre)
            + DIFFUSE * (west + east + south + north - 4.0 * centre)
            + RADIAL * (inner + outer - 2.0 * centre)
            + coef[2]
        )

    def windows(p, q, r):
        if r is None:
            r = jnp.zeros_like(q)
        centres = (
            jnp.where(group == 3, roll_lanes(q, 96), roll_lanes(p, -32)),
            jnp.where(group == 3, roll_lanes(r, 64), roll_lanes(q, -32)),
        )
        easts = (
            jnp.where(group >= 2, roll_lanes(q, 64), roll_lanes(p, -64)),
            jnp.where(group >= 2, roll_lanes(r, 32), roll_lanes(q, -64)),
        )
        return centres, (p, q), easts

    def shifted(zero, one, two=None):
        west = (roll_lanes(zero, 32), jnp.where(group == 0, roll_lanes(zero, 32), roll_lanes(one, 32)))
        last = roll_lanes(one, -32)
        if two is not None:
            last = jnp.where(group == 3, roll_lanes(two, 96), last)
        east = (jnp.where(group == 3, roll_lanes(one, -32), roll_lanes(zero, -32)), last)
        return west, east

    none = jnp.zeros((naz, 128), F32)
    centre_124 = windows(gas_p[0], gas_q[0], None)[0]
    centre_125, west_125, east_125 = windows(gas_p[1], gas_q[1], gas_r[1])
    centre_126, west_126, east_126 = windows(gas_p[2], gas_q[2], gas_r[2])
    centre_127, west_127, east_127 = windows(gas_p[3], gas_q[3], gas_r[3])
    firsts = (-4, 0, 4)
    base = [
        masked(firsts[w], stencil(coef_127[w], centre_127[w], west_127[w], east_127[w], centre_126[w], none))
        for w in range(2)
    ]
    base.append(masked(4, stencil(
        coef_127[2], roll_lanes(gas_r[3], -64), roll_lanes(gas_r[3], -32), roll_lanes(gas_r[3], -96),
        roll_lanes(gas_r[2], -64), none,
    )))
    one_126 = [
        masked(firsts[w], stencil(coef_126[w], centre_126[w], west_126[w], east_126[w], centre_125[w], centre_127[w]))
        for w in range(2)
    ]
    one_125 = [
        stencil(coef_125[w], centre_125[w], west_125[w], east_125[w], centre_124[w], centre_126[w]) for w in range(2)
    ]
    west_one_126, east_one_126 = shifted(*one_126)

    def near_flux(edges, wanted):
        one = [base[w] + masked(firsts[w], RADIAL * edges[w]) for w in range(3)]
        west, east = shifted(*one)
        two = [
            masked(firsts[w], stencil(coef_127[w], one[w], west[w], east[w], one_126[w], edges[w])) for w in range(2)
        ]
        west, east = shifted(*two)
        result = []
        for w in wanted:
            two_126 = stencil(coef_126[w], one_126[w], west_one_126[w], east_one_126[w], one_125[w], one[w])
            three = stencil(coef_127[w], two[w], west[w], east[w], two_126, edges[w])
            result.append(jnp.where(
                coupling[w] < 0, -BED_COEF * edges[w], coupling[w] * (three - edges[w])
            ))
        return result

    shift = rot_ref[0]
    shift_back = length - shift

    def wall_face(flux, without):
        turned_flux = pltpu.roll(flux, shift_back, 1)
        face = rows_times_table(turned_flux, gh, gl) + without
        return turned_flux, pltpu.roll(face, shift, 1)

    flux = near_flux(start_edges, (0, 1))
    flux = jnp.concatenate(flatten(flux[0], (2, 3)) + flatten(flux[1], (0, 1, 2)), axis=0)
    wait_bytes(base_rows.at[pl.ds(0, 4)], base_sem.at[1])
    _, face = wall_face(flux, base_rows[0:5, :])
    residual1 = face - start[2:7]
    theta1 = start[2:7] + FIRST_RELAX * residual1
    flux = near_flux(
        [rows_of(theta1, None, None, 0, 1), rows_of(theta1, 2, 3, 4, None), none], (1,)
    )
    turned_flux, face = wall_face(flatten(flux[0], (0,))[0], base_rows[2:3, :])
    residual1 = residual1[2:3]
    theta1 = theta1[2:3]
    residual2 = face - theta1
    change = residual2 - residual1
    top = jnp.sum(residual1 * change, axis=1, keepdims=True)
    bottom = jnp.sum(change * change, axis=1, keepdims=True)
    lane1 = lax.broadcasted_iota(jnp.int32, (1, 128), 1)
    redsrc[0:1] = jnp.where(lane1 == 0, top, jnp.where(lane1 == 1, bottom, 0.0))

    @pl.loop(1, naz)
    def _(k):
        to = lax.rem(az + k, naz)
        remote(redsrc.at[pl.ds(0, 1)], redbuf.at[0, pl.ds(az, 1)], red_sem.at[0], red_sem.at[1], ax, to).start()

    redbuf[0, pl.ds(az, 1), :] = redsrc[0:1]

    turned = [roll_lanes(theta1, -SECTOR * (p - 1)) for p in range(4)]
    window[...] = jnp.concatenate(
        [turned[k % 4][:, 128 * (k // 4) : 128 * (k // 4) + 128] for k in range(naz)], axis=0
    )

    @pl.loop(1, naz)
    def _(k):
        to = lax.rem(az + k, naz)
        remote(
            window.at[pl.ds(to, 1)], edge.at[pl.ds(TOP + az, 1)], edge_sem.at[0], edge_sem.at[1], ax, to
        ).start()

    rim_ax = jnp.where(az < 2, down_ax, up_ax)
    rim_row = jnp.where(az < 2, TOP + rows + az, TOP - naz + az)

    @pl.when(at_rim)
    def _():
        @pl.loop(0, naz)
        def _(k):
            remote(
                window.at[pl.ds(k, 1)], edge.at[pl.ds(rim_row, 1)], edge_sem.at[2], edge_sem.at[3], rim_ax, k
            ).start()

    edge[pl.ds(TOP + az, 1), :] = window[pl.ds(az, 1), :]

    for copy in coef_copies:
        copy.start()

    wall_res[...] = times_table(blend[...] + inv[:, 0, :] * rows_times_table(turned_flux))

    take_halo(1)
    sweep(1, store_pad(2))
    stage_columns(2)
    send_halo(2)

    wait_bytes(redbuf.at[0, pl.ds(0, naz - 1)], red_sem.at[1])
    redsrc[1:2] = jnp.sum(redbuf[0, 0:naz], axis=0, keepdims=True)

    @pl.loop(1, nax)
    def _(k):
        to = lax.rem(ax + k, nax)
        remote(redsrc.at[pl.ds(1, 1)], redbuf.at[1, pl.ds(ax, 1)], red_sem.at[2], red_sem.at[3], to, az).start()

    redbuf[1, pl.ds(ax, 1), :] = redsrc[1:2]

    take_halo(2)

    def store_result(x, value):
        gas_res[x] = value

    sweep(2, store_result)

    for copy in coef_copies:
        copy.wait()
    wait_bytes(edge.at[pl.ds(0, naz - 1)], edge_sem.at[1])
    wait_bytes(edge.at[pl.ds(0, 4)], edge_sem.at[3])
    tall = rows + 2 * TOP
    place = lax.broadcasted_iota(jnp.int32, (tall, 128), 0)
    row_x = ax * rows + place - TOP
    valid = jnp.logical_and(jnp.logical_and(row_x >= 0, row_x < total),
                            jnp.logical_and(place >= TOP - 2, place < TOP + rows + 2))
    theta = jnp.where(valid, edge[...], 0.0)

    def tall_coef(j):
        middle = jnp.where(group == 0, coef_in[2, j], jnp.where(group == 2, coef_in[3, j], courant[j]))
        below = jnp.broadcast_to(coef_in[0, j, rows - 1 : rows, :], (TOP, 128))
        above = jnp.broadcast_to(coef_in[1, j, 0:1, :], (TOP, 128))
        return jnp.concatenate([below, middle, above], axis=0)

    def tall_only(value):
        return jnp.concatenate([jnp.zeros((TOP, 128), F32), value, jnp.zeros((TOP, 128), F32)], axis=0)

    def answer(coef_x, coef_a, centre):
        west, east = pltpu.roll(centre, 1, 0), pltpu.roll(centre, tall - 1, 0)
        south, north = roll_lanes(centre, 1), roll_lanes(centre, -1)
        return (
            centre + coef_x * (west - centre) + coef_a * (south - centre)
            + DIFFUSE * (west + east + south + north - 4.0 * centre)
        )

    coef_x, coef_a = tall_coef(0), tall_coef(1)
    first = RADIAL * theta
    second = jnp.where(valid, answer(coef_x, coef_a, first) + RADIAL * (theta - 2.0 * first), 0.0)
    second_126 = RADIAL * first
    third = answer(coef_x, coef_a, second) + RADIAL * (second_126 + theta - 2.0 * second)
    third_126 = answer(tall_only(courant[2]), tall_only(courant[3]), second_126) + RADIAL * (second - 2.0 * second_126)
    third_125 = RADIAL * second_126
    added = [flatten(value[TOP : TOP + rows], (1,))[0] for value in (third_125, third_126, third)]
    added = jnp.concatenate(added + [jnp.zeros((5, length), F32)], axis=0)
    added_high = added.astype(BF16).astype(F32)
    added = jnp.concatenate([added_high, added - added_high], axis=0).astype(BF16)
    radius = lax.broadcasted_iota(jnp.int32, (16, 128), 1) - 125
    which = lax.broadcasted_iota(jnp.int32, (16, 128), 0) % 8
    spread = jnp.where(jnp.logical_and(radius == which, which < 3), 1.0, 0.0).astype(BF16)
    added = lax.dot_general(added, spread, (((0,), (0,)), ((), ())), preferred_element_type=F32)
    gas_res[...] = gas_res[...] + added.reshape(rows, SECTOR, 128)

    wait_bytes(redbuf.at[1, pl.ds(0, nax - 1)], red_sem.at[3])
    sums = jnp.sum(redbuf[1, 0:nax], axis=0, keepdims=True)
    top = jnp.sum(jnp.where(lane1 == 0, sums, 0.0), axis=1, keepdims=True)
    bottom = jnp.sum(jnp.where(lane1 == 1, sums, 0.0), axis=1, keepdims=True)
    relax = -FIRST_RELAX * top / (bottom + TINY)
    th_res[...] = theta1 + relax * residual2

    wait_bytes(msg.at[pl.ds(0, naz - 1)], msg_sem.at[0])
    wait_bytes(msg.at[pl.ds(0, 8), pl.ds(0, 32)], nb_sem.at[0])
    wait_bytes(th_rows.at[pl.ds(0, 8)], th_sem.at[0])
    wait_bytes(base_rows.at[pl.ds(0, 4)], base_sem.at[0])
    wait_bytes(edge.at[pl.ds(0, naz - 1)], edge_sem.at[0])

    @pl.when(at_rim)
    def _():
        wait_bytes(edge.at[pl.ds(0, naz)], edge_sem.at[2])

    wait_bytes(redbuf.at[0, pl.ds(0, naz - 1)], red_sem.at[0])
    wait_bytes(redbuf.at[1, pl.ds(0, nax - 1)], red_sem.at[2])


def write_out(gas_res, wall_res, th_res, gas_out, wall_out, th_out, sem):
    copies = [
        pltpu.make_async_copy(source, target, sem.at[index])
        for index, (source, target) in enumerate(((gas_res, gas_out), (wall_res, wall_out), (th_res, th_out)))
    ]
    for copy in copies:
        copy.start()
    for copy in copies:
        copy.wait()


def on_device(
    nax, naz, gas_init, transport, heat_coef, bed_mask, wall_init, interface_init, inverse_blocks, rotation
):
    rows = gas_init.shape[0]
    layers, length = wall_init.shape[1:]
    table_high, table_low = hartley_parts(length)
    anywhere = pl.BlockSpec(memory_space=pltpu.HBM)
    vmem = pl.BlockSpec(memory_space=pltpu.VMEM)
    dma = pltpu.SemaphoreType.DMA
    operands = [
        pltpu.with_memory_space_constraint(value, pltpu.HBM)
        for value in (
            gas_init, transport, heat_coef, bed_mask, wall_init.reshape(layers, length), interface_init,
            jnp.transpose(inverse_blocks, (1, 2, 0)),
            jnp.asarray(table_high), jnp.asarray(table_low), jnp.asarray(selector()),
        )
    ]
    gas_now, wall_now, theta = pl.pallas_call(
        functools.partial(kernel, nax, naz),
        out_shape=(
            jax.ShapeDtypeStruct(gas_init.shape, F32),
            jax.ShapeDtypeStruct((layers, length), F32),
            jax.ShapeDtypeStruct((1, length), F32),
        ),
        in_specs=[anywhere] * 7 + [pl.BlockSpec(memory_space=pltpu.SMEM)] + [anywhere] * 3,
        out_specs=(vmem,) * 3,
        scratch_shapes=[
            pltpu.VMEM((3, rows + 2, SECTOR + 2 * TOP, 128), F32),
            pltpu.VMEM(transport.shape, BF16),
            pltpu.VMEM(heat_coef.shape, F32),
            pltpu.VMEM(bed_mask.shape, jnp.int32),
            pltpu.VMEM((layers, length), F32),
            pltpu.VMEM((1, length), F32),
            pltpu.VMEM((layers, layers, length), F32),
            pltpu.VMEM((length, length), BF16),
            pltpu.VMEM((length, length), BF16),
            pltpu.VMEM((length, length), BF16),
            pltpu.VMEM((length, length), BF16),
            pltpu.VMEM((NFIELD, 5 * 128), BF16),
            pltpu.VMEM((rows, NFIELD, 128), BF16),
            pltpu.VMEM((naz, NFIELD, 128), BF16),
            pltpu.VMEM((naz, 32, 128), BF16),
            pltpu.VMEM((naz * NFIELD, 128), F32),
            pltpu.VMEM((16, length), F32),
            pltpu.VMEM((8, length), F32),
            pltpu.VMEM((naz, 128), F32),
            pltpu.VMEM((rows + 2 * TOP, 128), F32),
            pltpu.VMEM((2, rows, 128), F32),
            pltpu.VMEM((4, 2, rows, 128), F32),
            pltpu.VMEM((3, 2, rows, 128), F32),
            pltpu.VMEM((3, 2, rows, 128), F32),
            pltpu.VMEM((layers, length), F32),
            pltpu.VMEM((2, 128), F32),
            pltpu.VMEM((2, max(nax, naz), 128), F32),
            dma((10,)),
            dma((2,)),
            dma((2,)),
            dma((2,)),
            dma((2,)),
            dma((4,)),
            dma((3, 4)),
            dma((3, 4)),
            dma((4,)),
            dma((4,)),
            dma((4,)),
        ],
        compiler_params=pltpu.CompilerParams(
            collective_id=0, has_side_effects=True, vmem_limit_bytes=48 * 1024 * 1024
        ),
        name="kiln_step",
    )(
        *operands[:7], rotation, *operands[7:],
    )
    gas_now, wall_now, theta = pl.pallas_call(
        write_out,
        out_shape=[jax.ShapeDtypeStruct(value.shape, F32) for value in (gas_now, wall_now, theta)],
        in_specs=[vmem] * 3,
        out_specs=[anywhere] * 3,
        scratch_shapes=[dma((3,))],
        compiler_params=pltpu.CompilerParams(vmem_limit_bytes=1024 * 1024),
        name="write_out",
    )(gas_now, wall_now, theta)
    return gas_now, wall_now.reshape(1, layers, length), theta


def solution(mesh):
    return jax.shard_map(
        functools.partial(on_device, mesh.shape["ax"], mesh.shape["az"]),
        mesh=mesh,
        in_specs=(
            P("ax", "az", None),
            P(None, "ax", "az", None),
            P("ax", "az"),
            P("ax", "az"),
            P(("ax", "az"), None, None),
            P(("ax", "az"), None),
            P(),
            P(),
        ),
        out_specs=(P("ax", "az", None), P(("ax", "az"), None, None), P(("ax", "az"), None)),
        check_vma=False,
    )
```

```python
import functools

import jax
import jax.numpy as jnp
import ml_dtypes
import numpy as np
from jax import lax
from jax.experimental import pallas as pl
from jax.experimental.pallas import tpu as pltpu
from jax.sharding import PartitionSpec as P

DIFFUSE = 0.04
RADIAL = 0.06
BED_COEF = 0.8
FIRST_RELAX = 0.5
TINY = 1e-06
MESH = pl.DeviceIdType.MESH
F32 = jnp.float32
BF16 = jnp.bfloat16
SECTOR = 32
TOP = 8
COUPLING, LOW = "coupling", "low"
GAS = [(part, r) for part in (0, 1) for r in (124, 125, 126, 127)]
WALLSIDE = [(2, 127), (3, 127), (4, 127), (2, 126), (3, 126), (4, 126), COUPLING, LOW]
FIELDS = (
    GAS
    + WALLSIDE
    + GAS
    + [(2, 125), (3, 125), (4, 125)] * 2 + [(4, 127), None]
    + [(part, r) for part in (0, 1) for r in (125, 126, 127)] + [(2, 127), (3, 127)]
    + WALLSIDE
)
NFIELD = len(FIELDS)
FIRSTS = [-5] * 8 + [-4] * 8 + [-1] * 8 + [-4] * 3 + [0] * 3 + [2] * 2 + [2] * 8 + [0] * 8
REACH = 5


def hartley_parts(length):
    positions = np.arange(length, dtype=np.int64)
    phases = 2.0 * np.pi / length * ((positions[:, None] * positions[None, :]) % length)
    table = ((np.cos(phases) + np.sin(phases)) / np.sqrt(length)).astype(np.float32)
    high = table.astype(ml_dtypes.bfloat16)
    low = (table - high.astype(np.float32)).astype(ml_dtypes.bfloat16)
    return high, low


def selector():
    table = np.zeros((NFIELD, 5 * 128), np.float32)
    for row, field in enumerate(FIELDS):
        if isinstance(field, tuple):
            table[row, field[0] * 128 + field[1]] = 1.0
    return table.astype(ml_dtypes.bfloat16)


def split(value):
    high = value.astype(BF16)
    return high, (value - high.astype(F32)).astype(BF16)


def roll_lanes(value, amount):
    amount = amount % value.shape[1]
    return pltpu.roll(value, amount, 1) if amount else value


def kernel(
    nax, naz,
    gas_hbm, tr_hbm, heat_hbm, bed_hbm, wall_hbm, th_hbm, inv_hbm, rot_ref, hh_hbm, hl_hbm, sel_hbm,
    gas_res, wall_res, th_res,
    pad, tr, heat, bed, wall, th, inv, hh, hl, gh, gl, sel,
    msg, recv, recv_nb, fields, th_rows, base_rows, window, edge, coef_out, coef_in, col_out, col_in, row_in, blend,
    redsrc, redbuf,
    load_sem, msg_sem, nb_sem, th_sem, base_sem, edge_sem, halo_ss, halo_rs, coef_ss, coef_rs, red_sem,
):
    ax, az = lax.axis_index("ax"), lax.axis_index("az")
    rows = naz
    length = SECTOR * naz
    quads = length // 128
    total = nax * rows
    flat = ax * naz + az
    up_ax, down_ax = lax.rem(ax + 1, nax), lax.rem(ax + nax - 1, nax)
    up_az, down_az = lax.rem(az + 1, naz), lax.rem(az + naz - 1, naz)
    inside = pl.ds(TOP, SECTOR)

    barrier = pltpu.get_barrier_semaphore()

    def greet(to_ax, to_az):
        pl.semaphore_signal(barrier, inc=1, device_id=(to_ax, to_az), device_id_type=MESH)

    low_edge, high_edge = az < REACH, az >= naz - REACH
    at_edge = jnp.logical_or(low_edge, high_edge)
    beside = jnp.where(low_edge, down_ax, up_ax)
    at_rim = jnp.logical_or(az < 2, az >= naz - 2)

    @pl.when(at_edge)
    def _():
        @pl.loop(0, naz)
        def _(k):
            greet(beside, k)

    for k in range(2):
        greet(up_ax, k)
        greet(down_ax, naz - 2 + k)

    for k in sorted(range(1, max(nax, naz)), key=lambda k: -min(k, max(nax, naz) - k)):
        if k < nax:
            greet(lax.rem(ax + k, nax), az)
        if k < naz:
            greet(ax, lax.rem(az + k, naz))

    loads = {}
    for index, (name, source, target) in enumerate((
        ("gas", gas_hbm, pad.at[0, pl.ds(1, rows), inside]),
        ("tr", tr_hbm, tr),
        ("heat", heat_hbm, heat),
        ("bed", bed_hbm, bed),
        ("sel", sel_hbm, sel),
        ("th", th_hbm, th),
        ("wall", wall_hbm, wall),
        ("hh", hh_hbm, hh),
        ("hl", hl_hbm, hl),
        ("inv", inv_hbm, inv),
    )):
        loads[name] = pltpu.make_async_copy(source, target, load_sem.at[index])
        loads[name].start()

    lane = lax.broadcasted_iota(jnp.int32, (naz, 128), 1)
    sector = lax.broadcasted_iota(jnp.int32, (naz, 128), 0)
    cell = lane % SECTOR
    group = lane // SECTOR
    turn = sector % 4

    def tile_rows(values):
        result = jnp.zeros((naz, 128), F32)
        for g, row in enumerate(values):
            if row is None:
                continue
            wide = jnp.concatenate(
                [jnp.broadcast_to(row[:, 128 * q : 128 * q + 128], (4, 128)) for q in range(quads)], axis=0
            )
            for p in range(4):
                here = jnp.logical_and(turn == p, group == g)
                result = jnp.where(here, roll_lanes(wide, SECTOR * (g - p)), result)
        return result

    def flatten(value, groups):
        moved = [roll_lanes(value, SECTOR * k) for k in range(4)]
        found = []
        for g in groups:
            result = jnp.zeros_like(value)
            for p in range(4):
                result = jnp.where(jnp.logical_and(turn == p, group == p), moved[(p - g) % 4], result)
            parts = [jnp.sum(result[4 * q : 4 * q + 4], axis=0, keepdims=True) for q in range(quads)]
            found.append(jnp.concatenate(parts, axis=1))
        return found

    def four_times(value):
        return jnp.concatenate([value] * 4, axis=1)

    loads["th"].wait()
    theta0 = th[...]
    th_rows[4:5, :] = theta0

    for name in ("gas", "tr", "heat", "bed", "sel"):
        loads[name].wait()
    gas = pad[0, 1 : rows + 1, TOP : TOP + SECTOR, :].reshape(rows * SECTOR, 128)
    gas_high, gas_low = split(gas)
    stacked = jnp.concatenate(
        [gas_high, gas_low] + [tr[j].reshape(rows * SECTOR, 128) for j in range(3)], axis=1
    )
    near = lax.dot_general(
        sel[...], stacked, (((1,), (1,)), ((), ())), preferred_element_type=F32
    )
    coded = four_times(jnp.where(bed[...] == 1, -heat[...], heat[...]))
    coded, = flatten(coded, (0,))
    coded_high = coded.astype(BF16).astype(F32)
    field_row = lax.broadcasted_iota(jnp.int32, (NFIELD, rows * SECTOR), 0)
    for index, one in enumerate(FIELDS):
        if one == COUPLING:
            near = jnp.where(field_row == index, coded_high, near)
        if one == LOW:
            near = jnp.where(field_row == index, coded - coded_high, near)
    turned = [near] + [roll_lanes(near, -SECTOR * k) for k in range(1, 4)]
    field8 = lax.broadcasted_iota(jnp.int32, (8, 128), 0)
    for i in range(rows):
        parts = []
        for part in range(NFIELD // 8):
            value = None
            for j in range(8):
                first = FIRSTS[8 * part + j]
                if j and first == FIRSTS[8 * part + j - 1]:
                    continue
                start = (i + first) % rows
                piece = turned[start % 4][8 * part : 8 * part + 8, 128 * (start // 4) : 128 * (start // 4) + 128]
                value = piece if value is None else jnp.where(field8 >= j, piece, value)
            parts.append(value)
        msg[i] = jnp.concatenate(parts, axis=0).astype(BF16)

    def stage_columns(step):
        col_out[step, 0] = pad[step, 1 : rows + 1, TOP, :]
        col_out[step, 1] = pad[step, 1 : rows + 1, TOP + SECTOR - 1, :]

    stage_columns(0)
    courant = [tile_rows([near[index : index + 1]] * 4) for index in (8, 9, 11, 12)]
    coef_out[0] = courant[0]
    coef_out[1] = courant[1]

    pl.semaphore_wait(barrier, naz - 1 + nax - 1 + 2 * REACH + jnp.where(at_rim, naz, 0))

    def remote(source, target, send, receive, to_ax, to_az):
        return pltpu.make_async_remote_copy(
            src_ref=source, dst_ref=target, send_sem=send, recv_sem=receive,
            device_id=(to_ax, to_az), device_id_type=MESH,
        )

    def wait_bytes(ref, sem):
        pltpu.make_async_copy(ref, ref, sem).wait()

    def edge_part(row):
        if row < REACH:
            return pl.ds(0, 32 if row < 2 else 16)
        return pl.ds(16, 32) if row > naz - REACH else pl.ds(32, 16)

    def send_row(ref, slot, reach, sems):
        for offset in range(-reach, reach + 1):
            if offset:
                to = lax.rem(flat + offset + total, total)
                remote(
                    ref.at[pl.ds(slot, 1)], ref.at[pl.ds(slot - offset, 1)], sems.at[0], sems.at[1],
                    lax.div(to, naz), lax.rem(to, naz),
                ).start()

    send_row(th_rows, 4, 4, th_sem)

    def halo_copies(step):
        return (
            remote(pad.at[step, rows, inside], pad.at[step, 0, inside] if step else row_in.at[0],
                   halo_ss.at[step, 0], halo_rs.at[step, 0], up_ax, az),
            remote(pad.at[step, 1, inside], pad.at[step, rows + 1, inside] if step else row_in.at[1],
                   halo_ss.at[step, 1], halo_rs.at[step, 1], down_ax, az),
            remote(col_out.at[step, 1], col_in.at[step, 0],
                   halo_ss.at[step, 2], halo_rs.at[step, 2], ax, up_az),
            remote(col_out.at[step, 0], col_in.at[step, 1],
                   halo_ss.at[step, 3], halo_rs.at[step, 3], ax, down_az),
        )

    def send_halo(step):
        for copy in halo_copies(step):
            copy.start()

    send_halo(0)

    for k in sorted(range(1, naz), key=lambda k: -min(k // 4, 4 - k // 4) - min(k % 4, 4 - k % 4)):
        to = lax.rem(az + k, naz)
        remote(msg.at[to], recv.at[az], msg_sem.at[0], msg_sem.at[1], ax, to).start()

    for k in range(REACH):
        part = edge_part(k)
        remote(msg.at[k, part], recv_nb.at[az, pl.ds(0, part.size)], nb_sem.at[0], nb_sem.at[1], up_ax, k).start()
        high = naz - REACH + k
        part = edge_part(high)
        remote(
            msg.at[high, part], recv_nb.at[az, pl.ds(0, part.size)], nb_sem.at[0], nb_sem.at[1], down_ax, high
        ).start()

    def times_table(value):
        high, low = split(value)
        count = value.shape[0]
        both = jnp.dot(jnp.concatenate([high, low], axis=0), hh[...], preferred_element_type=F32)
        return both[:count] + both[count:] + jnp.dot(high, hl[...], preferred_element_type=F32)

    def rows_times_table(value, high_table=hh, low_table=hl):
        count = value.shape[0]
        value = jnp.concatenate([value, jnp.zeros((8 - count, length), F32)], axis=0)
        high = value.astype(BF16).astype(F32)
        both = jnp.concatenate([high, value - high], axis=0).astype(BF16)
        first = jnp.dot(both, high_table[...], preferred_element_type=F32)
        second = jnp.dot(both, low_table[...], preferred_element_type=F32)
        return (first[0:8] + first[8:16] + second[0:8])[:count]

    loads["wall"].wait()
    loads["hh"].wait()
    loads["hl"].wait()
    layers = wall.shape[0]
    spectral = times_table(wall[...])
    loads["inv"].wait()
    mode_gain = inv[0, 0:1, :]
    mode_base = jnp.sum(inv[0] * spectral, axis=0, keepdims=True)
    base_rows[2:3, :] = rows_times_table(mode_base)
    send_row(base_rows, 2, 2, base_sem)

    def take_halo(step):
        for copy in halo_copies(step):
            copy.wait()

        @pl.when(ax == 0)
        def _():
            pad[step, 0, inside, :] = jnp.zeros((SECTOR, 128), F32)

        @pl.when(ax == nax - 1)
        def _():
            pad[step, rows + 1, inside, :] = jnp.zeros((SECTOR, 128), F32)

        pad[step, 1 : rows + 1, TOP - 1, :] = col_in[step, 0]
        pad[step, 1 : rows + 1, TOP + SECTOR, :] = col_in[step, 1]

    coef_copies = [
        remote(coef_out, coef_in.at[slot], coef_ss.at[slot], coef_rs.at[slot], to_ax, to_az)
        for slot, (to_ax, to_az) in enumerate(((up_ax, az), (down_ax, az), (ax, up_az), (ax, down_az)))
    ]
    recv[az] = msg[az]

    scaled_high, scaled_low = split((hh[...].astype(F32) + hl[...].astype(F32)) * mode_gain)
    both = (
        jnp.dot(scaled_high, hh[...], preferred_element_type=F32)
        + jnp.dot(scaled_low, hh[...], preferred_element_type=F32)
        + jnp.dot(scaled_high, hl[...], preferred_element_type=F32)
    )
    gh[...], gl[...] = split(both)

    lane_row = lax.broadcasted_iota(jnp.int32, (SECTOR, 128), 1)

    def sweep(step, store):
        @pl.loop(0, rows, unroll=2)
        def _(x):
            centre = pad[step, x + 1, inside, :]
            west = pad[step, x, inside, :]
            east = pad[step, x + 2, inside, :]
            south = pad[step, x + 1, pl.ds(TOP - 1, SECTOR), :]
            north = pad[step, x + 1, pl.ds(TOP + 1, SECTOR), :]
            inner = jnp.where(lane_row == 0, centre, roll_lanes(centre, 1))
            outer = jnp.where(lane_row == 127, 0.0, roll_lanes(centre, -1))
            store(x, (
                centre
                + tr[0, x].astype(F32) * (west - centre)
                + tr[1, x].astype(F32) * (south - centre)
                + DIFFUSE * (west + east + south + north - 4.0 * centre)
                + RADIAL * (inner + outer - 2.0 * centre)
                + tr[2, x].astype(F32)
            ))

    def store_pad(step):
        def store(x, value):
            pad[step, x + 1, inside, :] = value
        return store

    wait_bytes(th_rows.at[pl.ds(0, 8)], th_sem.at[1])
    start = th_rows[0:9, :]
    rows_of = lambda values, *picks: tile_rows([None if k is None else values[k : k + 1] for k in picks])
    start_edges = [rows_of(start, 0, 1, 2, 3), rows_of(start, 4, 5, 6, 7), rows_of(start, 8, None, None, None)]

    for edge_row in (0, rows + 1):
        pad[0, edge_row, inside, :] = jnp.zeros((SECTOR, 128), F32)
    for edge_column in (TOP - 1, TOP + SECTOR):
        pad[0, 1 : rows + 1, edge_column, :] = jnp.zeros((rows, 128), F32)
    sweep(0, store_pad(1))
    swirl = tr[1, :, 0:16, :].astype(F32)[:, 0, :]
    for copy in halo_copies(0):
        copy.wait()
    west = jnp.where(ax > 0, row_in[0], 0.0)
    east = jnp.where(ax < nax - 1, row_in[1], 0.0)
    pad[1, 1, inside, :] = pad[1, 1, inside, :] + (tr[0, 0].astype(F32) + DIFFUSE) * west
    pad[1, rows, inside, :] = pad[1, rows, inside, :] + DIFFUSE * east
    pad[1, 1 : rows + 1, TOP, :] = pad[1, 1 : rows + 1, TOP, :] + (swirl + DIFFUSE) * col_in[0, 0]
    pad[1, 1 : rows + 1, TOP + SECTOR - 1, :] = pad[1, 1 : rows + 1, TOP + SECTOR - 1, :] + DIFFUSE * col_in[0, 1]
    stage_columns(1)
    send_halo(1)

    wait_bytes(recv.at[pl.ds(0, naz - 1)], msg_sem.at[1])

    @pl.loop(0, naz, unroll=True)
    def _(source):
        fields[pl.ds(pl.multiple_of(source * NFIELD, NFIELD), NFIELD), :] = recv[source].astype(F32)

    def merge(start, count):
        wait_bytes(recv_nb.at[pl.ds(0, naz), pl.ds(0, count)], nb_sem.at[1])
        firsts = jnp.zeros((count, 128), jnp.int32)
        index = lax.broadcasted_iota(jnp.int32, (count, 128), 0)
        for j in range(count):
            if j == 0 or FIRSTS[start + j] != FIRSTS[start + j - 1]:
                firsts = jnp.where(index >= j, FIRSTS[start + j], firsts)
        place = az + firsts + lax.broadcasted_iota(jnp.int32, (count, 128), 1) // SECTOR
        own = jnp.logical_and(place >= 0, place < rows)

        @pl.loop(0, naz, unroll=4)
        def _(source):
            here = pl.ds(pl.multiple_of(source * NFIELD + start, 16), count)
            fields[here, :] = jnp.where(own, fields[here, :], recv_nb[source, 0:count].astype(F32))

    for chosen, row in (
        (az < 2, 0),
        (jnp.logical_and(az >= 2, low_edge), 2),
        (az == naz - REACH, naz - REACH),
        (az > naz - REACH, naz - 1),
    ):
        part = edge_part(row)
        pl.when(chosen)(functools.partial(merge, part.start, part.size))

    def field(index):
        return fields[pl.ds(index, naz, stride=NFIELD), :]

    def in_domain(first):
        place = flat + first + group
        return jnp.logical_and(place >= 0, place < total)

    def masked(first, value):
        return jnp.where(in_domain(first), value, 0.0)

    gas_p = [masked(-5, field(j) + field(4 + j)) for j in range(4)]
    gas_q = [masked(-1, field(16 + j) + field(20 + j)) for j in range(4)]
    gas_r = [None] + [masked(2, field(32 + j) + field(35 + j)) for j in range(3)]
    coef_127 = [[field(8 + j) for j in range(3)], [field(40 + j) for j in range(3)]]
    coef_127.append([roll_lanes(field(j), -64) for j in (38, 39, 30)])
    coef_126 = [[field(11 + j) for j in range(3)], [field(43 + j) for j in range(3)]]
    coef_125 = [[field(24 + j) for j in range(3)], [field(27 + j) for j in range(3)]]
    coupling = [field(14) + field(15), field(46) + field(47)]

    def stencil(coef, centre, west, east, inner, outer):
        south = jnp.where(cell == 0, pltpu.roll(roll_lanes(centre, -31), 1, 0), roll_lanes(centre, 1))
        north = jnp.where(
            cell == SECTOR - 1, pltpu.roll(roll_lanes(centre, 31), naz - 1, 0), roll_lanes(centre, -1)
        )
        return (
            centre
            + coef[0] * (west - centre)
            + coef[1] * (south - centre)
            + DIFFUSE * (west + east + south + north - 4.0 * centre)
            + RADIAL * (inner + outer - 2.0 * centre)
            + coef[2]
        )

    def windows(p, q, r):
        if r is None:
            r = jnp.zeros_like(q)
        centres = (
            jnp.where(group == 3, roll_lanes(q, 96), roll_lanes(p, -32)),
            jnp.where(group == 3, roll_lanes(r, 64), roll_lanes(q, -32)),
        )
        easts = (
            jnp.where(group >= 2, roll_lanes(q, 64), roll_lanes(p, -64)),
            jnp.where(group >= 2, roll_lanes(r, 32), roll_lanes(q, -64)),
        )
        return centres, (p, q), easts

    def shifted(zero, one, two=None):
        west = (roll_lanes(zero, 32), jnp.where(group == 0, roll_lanes(zero, 32), roll_lanes(one, 32)))
        last = roll_lanes(one, -32)
        if two is not None:
            last = jnp.where(group == 3, roll_lanes(two, 96), last)
        east = (jnp.where(group == 3, roll_lanes(one, -32), roll_lanes(zero, -32)), last)
        return west, east

    none = jnp.zeros((naz, 128), F32)
    centre_124 = windows(gas_p[0], gas_q[0], None)[0]
    centre_125, west_125, east_125 = windows(gas_p[1], gas_q[1], gas_r[1])
    centre_126, west_126, east_126 = windows(gas_p[2], gas_q[2], gas_r[2])
    centre_127, west_127, east_127 = windows(gas_p[3], gas_q[3], gas_r[3])
    firsts = (-4, 0, 4)
    base = [
        masked(firsts[w], stencil(coef_127[w], centre_127[w], west_127[w], east_127[w], centre_126[w], none))
        for w in range(2)
    ]
    base.append(masked(4, stencil(
        coef_127[2], roll_lanes(gas_r[3], -64), roll_lanes(gas_r[3], -32), roll_lanes(gas_r[3], -96),
        roll_lanes(gas_r[2], -64), none,
    )))
    one_126 = [
        masked(firsts[w], stencil(coef_126[w], centre_126[w], west_126[w], east_126[w], centre_125[w], centre_127[w]))
        for w in range(2)
    ]
    one_125 = [
        stencil(coef_125[w], centre_125[w], west_125[w], east_125[w], centre_124[w], centre_126[w]) for w in range(2)
    ]
    west_one_126, east_one_126 = shifted(*one_126)

    def near_flux(edges, wanted):
        one = [base[w] + masked(firsts[w], RADIAL * edges[w]) for w in range(3)]
        west, east = shifted(*one)
        two = [
            masked(firsts[w], stencil(coef_127[w], one[w], west[w], east[w], one_126[w], edges[w])) for w in range(2)
        ]
        west, east = shifted(*two)
        result = []
        for w in wanted:
            two_126 = stencil(coef_126[w], one_126[w], west_one_126[w], east_one_126[w], one_125[w], one[w])
            three = stencil(coef_127[w], two[w], west[w], east[w], two_126, edges[w])
            result.append(jnp.where(
                coupling[w] < 0, -BED_COEF * edges[w], coupling[w] * (three - edges[w])
            ))
        return result

    shift = rot_ref[0]
    shift_back = length - shift

    def wall_face(flux, without):
        turned_flux = pltpu.roll(flux, shift_back, 1)
        face = rows_times_table(turned_flux, gh, gl) + without
        return turned_flux, pltpu.roll(face, shift, 1)

    flux = near_flux(start_edges, (0, 1))
    flux = jnp.concatenate(flatten(flux[0], (2, 3)) + flatten(flux[1], (0, 1, 2)), axis=0)
    wait_bytes(base_rows.at[pl.ds(0, 4)], base_sem.at[1])
    _, face = wall_face(flux, base_rows[0:5, :])
    residual1 = face - start[2:7]
    theta1 = start[2:7] + FIRST_RELAX * residual1
    flux = near_flux(
        [rows_of(theta1, None, None, 0, 1), rows_of(theta1, 2, 3, 4, None), none], (1,)
    )
    turned_flux, face = wall_face(flatten(flux[0], (0,))[0], base_rows[2:3, :])
    residual1 = residual1[2:3]
    theta1 = theta1[2:3]
    residual2 = face - theta1
    change = residual2 - residual1
    top = jnp.sum(residual1 * change, axis=1, keepdims=True)
    bottom = jnp.sum(change * change, axis=1, keepdims=True)
    lane1 = lax.broadcasted_iota(jnp.int32, (1, 128), 1)
    redsrc[0:1] = jnp.where(lane1 == 0, top, jnp.where(lane1 == 1, bottom, 0.0))

    @pl.loop(1, naz)
    def _(k):
        to = lax.rem(az + k, naz)
        remote(redsrc.at[pl.ds(0, 1)], redbuf.at[0, pl.ds(az, 1)], red_sem.at[0], red_sem.at[1], ax, to).start()

    redbuf[0, pl.ds(az, 1), :] = redsrc[0:1]

    turned = [roll_lanes(theta1, -SECTOR * (p - 1)) for p in range(4)]
    window[...] = jnp.concatenate(
        [turned[k % 4][:, 128 * (k // 4) : 128 * (k // 4) + 128] for k in range(naz)], axis=0
    )

    @pl.loop(1, naz)
    def _(k):
        to = lax.rem(az + k, naz)
        remote(
            window.at[pl.ds(to, 1)], edge.at[pl.ds(TOP + az, 1)], edge_sem.at[0], edge_sem.at[1], ax, to
        ).start()

    rim_ax = jnp.where(az < 2, down_ax, up_ax)
    rim_row = jnp.where(az < 2, TOP + rows + az, TOP - naz + az)

    @pl.when(at_rim)
    def _():
        @pl.loop(0, naz)
        def _(k):
            remote(
                window.at[pl.ds(k, 1)], edge.at[pl.ds(rim_row, 1)], edge_sem.at[2], edge_sem.at[3], rim_ax, k
            ).start()

    edge[pl.ds(TOP + az, 1), :] = window[pl.ds(az, 1), :]

    for copy in coef_copies:
        copy.start()

    @pl.loop(0, layers // 2)
    def _(pair):
        for j in range(2):
            layer = 2 * pair + j
            blend[pl.ds(layer, 1), :] = jnp.sum(inv[layer] * spectral, axis=0, keepdims=True)

    wall_res[...] = times_table(blend[...] + inv[:, 0, :] * rows_times_table(turned_flux))

    take_halo(1)
    sweep(1, store_pad(2))
    stage_columns(2)
    send_halo(2)

    wait_bytes(redbuf.at[0, pl.ds(0, naz - 1)], red_sem.at[1])
    redsrc[1:2] = jnp.sum(redbuf[0, 0:naz], axis=0, keepdims=True)

    @pl.loop(1, nax)
    def _(k):
        to = lax.rem(ax + k, nax)
        remote(redsrc.at[pl.ds(1, 1)], redbuf.at[1, pl.ds(ax, 1)], red_sem.at[2], red_sem.at[3], to, az).start()

    redbuf[1, pl.ds(ax, 1), :] = redsrc[1:2]

    take_halo(2)

    def store_result(x, value):
        gas_res[x] = value

    sweep(2, store_result)

    for copy in coef_copies:
        copy.wait()
    wait_bytes(edge.at[pl.ds(0, naz - 1)], edge_sem.at[1])
    wait_bytes(edge.at[pl.ds(0, 4)], edge_sem.at[3])
    tall = rows + 2 * TOP
    place = lax.broadcasted_iota(jnp.int32, (tall, 128), 0)
    row_x = ax * rows + place - TOP
    valid = jnp.logical_and(jnp.logical_and(row_x >= 0, row_x < total),
                            jnp.logical_and(place >= TOP - 2, place < TOP + rows + 2))
    theta = jnp.where(valid, edge[...], 0.0)

    def tall_coef(j):
        middle = jnp.where(group == 0, coef_in[2, j], jnp.where(group == 2, coef_in[3, j], courant[j]))
        below = jnp.broadcast_to(coef_in[0, j, rows - 1 : rows, :], (TOP, 128))
        above = jnp.broadcast_to(coef_in[1, j, 0:1, :], (TOP, 128))
        return jnp.concatenate([below, middle, above], axis=0)

    def tall_only(value):
        return jnp.concatenate([jnp.zeros((TOP, 128), F32), value, jnp.zeros((TOP, 128), F32)], axis=0)

    def answer(coef_x, coef_a, centre):
        west, east = pltpu.roll(centre, 1, 0), pltpu.roll(centre, tall - 1, 0)
        south, north = roll_lanes(centre, 1), roll_lanes(centre, -1)
        return (
            centre + coef_x * (west - centre) + coef_a * (south - centre)
            + DIFFUSE * (west + east + south + north - 4.0 * centre)
        )

    coef_x, coef_a = tall_coef(0), tall_coef(1)
    first = RADIAL * theta
    second = jnp.where(valid, answer(coef_x, coef_a, first) + RADIAL * (theta - 2.0 * first), 0.0)
    second_126 = RADIAL * first
    third = answer(coef_x, coef_a, second) + RADIAL * (second_126 + theta - 2.0 * second)
    third_126 = answer(tall_only(courant[2]), tall_only(courant[3]), second_126) + RADIAL * (second - 2.0 * second_126)
    third_125 = RADIAL * second_126
    added = [flatten(value[TOP : TOP + rows], (1,))[0] for value in (third_125, third_126, third)]
    added = jnp.concatenate(added + [jnp.zeros((5, length), F32)], axis=0)
    added_high = added.astype(BF16).astype(F32)
    added = jnp.concatenate([added_high, added - added_high], axis=0).astype(BF16)
    radius = lax.broadcasted_iota(jnp.int32, (16, 128), 1) - 125
    which = lax.broadcasted_iota(jnp.int32, (16, 128), 0) % 8
    spread = jnp.where(jnp.logical_and(radius == which, which < 3), 1.0, 0.0).astype(BF16)
    added = lax.dot_general(added, spread, (((0,), (0,)), ((), ())), preferred_element_type=F32)
    gas_res[...] = gas_res[...] + added.reshape(rows, SECTOR, 128)

    wait_bytes(redbuf.at[1, pl.ds(0, nax - 1)], red_sem.at[3])
    sums = jnp.sum(redbuf[1, 0:nax], axis=0, keepdims=True)
    top = jnp.sum(jnp.where(lane1 == 0, sums, 0.0), axis=1, keepdims=True)
    bottom = jnp.sum(jnp.where(lane1 == 1, sums, 0.0), axis=1, keepdims=True)
    relax = -FIRST_RELAX * top / (bottom + TINY)
    th_res[...] = theta1 + relax * residual2

    wait_bytes(msg.at[pl.ds(0, naz - 1)], msg_sem.at[0])
    wait_bytes(msg.at[pl.ds(0, 8), pl.ds(0, 32)], nb_sem.at[0])
    wait_bytes(th_rows.at[pl.ds(0, 8)], th_sem.at[0])
    wait_bytes(base_rows.at[pl.ds(0, 4)], base_sem.at[0])
    wait_bytes(edge.at[pl.ds(0, naz - 1)], edge_sem.at[0])

    @pl.when(at_rim)
    def _():
        wait_bytes(edge.at[pl.ds(0, naz)], edge_sem.at[2])

    wait_bytes(redbuf.at[0, pl.ds(0, naz - 1)], red_sem.at[0])
    wait_bytes(redbuf.at[1, pl.ds(0, nax - 1)], red_sem.at[2])


def write_out(gas_res, wall_res, th_res, gas_out, wall_out, th_out, sem):
    copies = [
        pltpu.make_async_copy(source, target, sem.at[index])
        for index, (source, target) in enumerate(((gas_res, gas_out), (wall_res, wall_out), (th_res, th_out)))
    ]
    for copy in copies:
        copy.start()
    for copy in copies:
        copy.wait()


def on_device(
    nax, naz, gas_init, transport, heat_coef, bed_mask, wall_init, interface_init, inverse_blocks, rotation
):
    rows = gas_init.shape[0]
    layers, length = wall_init.shape[1:]
    table_high, table_low = hartley_parts(length)
    anywhere = pl.BlockSpec(memory_space=pltpu.HBM)
    vmem = pl.BlockSpec(memory_space=pltpu.VMEM)
    dma = pltpu.SemaphoreType.DMA
    operands = [
        pltpu.with_memory_space_constraint(value, pltpu.HBM)
        for value in (
            gas_init, transport, heat_coef, bed_mask, wall_init.reshape(layers, length), interface_init,
            jnp.transpose(inverse_blocks, (1, 2, 0)),
            jnp.asarray(table_high), jnp.asarray(table_low), jnp.asarray(selector()),
        )
    ]
    gas_now, wall_now, theta = pl.pallas_call(
        functools.partial(kernel, nax, naz),
        out_shape=(
            jax.ShapeDtypeStruct(gas_init.shape, F32),
            jax.ShapeDtypeStruct((layers, length), F32),
            jax.ShapeDtypeStruct((1, length), F32),
        ),
        in_specs=[anywhere] * 7 + [pl.BlockSpec(memory_space=pltpu.SMEM)] + [anywhere] * 3,
        out_specs=(vmem,) * 3,
        scratch_shapes=[
            pltpu.VMEM((3, rows + 2, SECTOR + 2 * TOP, 128), F32),
            pltpu.VMEM(transport.shape, BF16),
            pltpu.VMEM(heat_coef.shape, F32),
            pltpu.VMEM(bed_mask.shape, jnp.int32),
            pltpu.VMEM((layers, length), F32),
            pltpu.VMEM((1, length), F32),
            pltpu.VMEM((layers, layers, length), F32),
            pltpu.VMEM((length, length), BF16),
            pltpu.VMEM((length, length), BF16),
            pltpu.VMEM((length, length), BF16),
            pltpu.VMEM((length, length), BF16),
            pltpu.VMEM((NFIELD, 5 * 128), BF16),
            pltpu.VMEM((rows, NFIELD, 128), BF16),
            pltpu.VMEM((naz, NFIELD, 128), BF16),
            pltpu.VMEM((naz, 32, 128), BF16),
            pltpu.VMEM((naz * NFIELD, 128), F32),
            pltpu.VMEM((16, length), F32),
            pltpu.VMEM((8, length), F32),
            pltpu.VMEM((naz, 128), F32),
            pltpu.VMEM((rows + 2 * TOP, 128), F32),
            pltpu.VMEM((2, rows, 128), F32),
            pltpu.VMEM((4, 2, rows, 128), F32),
            pltpu.VMEM((3, 2, rows, 128), F32),
            pltpu.VMEM((3, 2, rows, 128), F32),
            pltpu.VMEM((2, SECTOR, 128), F32),
            pltpu.VMEM((layers, length), F32),
            pltpu.VMEM((2, 128), F32),
            pltpu.VMEM((2, max(nax, naz), 128), F32),
            dma((10,)),
            dma((2,)),
            dma((2,)),
            dma((2,)),
            dma((2,)),
            dma((4,)),
            dma((3, 4)),
            dma((3, 4)),
            dma((4,)),
            dma((4,)),
            dma((4,)),
        ],
        compiler_params=pltpu.CompilerParams(
            collective_id=0, has_side_effects=True, vmem_limit_bytes=48 * 1024 * 1024
        ),
        name="kiln_step",
    )(
        *operands[:7], rotation, *operands[7:],
    )
    gas_now, wall_now, theta = pl.pallas_call(
        write_out,
        out_shape=[jax.ShapeDtypeStruct(value.shape, F32) for value in (gas_now, wall_now, theta)],
        in_specs=[vmem] * 3,
        out_specs=[anywhere] * 3,
        scratch_shapes=[dma((3,))],
        compiler_params=pltpu.CompilerParams(vmem_limit_bytes=1024 * 1024),
        name="write_out",
    )(gas_now, wall_now, theta)
    return gas_now, wall_now.reshape(1, layers, length), theta


def solution(mesh):
    return jax.shard_map(
        functools.partial(on_device, mesh.shape["ax"], mesh.shape["az"]),
        mesh=mesh,
        in_specs=(
            P("ax", "az", None),
            P(None, "ax", "az", None),
            P("ax", "az"),
            P("ax", "az"),
            P(("ax", "az"), None, None),
            P(("ax", "az"), None),
            P(),
            P(),
        ),
        out_specs=(P("ax", "az", None), P(("ax", "az"), None, None), P(("ax", "az"), None)),
        check_vma=False,
    )
```
